256 devices in a mesh: row: 32 (over y, z), col: 8 (over x, core).
Axes of the slice: x: 4, y: 4, z: 8, core: 2. Of those that a mesh axis runs over, the one named last changes fastest.
Arguments:
- momentum: float32 [28672, 8192], P('row', 'col'), may hold values from -6 to 6
- gradient: bfloat16 [28672, 8192], P('row', 'col'), may hold values from -40 to 40
- old_basis: float32 [8192, 256], P('col'), may hold values from -0.0625 to 0.0625
Outputs:
- new_momentum: float32 [28672, 8192], P('row', 'col')
- new_basis: float32 [8192, 256], P('col')
- update: bfloat16 [28672, 8192], P('row', 'col')
The draws below stay inside these ranges and needn't reach their ends.
All inputs are finite; a program needn't handle non-finite values.
Results may differ from the reference program's by a relative error of at most 0.002.
Values sent between devices are 32-bit elements; how exact they have to be, the bound alone decides.
No kernel may reach another device: no remote copies, remote signals or barrier semaphores. Data moves between devices by JAX's collectives and lax.ppermute only.
A program may use at most 128 MiB of HBM per device.

```python
import math
import jax
import jax.numpy as jnp
from jax import lax

M_ROWS = 28672
N_COLS = 8192
RANK = 256


def draw_gradient(key, part):
    key = jax.random.fold_in(key, 7)
    key_base, key_cols = jax.random.split(key, 2)
    column_scale = jnp.exp(jax.random.uniform(key_cols, (1, N_COLS), jnp.float32, 0.0, math.log(10.0)))
    base_values = jnp.clip(jax.random.normal(key_base, (M_ROWS, N_COLS), jnp.float32), -4.0, 4.0)
    values = base_values * column_scale
    return values.astype(jnp.bfloat16)


def block_scale(own_key, dims, cuts, smallest, top_value):
    factor_of, own = 1.0, jax.random.fold_in(own_key, 6)
    for position, blocks in cuts:
        steps = jnp.exp(jax.random.uniform(jax.random.fold_in(own, position), (blocks,), jnp.float32, smallest / len(cuts), top_value / len(cuts)))
        factor_of = factor_of * jnp.repeat(steps, dims[position] // blocks).reshape([-1 if axis == position else 1 for axis in range(len(dims))])
    return factor_of


def gaussian(stream_key, extent, deviation, bound, pieces=(), held_as=jnp.bfloat16):
    drawn = deviation * jax.random.normal(stream_key, extent, jnp.float32)
    if pieces:
        drawn = drawn * block_scale(stream_key, extent, pieces, -0.22, 0.18)
    return jnp.clip(drawn, -bound, bound).astype(held_as)


def setup_inputs(seed: int = 0) -> dict:
    seeds = jax.random.split(jax.random.key(seed), 4)
    return {
        "momentum": gaussian(seeds[0], (M_ROWS, N_COLS), 1.0, 6.0, ((0, 32), (1, 8)), jnp.float32),
        "gradient": draw_gradient(jax.random.fold_in(seeds[3], 71), 0),
        "old_basis": gaussian(seeds[2], (N_COLS, RANK), N_COLS ** -0.5, 0.0625, ((0, 8),), jnp.float32),
    }


def reference(momentum, gradient, old_basis):
    high = lax.Precision.HIGHEST
    summed = momentum + gradient.astype(jnp.float32)
    powered = jnp.dot(summed, old_basis, precision=high)
    gram_total = jnp.einsum('ik,il->kl', powered, powered, precision=high)
    factor = jnp.linalg.cholesky(gram_total)
    orthonormal = lax.linalg.triangular_solve(factor, powered, left_side=False, lower=True, transpose_a=True)
    coefficients = jnp.einsum('ik,ir->kr', summed, orthonormal, precision=high)
    new_momentum = summed - 0.05 * jnp.einsum('ir,kr->ik', orthonormal, coefficients, precision=high)
    squares = lax.optimization_barrier(jnp.sum(coefficients * coefficients, axis=0))
    new_basis = coefficients / jnp.sqrt(squares + 1e-06)
    rms_scale = (M_ROWS * N_COLS / RANK) ** 0.5
    update = (rms_scale * jnp.einsum('ir,kr->ik', orthonormal, new_basis, precision=high)).astype(jnp.bfloat16)
    return (new_momentum, new_basis, update)
```

```python
import jax
import jax.numpy as jnp
from jax import lax
from jax.experimental import pallas as pl
from jax.experimental.pallas import tpu as pltpu
from jax.sharding import PartitionSpec as P

HIGH = lax.Precision.HIGH
HIGHEST = lax.Precision.HIGHEST
HALF = 128
GROUP = 8


def col_core(i):
    return i ^ 1


def col_x(i, s):
    return ((i // 2 + s) % 4) * 2 + i % 2


def row_y(i, s):
    return ((i // 8 + s) % 4) * 8 + i % 8


def row_z(i, s):
    return (i // 8) * 8 + (i % 8 + s) % 8


def send(value, axis, move, size):
    return lax.ppermute(value, axis, [(i, move(i)) for i in range(size)])


def scatter_sum(value, axis, move, size, parts, position):
    chunks = value.reshape(parts, value.shape[0] // parts, value.shape[1])
    total = lax.dynamic_index_in_dim(chunks, position, 0, False)
    for s in range(1, parts):
        away = lax.dynamic_index_in_dim(chunks, (position + s) % parts, 0, False)
        total = total + send(away, axis, lambda i: move(i, s), size)
    return total


def gather(value, axis, move, size, parts, position):
    out = jnp.zeros((parts,) + value.shape, value.dtype)
    out = lax.dynamic_update_index_in_dim(out, value, position, 0)
    for s in range(1, parts):
        came = send(value, axis, lambda i: move(i, s), size)
        out = lax.dynamic_update_index_in_dim(out, came, (position - s) % parts, 0)
    return out.reshape(parts * value.shape[0], value.shape[1])


def splat_row(value, row):
    return jnp.broadcast_to(value[row : row + 1, :], value.shape)


def splat_col(value, col):
    return jnp.broadcast_to(value[:, col : col + 1], value.shape)


def inverse_factor(groups):
    lane = lax.broadcasted_iota(jnp.int32, (GROUP, HALF), 1)
    sub = lax.broadcasted_iota(jnp.int32, (GROUP, HALF), 0)
    groups = list(groups)
    count = len(groups)
    result = []
    for g in range(count):
        base = g * GROUP
        inside = (lane >= base) & (lane < base + GROUP)
        pivot = groups[g]
        cols = [splat_col(pivot, base + a) for a in range(GROUP)]
        s = [[splat_row(cols[a], b) if b >= a else None for a in range(GROUP)] for b in range(GROUP)]
        low = [[None] * GROUP for _ in range(GROUP)]
        inverse = []
        for a in range(GROUP):
            inverse.append(1.0 / s[a][a])
            for b in range(a + 1, GROUP):
                low[b][a] = s[b][a] * inverse[a]
            for b in range(a + 1, GROUP):
                for c in range(a + 1, b + 1):
                    s[b][c] = s[b][c] - low[b][a] * s[c][a]
        outside = jnp.where(inside, 0.0, pivot)
        rows = []
        for a in range(GROUP):
            row = splat_row(outside, a)
            for e in range(a):
                row = row - low[a][e] * rows[e]
            rows.append(jnp.where(lane == base + a, 1.0, row))
        for i in range(g + 1, count):
            here = groups[i]
            kept = jnp.where(inside, 0.0, here)
            factors = []
            for a in range(GROUP):
                c = splat_col(here, base + a)
                for e in range(a):
                    c = c - factors[e] * s[a][e]
                factors.append(c * inverse[a])
            for a in range(GROUP):
                kept = kept - factors[a] * rows[a]
            groups[i] = kept
        final = jnp.zeros_like(pivot)
        for a in range(GROUP):
            final = jnp.where(sub == a, rows[a] * lax.rsqrt(s[a][a]), final)
        result.append(jnp.where(lane <= sub + base, final, 0.0))
    return result


def mm(a, b, ca, cb, precision):
    return lax.dot_general(
        a, b, (((ca,), (cb,)), ((), ())), precision=precision, preferred_element_type=jnp.float32
    )


def factor_kernel(gram_ref, square_ref, inverse_ref, scale_ref):
    def rows_of(value):
        return [value[GROUP * g : GROUP * (g + 1), :] for g in range(HALF // GROUP)]

    w11 = jnp.concatenate(inverse_factor(rows_of(gram_ref[:HALF, :HALF])), axis=0)
    l21 = mm(gram_ref[HALF:, :HALF], w11, 1, 1, HIGHEST)
    rest = gram_ref[HALF:, HALF:] - mm(l21, l21, 1, 1, HIGHEST)
    w22 = jnp.concatenate(inverse_factor(rows_of(rest)), axis=0)
    w21 = -mm(w22, mm(l21, w11, 1, 0, HIGHEST), 1, 0, HIGHEST)
    inverse_ref[:HALF, :HALF] = w11
    inverse_ref[:HALF, HALF:] = jnp.zeros_like(w11)
    inverse_ref[HALF:, :HALF] = w21
    inverse_ref[HALF:, HALF:] = w22
    w = inverse_ref[...]
    squares = jnp.sum(mm(w, square_ref[...], 1, 0, HIGHEST) * w, axis=1, keepdims=True)
    scale_ref[...] = jnp.broadcast_to(lax.rsqrt(squares + 1e-6), scale_ref.shape)


def factor(gram, square):
    rank = gram.shape[0]
    return pl.pallas_call(
        factor_kernel,
        out_shape=(
            jax.ShapeDtypeStruct((rank, rank), jnp.float32),
            jax.ShapeDtypeStruct((rank, HALF), jnp.float32),
        ),
        compiler_params=pltpu.CompilerParams(vmem_limit_bytes=32 * 1024 * 1024),
        name="factor",
    )(gram, square)


def shards(momentum, gradient, old_basis):
    row = lax.axis_index("row")
    col = lax.axis_index("col")
    y, z, x, core = row // 8, row % 8, col // 2, col % 2
    summed = momentum + gradient.astype(jnp.float32)
    part = jnp.dot(summed, old_basis, precision=HIGH)
    half = part.reshape(2, part.shape[0] // 2, -1)
    mine = lax.dynamic_index_in_dim(half, core, 0, False)
    mine = mine + send(lax.dynamic_index_in_dim(half, 1 - core, 0, False), "col", col_core, 8)
    mine = scatter_sum(mine, "col", col_x, 8, 4, x)
    mine = gather(mine, "col", col_x, 8, 4, x)
    other = send(mine, "col", col_core, 8)
    powered = jnp.where(core == 0, jnp.concatenate([mine, other]), jnp.concatenate([other, mine]))
    raw = lax.dot_general(summed, powered, (((0,), (0,)), ((), ())), precision=HIGH)
    raw = scatter_sum(raw, "row", row_y, 32, 4, y)
    raw = scatter_sum(raw, "row", row_z, 32, 8, z)
    raw = gather(raw, "row", row_z, 32, 8, z)
    raw = gather(raw, "row", row_y, 32, 4, y)
    gram = lax.dot_general(old_basis, raw, (((0,), (0,)), ((), ())), precision=HIGHEST)
    square = lax.dot_general(raw, raw, (((0,), (0,)), ((), ())), precision=HIGHEST)
    mine = jnp.where(core == 0, gram, square)
    mine = mine + send(jnp.where(core == 0, square, gram), "col", col_core, 8)
    mine = mine + sum(send(mine, "col", lambda i, s=s: col_x(i, s), 8) for s in (1, 2, 3))
    other = send(mine, "col", col_core, 8)
    gram = jnp.where(core == 0, mine, other)
    square = jnp.where(core == 0, other, mine)
    inverse, scale = factor(gram, square)
    scale = scale[:, 0]
    orthonormal = lax.dot_general(powered, inverse, (((1,), (1,)), ((), ())), precision=HIGH)
    coefficients = lax.dot_general(raw, inverse, (((1,), (1,)), ((), ())), precision=HIGH)
    new_basis = coefficients * scale
    new_momentum = summed - 0.05 * lax.dot_general(
        orthonormal, coefficients, (((1,), (1,)), ((), ()))
    )
    rms_scale = (28672 * 8192 / 256) ** 0.5
    update = rms_scale * lax.dot_general(
        orthonormal, new_basis, (((1,), (1,)), ((), ())), precision=HIGH
    )
    return (new_momentum, new_basis, update.astype(jnp.bfloat16))


def solution(mesh):
    placed = (P("row", "col"), P("row", "col"), P("col", None))
    return jax.shard_map(
        shards,
        mesh=mesh,
        in_specs=placed,
        out_specs=(P("row", "col"), P("col", None), P("row", "col")),
        check_vma=False,
    )
```

```python
import functools

import jax
import jax.numpy as jnp
from jax import lax
from jax.experimental import pallas as pl
from jax.experimental.pallas import tpu as pltpu
from jax.sharding import PartitionSpec as P

HIGHEST = lax.Precision.HIGHEST
F32 = jnp.float32
BF16 = jnp.bfloat16
HALF = 128
GROUP = 8
ROWS = 896
COLS = 1024
RANK = 256
PIECE = 112
SLAB = 256
CHUNK = 32
LIMIT = pltpu.CompilerParams(vmem_limit_bytes=32 * 1024 * 1024)


def send(value, axis, move, size):
    return lax.ppermute(value, axis, [(i, move(i)) for i in range(size)])


def send_core(value):
    return send(value, "col", lambda i: i ^ 1, 8)


def send_x(value, s):
    return send(value, "col", lambda i: ((i // 2 + s) % 4) * 2 + i % 2, 8)


def send_y(value, s):
    return send(value, "row", lambda i: ((i // 8 + s) % 4) * 8 + i % 8, 32)


def send_z(value, s):
    return send(value, "row", lambda i: (i // 8) * 8 + (i % 8 + s) % 8, 32)


def send_pair(value):
    return send(value, "row", lambda i: i ^ 1, 32)


def ring_sum(own, came):
    return (own + came[2]) + (came[1] + came[3])


def mm(a, b, ca, cb, precision=None):
    return lax.dot_general(
        a, b, (((ca,), (cb,)), ((), ())), precision=precision, preferred_element_type=F32
    )


def split(value):
    high = value.astype(BF16)
    return high, (value - high.astype(F32)).astype(BF16)


def mm3(a, b, ca, cb):
    return mm(a[0], b[0], ca, cb) + (mm(a[0], b[1], ca, cb) + mm(a[1], b[0], ca, cb))


def whole():
    return pl.BlockSpec(memory_space=pltpu.VMEM)


def anywhere():
    return pl.BlockSpec(memory_space=pl.ANY)


def scalars():
    return pl.BlockSpec(memory_space=pltpu.SMEM)


def power_kernel(own, pos_ref, m_ref, g_ref, b_ref, out_ref, m_buf, g_buf, sems):
    x, core = pos_ref[2], pos_ref[3]
    half = core if own else 1 - core
    copies = []
    for s in range(4):
        start = pl.multiple_of(half * (4 * PIECE) + lax.rem(x + s, 4) * PIECE, PIECE)
        there = pl.ds(s * PIECE, PIECE)
        copies.append(pltpu.make_async_copy(m_ref.at[pl.ds(start, PIECE)], m_buf.at[there], sems.at[s, 0]))
        copies.append(pltpu.make_async_copy(g_ref.at[pl.ds(start, PIECE)], g_buf.at[there], sems.at[s, 1]))
    for copy in copies:
        copy.start()
    basis = split(b_ref[...])
    for t in range(2):
        for copy in copies[4 * t : 4 * t + 4]:
            copy.wait()
        rows = pl.ds(t * 2 * PIECE, 2 * PIECE)
        out_ref[rows] = mm3(split(m_buf[rows] + g_buf[rows].astype(F32)), basis, 1, 0)


def power(pos, momentum, gradient, basis, own):
    return pl.pallas_call(
        functools.partial(power_kernel, own),
        out_shape=jax.ShapeDtypeStruct((4 * PIECE, RANK), F32),
        in_specs=[scalars(), anywhere(), anywhere(), whole()],
        out_specs=whole(),
        scratch_shapes=[
            pltpu.VMEM((4 * PIECE, COLS), F32),
            pltpu.VMEM((4 * PIECE, COLS), BF16),
            pltpu.SemaphoreType.DMA((4, 2)),
        ],
        compiler_params=LIMIT,
        cost_estimate=pl.CostEstimate(flops=6 * 448 * 1024 * 256, bytes_accessed=4 << 20, transcendentals=0),
        name="power",
    )(pos, momentum, gradient, basis)


def assemble_kernel(pos_ref, *refs):
    x, core = pos_ref[2], pos_ref[3]
    pieces, (out_ref, high_ref, low_ref, gram_ref) = refs[:8], refs[8:]
    for a in range(4):
        place = lax.rem(x + 4 - a, 4) * PIECE
        for half, piece in ((core, pieces[a]), (1 - core, pieces[4 + a])):
            out_ref[pl.ds(pl.multiple_of(half * (4 * PIECE) + place, PIECE), PIECE), :] = piece[...]
    value = out_ref[...]
    high, low = split(value)
    high_ref[...] = high
    low_ref[...] = low
    gram_ref[...] = mm(value, value, 0, 0, HIGHEST)


def assemble(pos, pieces):
    return pl.pallas_call(
        assemble_kernel,
        out_shape=(
            jax.ShapeDtypeStruct((ROWS, RANK), F32),
            jax.ShapeDtypeStruct((ROWS, RANK), BF16),
            jax.ShapeDtypeStruct((ROWS, RANK), BF16),
            jax.ShapeDtypeStruct((RANK, RANK), F32),
        ),
        in_specs=[scalars()] + [whole()] * 8,
        out_specs=(whole(),) * 4,
        compiler_params=LIMIT,
        name="assemble",
    )(pos, *pieces)


def slab_kernel(shift, pos_ref, m_ref, g_ref, high_ref, low_ref, gram_ref, out_ref, m_buf, g_buf, total, sems):
    y, z, x, core = pos_ref[0], pos_ref[1], pos_ref[2], pos_ref[3]
    target = lax.rem(y + shift, 4)
    columns = pl.ds(pl.multiple_of(target * SLAB, SLAB), SLAB)
    copies = []
    for t in range(2):
        rows = pl.ds(t * (ROWS // 2), ROWS // 2)
        copies.append(pltpu.make_async_copy(m_ref.at[rows, columns], m_buf.at[rows], sems.at[t, 0]))
        copies.append(pltpu.make_async_copy(g_ref.at[rows, columns], g_buf.at[rows], sems.at[t, 1]))
    for copy in copies:
        copy.start()
    for t in range(2):
        copies[2 * t].wait()
        copies[2 * t + 1].wait()
        rows = pl.ds(t * (ROWS // 2), ROWS // 2)
        summed = split(m_buf[rows] + g_buf[rows].astype(F32))
        part = mm3(summed, (high_ref[rows], low_ref[rows]), 0, 0)
        total[...] = part if t == 0 else total[...] + part
    for a in range(4):
        for b in range(2):
            source = lax.rem(z + 2 * a, 8) + (b - 2 * b * lax.rem(z, 2))
            source = pl.multiple_of(source * CHUNK, CHUNK)
            out_ref[pl.ds((2 * a + b) * CHUNK, CHUNK), :] = total[pl.ds(source, CHUNK), :]
    line = pl.multiple_of((x * 2 + core) * 32 + target * GROUP, GROUP)
    out_ref[pl.ds(SLAB, GROUP), :] = gram_ref[pl.ds(line, GROUP), :]


def slab(pos, momentum, gradient, high, low, gram, shift):
    return pl.pallas_call(
        functools.partial(slab_kernel, shift),
        out_shape=jax.ShapeDtypeStruct((SLAB + GROUP, RANK), F32),
        in_specs=[scalars(), anywhere(), anywhere(), whole(), whole(), whole()],
        out_specs=whole(),
        scratch_shapes=[
            pltpu.VMEM((ROWS, SLAB), F32),
            pltpu.VMEM((ROWS, SLAB), BF16),
            pltpu.VMEM((SLAB, RANK), F32),
            pltpu.SemaphoreType.DMA((2, 2)),
        ],
        compiler_params=LIMIT,
        cost_estimate=pl.CostEstimate(flops=6 * 896 * 256 * 256, bytes_accessed=3 << 20, transcendentals=0),
        name="slab",
    )(pos, momentum, gradient, high, low, gram)


def splat_row(value, row):
    return jnp.broadcast_to(value[row : row + 1, :], value.shape)


def splat_col(value, col):
    return jnp.broadcast_to(value[:, col : col + 1], value.shape)


def inverse_factor(groups):
    lane = lax.broadcasted_iota(jnp.int32, (GROUP, HALF), 1)
    sub = lax.broadcasted_iota(jnp.int32, (GROUP, HALF), 0)
    groups = list(groups)
    count = len(groups)
    result = []
    for g in range(count):
        base = g * GROUP
        inside = (lane >= base) & (lane < base + GROUP)
        pivot = groups[g]
        cols = [splat_col(pivot, base + a) for a in range(GROUP)]
        s = [[splat_row(cols[a], b) if b >= a else None for a in range(GROUP)] for b in range(GROUP)]
        low = [[None] * GROUP for _ in range(GROUP)]
        inverse = []
        for a in range(GROUP):
            inverse.append(1.0 / s[a][a])
            for b in range(a + 1, GROUP):
                low[b][a] = s[b][a] * inverse[a]
            for b in range(a + 1, GROUP):
                for c in range(a + 1, b + 1):
                    s[b][c] = s[b][c] - low[b][a] * s[c][a]
        outside = jnp.where(inside, 0.0, pivot)
        rows = []
        for a in range(GROUP):
            row = splat_row(outside, a)
            for e in range(a):
                row = row - low[a][e] * rows[e]
            rows.append(jnp.where(lane == base + a, 1.0, row))
        for i in range(g + 1, count):
            here = groups[i]
            kept = jnp.where(inside, 0.0, here)
            factors = []
            for a in range(GROUP):
                c = splat_col(here, base + a)
                for e in range(a):
                    c = c - factors[e] * s[a][e]
                factors.append(c * inverse[a])
            for a in range(GROUP):
                kept = kept - factors[a] * rows[a]
            groups[i] = kept
        final = jnp.zeros_like(pivot)
        for a in range(GROUP):
            final = jnp.where(sub == a, rows[a] * lax.rsqrt(s[a][a]), final)
        result.append(jnp.where(lane <= sub + base, final, 0.0))
    return result


def factor_kernel(pos_ref, p0, p1, p2, p3, inverse_ref, coeff_ref, square_ref, raw, gram):
    y, z, x, core = pos_ref[0], pos_ref[1], pos_ref[2], pos_ref[3]
    for j, piece in enumerate((p0, p1, p2, p3)):
        from_y = lax.rem(y + 4 - j, 4)
        for a in range(4):
            for b in range(2):
                from_z = lax.rem(z + 8 - 2 * a, 8) + (b - 2 * b * lax.rem(z, 2))
                place = pl.multiple_of((from_y * 8 + from_z) * CHUNK, CHUNK)
                raw[pl.ds(place, CHUNK), :] = piece[pl.ds((2 * a + b) * CHUNK, CHUNK), :]
                from_x = lax.rem(x + 4 - a, 4)
                from_core = core if b == 0 else 1 - core
                place = pl.multiple_of((from_x * 2 + from_core) * 32 + from_y * GROUP, GROUP)
                gram[pl.ds(place, GROUP), :] = piece[pl.ds(SLAB + b * 32 + a * GROUP, GROUP), :]

    def rows_of(value):
        return [value[GROUP * g : GROUP * (g + 1), :] for g in range(HALF // GROUP)]

    w11 = jnp.concatenate(inverse_factor(rows_of(gram[:HALF, :HALF])), axis=0)
    l21 = mm(gram[HALF:, :HALF], w11, 1, 1, HIGHEST)
    rest = gram[HALF:, HALF:] - mm(l21, l21, 1, 1, HIGHEST)
    w22 = jnp.concatenate(inverse_factor(rows_of(rest)), axis=0)
    w21 = -mm(w22, mm(l21, w11, 1, 0, HIGHEST), 1, 0, HIGHEST)
    inverse_ref[:HALF, :HALF] = w11
    inverse_ref[:HALF, HALF:] = jnp.zeros_like(w11)
    inverse_ref[HALF:, :HALF] = w21
    inverse_ref[HALF:, HALF:] = w22
    coefficients = mm3(split(raw[...]), split(inverse_ref[...]), 1, 1)
    coeff_ref[...] = coefficients
    square_ref[...] = jnp.sum(coefficients * coefficients, axis=0, keepdims=True)


def factor(pos, pieces):
    return pl.pallas_call(
        factor_kernel,
        out_shape=(
            jax.ShapeDtypeStruct((RANK, RANK), F32),
            jax.ShapeDtypeStruct((COLS, RANK), F32),
            jax.ShapeDtypeStruct((1, RANK), F32),
        ),
        in_specs=[scalars()] + [whole()] * 4,
        out_specs=(whole(),) * 3,
        scratch_shapes=[pltpu.VMEM((COLS, RANK), F32), pltpu.VMEM((RANK, RANK), F32)],
        compiler_params=LIMIT,
        name="factor",
    )(pos, *pieces)


TILE = 224


def feedback_kernel(m_ref, g_ref, p_ref, w_ref, c_ref, out_ref, high_ref, low_ref, w_high, w_low, c_high):
    @pl.when(pl.program_id(0) == 0)
    def _():
        w_high[...], w_low[...] = split(w_ref[...])
        c_high[...] = c_ref[...].astype(BF16)

    q = mm3(split(p_ref[...]), (w_high[...], w_low[...]), 1, 1)
    high, low = split(q)
    high_ref[...] = high
    low_ref[...] = low
    out_ref[...] = m_ref[...] + g_ref[...].astype(F32) - 0.05 * mm(high, c_high[...], 1, 1)


def feedback(momentum, gradient, powered, inverse, coefficients):
    def tile(columns):
        return pl.BlockSpec((TILE, columns), lambda i: (i, 0))

    def fixed(shape):
        return pl.BlockSpec(shape, lambda i: (0, 0))

    return pl.pallas_call(
        feedback_kernel,
        grid=(ROWS // TILE,),
        out_shape=(
            jax.ShapeDtypeStruct((ROWS, COLS), F32),
            jax.ShapeDtypeStruct((ROWS, RANK), BF16),
            jax.ShapeDtypeStruct((ROWS, RANK), BF16),
        ),
        in_specs=[tile(COLS), tile(COLS), tile(RANK), fixed((RANK, RANK)), fixed((COLS, RANK))],
        out_specs=(tile(COLS), tile(RANK), tile(RANK)),
        scratch_shapes=[
            pltpu.VMEM((RANK, RANK), BF16),
            pltpu.VMEM((RANK, RANK), BF16),
            pltpu.VMEM((COLS, RANK), BF16),
        ],
        compiler_params=LIMIT,
        cost_estimate=pl.CostEstimate(flops=4 * 896 * 1024 * 256, bytes_accessed=10 << 20, transcendentals=0),
        name="feedback",
    )(momentum, gradient, powered, inverse, coefficients)


def update_kernel(scale, high_ref, low_ref, c_ref, s_ref, basis_ref, out_ref, b_high, b_low):
    @pl.when(pl.program_id(0) == 0)
    def _():
        basis = c_ref[...] / jnp.sqrt(s_ref[...] + 1e-6)
        basis_ref[...] = basis
        b_high[...], b_low[...] = split(basis)

    value = mm3((high_ref[...], low_ref[...]), (b_high[...], b_low[...]), 1, 1)
    out_ref[...] = (scale * value).astype(BF16)


def update(high, low, coefficients, squares, scale):
    def tile(columns):
        return pl.BlockSpec((TILE, columns), lambda i: (i, 0))

    def fixed(shape):
        return pl.BlockSpec(shape, lambda i: (0, 0))

    return pl.pallas_call(
        functools.partial(update_kernel, scale),
        grid=(ROWS // TILE,),
        out_shape=(
            jax.ShapeDtypeStruct((COLS, RANK), F32),
            jax.ShapeDtypeStruct((ROWS, COLS), BF16),
        ),
        in_specs=[tile(RANK), tile(RANK), fixed((COLS, RANK)), fixed((1, RANK))],
        out_specs=(fixed((COLS, RANK)), tile(COLS)),
        scratch_shapes=[pltpu.VMEM((COLS, RANK), BF16), pltpu.VMEM((COLS, RANK), BF16)],
        compiler_params=LIMIT,
        name="update",
    )(high, low, coefficients, squares)


def shards(momentum, gradient, old_basis):
    row = lax.axis_index("row")
    col = lax.axis_index("col")
    pos = jnp.stack([row // 8, row % 8, col // 2, col % 2]).astype(jnp.int32)

    away = power(pos, momentum, gradient, old_basis, False)
    came = send_core(away)
    here = power(pos, momentum, gradient, old_basis, True)
    parts = [here[s * PIECE : (s + 1) * PIECE] + came[s * PIECE : (s + 1) * PIECE] for s in range(4)]
    mine = ring_sum(parts[0], [None] + [send_x(parts[s], s) for s in (1, 2, 3)])
    pieces = [mine] + [send_x(mine, s) for s in (1, 2, 3)]
    pieces = pieces + [send_core(piece) for piece in pieces]
    powered, high, low, gram = assemble(pos, pieces)

    slabs = {s: slab(pos, momentum, gradient, high, low, gram, s) for s in (2, 1, 3, 0)}
    mine = ring_sum(slabs[0], [None] + [send_y(slabs[s], s) for s in (1, 2, 3)])
    lines = mine[SLAB:]
    parts = [jnp.concatenate([mine[64 * a : 64 * (a + 1)], lines]) for a in range(4)]
    mine = ring_sum(parts[0], [None] + [send_z(parts[a], 2 * a) for a in (1, 2, 3)])
    kept = jnp.concatenate([mine[:CHUNK], mine[64:]])
    mine = kept + send_pair(mine[CHUNK:])

    lines = mine[CHUNK:]
    mine = mine[:CHUNK]
    lines = jnp.concatenate([lines] + [send_x(lines, s) for s in (1, 2, 3)])
    lines = jnp.concatenate([lines, send_core(lines)])
    mine = jnp.concatenate([mine, send_pair(mine)])
    mine = jnp.concatenate([mine] + [send_z(mine, 2 * a) for a in (1, 2, 3)] + [lines])
    pieces = [mine] + [send_y(mine, s) for s in (1, 2, 3)]

    inverse, coefficients, squares = factor(pos, pieces)
    squares = squares + send_core(squares)
    squares = ring_sum(squares, [None] + [send_x(squares, s) for s in (1, 2, 3)])
    new_momentum, high, low = feedback(momentum, gradient, powered, inverse, coefficients)
    rms_scale = (28672 * 8192 / 256) ** 0.5
    new_basis, new_update = update(high, low, coefficients, squares, rms_scale)
    return (new_momentum, new_basis, new_update)


def solution(mesh):
    placed = (P("row", "col"), P("row", "col"), P("col", None))
    return jax.shard_map(
        shards,
        mesh=mesh,
        in_specs=placed,
        out_specs=(P("row", "col"), P("col", None), P("row", "col")),
        check_vma=False,
    )
```

```python
import functools

import jax
import jax.numpy as jnp
from jax import lax
from jax.experimental import pallas as pl
from jax.experimental.pallas import tpu as pltpu
from jax.sharding import PartitionSpec as P

HIGHEST = lax.Precision.HIGHEST
F32 = jnp.float32
BF16 = jnp.bfloat16
HALF = 128
GROUP = 8
ROWS = 896
COLS = 1024
RANK = 256
PIECE = 112
SLAB = 256
COEFF = 32
CHUNK = 40
LIMIT = pltpu.CompilerParams(vmem_limit_bytes=32 * 1024 * 1024)


def send(value, axis, move, size):
    return lax.ppermute(value, axis, [(i, move(i)) for i in range(size)])


def send_core(value):
    return send(value, "col", lambda i: i ^ 1, 8)


def send_x(value, s):
    return send(value, "col", lambda i: ((i // 2 + s) % 4) * 2 + i % 2, 8)


def send_y(value, s):
    return send(value, "row", lambda i: ((i // 8 + s) % 4) * 8 + i % 8, 32)


def send_z(value, s):
    return send(value, "row", lambda i: (i // 8) * 8 + (i % 8 + s) % 8, 32)


def send_pair(value):
    return send(value, "row", lambda i: i ^ 1, 32)


def ring_sum(own, came):
    return (own + came[2]) + (came[1] + came[3])


def mm(a, b, ca, cb, precision=None):
    return lax.dot_general(
        a, b, (((ca,), (cb,)), ((), ())), precision=precision, preferred_element_type=F32
    )


def split(value):
    high = value.astype(BF16)
    return high, (value - high.astype(F32)).astype(BF16)


def mm3(a, b, ca, cb):
    return mm(a[0], b[0], ca, cb) + (mm(a[0], b[1], ca, cb) + mm(a[1], b[0], ca, cb))


def whole():
    return pl.BlockSpec(memory_space=pltpu.VMEM)


def in_hbm():
    return pl.BlockSpec(memory_space=pltpu.HBM)


def scalars():
    return pl.BlockSpec(memory_space=pltpu.SMEM)


def row_start(half, x, s):
    return pl.multiple_of(half * (4 * PIECE) + lax.rem(x + s, 4) * PIECE, PIECE)


def power_kernel(own, pos_ref, m_ref, g_ref, b_ref, out_ref, high_ref, low_ref, m_buf, g_buf, b_buf, sems, b_sem):
    x, core = pos_ref[2], pos_ref[3]
    half = core if own else 1 - core
    load = pltpu.make_async_copy(b_ref, b_buf, b_sem)
    load.start()
    copies = []
    for s in range(4):
        here = pl.ds(row_start(half, x, s), PIECE)
        there = pl.ds(s * PIECE, PIECE)
        copies.append(pltpu.make_async_copy(m_ref.at[here], m_buf.at[there], sems.at[s, 0]))
        copies.append(pltpu.make_async_copy(g_ref.at[here], g_buf.at[there], sems.at[s, 1]))
    for copy in copies:
        copy.start()
    load.wait()
    basis = split(b_buf[...])
    for t in range(2):
        for copy in copies[4 * t : 4 * t + 4]:
            copy.wait()
        rows = pl.ds(t * 2 * PIECE, 2 * PIECE)
        high, low = split(m_buf[rows] + g_buf[rows].astype(F32))
        high_ref[rows] = high
        low_ref[rows] = low
        out_ref[rows] = mm3((high, low), basis, 1, 0)


def power(pos, momentum, gradient, basis, own):
    return pl.pallas_call(
        functools.partial(power_kernel, own),
        out_shape=(
            jax.ShapeDtypeStruct((4 * PIECE, RANK), F32),
            jax.ShapeDtypeStruct((4 * PIECE, COLS), BF16),
            jax.ShapeDtypeStruct((4 * PIECE, COLS), BF16),
        ),
        in_specs=[scalars(), in_hbm(), in_hbm(), in_hbm()],
        out_specs=(whole(),) * 3,
        scratch_shapes=[
            pltpu.VMEM((4 * PIECE, COLS), F32),
            pltpu.VMEM((4 * PIECE, COLS), BF16),
            pltpu.VMEM((COLS, RANK), F32),
            pltpu.SemaphoreType.DMA((4, 2)),
            pltpu.SemaphoreType.DMA,
        ],
        compiler_params=LIMIT,
        cost_estimate=pl.CostEstimate(flops=6 * 448 * 1024 * 256, bytes_accessed=4 << 20, transcendentals=0),
        name="power",
    )(pos, momentum, gradient, basis)


def assemble_kernel(own_ref, other_ref, high_ref, low_ref, gram_ref):
    for t, half_ref in enumerate((own_ref, other_ref)):
        high, low = split(half_ref[...])
        rows = pl.ds(t * 4 * PIECE, 4 * PIECE)
        high_ref[rows] = high
        low_ref[rows] = low
    value = (high_ref[...], low_ref[...])
    gram_ref[...] = mm3(value, value, 0, 0)


def assemble(own, other):
    return pl.pallas_call(
        assemble_kernel,
        out_shape=(
            jax.ShapeDtypeStruct((ROWS, RANK), BF16),
            jax.ShapeDtypeStruct((ROWS, RANK), BF16),
            jax.ShapeDtypeStruct((RANK, RANK), F32),
        ),
        in_specs=[whole()] * 2,
        out_specs=(whole(),) * 3,
        compiler_params=LIMIT,
        name="assemble",
    )(own, other)


def slab_kernel(shift, pos_ref, s0_high, s0_low, s1_high, s1_low, high_ref, low_ref, gram_ref, out_ref, total):
    y, z = pos_ref[0], pos_ref[1]
    target = lax.rem(y + shift, 4)
    columns = pl.ds(pl.multiple_of(target * SLAB, SLAB), SLAB)
    first, second = pl.ds(0, 4 * PIECE), pl.ds(4 * PIECE, 4 * PIECE)
    total[...] = mm3(
        (s0_high[:, columns], s0_low[:, columns]), (high_ref[first], low_ref[first]), 0, 0
    ) + mm3((s1_high[:, columns], s1_low[:, columns]), (high_ref[second], low_ref[second]), 0, 0)
    for a in range(4):
        for b in range(2):
            source = lax.rem(z + 2 * a, 8) + (b - 2 * b * lax.rem(z, 2))
            place = (2 * a + b) * CHUNK
            from_total = pl.ds(pl.multiple_of(source * COEFF, COEFF), COEFF)
            from_gram = pl.ds(pl.multiple_of(target * 64 + source * GROUP, GROUP), GROUP)
            out_ref[pl.ds(place, COEFF), :] = total[from_total, :]
            out_ref[pl.ds(place + COEFF, GROUP), :] = gram_ref[from_gram, :]


def slab(pos, summed, high, low, gram, shift):
    return pl.pallas_call(
        functools.partial(slab_kernel, shift),
        out_shape=jax.ShapeDtypeStruct((8 * CHUNK, RANK), F32),
        in_specs=[scalars()] + [whole()] * 7,
        out_specs=whole(),
        scratch_shapes=[pltpu.VMEM((SLAB, RANK), F32)],
        compiler_params=LIMIT,
        cost_estimate=pl.CostEstimate(flops=6 * 896 * 256 * 256, bytes_accessed=3 << 20, transcendentals=0),
        name="slab",
    )(pos, *summed, high, low, gram)


def splat_row(value, row):
    return jnp.broadcast_to(value[row : row + 1, :], value.shape)


def splat_col(value, col):
    return jnp.broadcast_to(value[:, col : col + 1], value.shape)


def inverse_factor(groups):
    lane = lax.broadcasted_iota(jnp.int32, (GROUP, HALF), 1)
    sub = lax.broadcasted_iota(jnp.int32, (GROUP, HALF), 0)
    groups = list(groups)
    count = len(groups)
    result = []
    for g in range(count):
        base = g * GROUP
        inside = (lane >= base) & (lane < base + GROUP)
        pivot = groups[g]
        cols = [splat_col(pivot, base + a) for a in range(GROUP)]
        s = [[splat_row(cols[a], b) if b >= a else None for a in range(GROUP)] for b in range(GROUP)]
        low = [[None] * GROUP for _ in range(GROUP)]
        inverse = []
        for a in range(GROUP):
            inverse.append(1.0 / s[a][a])
            for b in range(a + 1, GROUP):
                low[b][a] = s[b][a] * inverse[a]
            for b in range(a + 1, GROUP):
                for c in range(a + 1, b + 1):
                    s[b][c] = s[b][c] - low[b][a] * s[c][a]
        outside = jnp.where(inside, 0.0, pivot)
        rows = []
        for a in range(GROUP):
            row = splat_row(outside, a)
            for e in range(a):
                row = row - low[a][e] * rows[e]
            rows.append(jnp.where(lane == base + a, 1.0, row))
        for i in range(g + 1, count):
            here = groups[i]
            kept = jnp.where(inside, 0.0, here)
            factors = []
            for a in range(GROUP):
                c = splat_col(here, base + a)
                for e in range(a):
                    c = c - factors[e] * s[a][e]
                factors.append(c * inverse[a])
            for a in range(GROUP):
                kept = kept - factors[a] * rows[a]
            groups[i] = kept
        final = jnp.zeros_like(pivot)
        for a in range(GROUP):
            final = jnp.where(sub == a, rows[a] * lax.rsqrt(s[a][a]), final)
        result.append(jnp.where(lane <= sub + base, final, 0.0))
    return result


def factor_kernel(pos_ref, p0, p1, p2, p3, inverse_ref, coeff_ref, square_ref, raw, gram):
    y, z = pos_ref[0], pos_ref[1]
    for j, piece in enumerate((p0, p1, p2, p3)):
        from_y = lax.rem(y + 4 - j, 4)
        for a in range(4):
            for b in range(2):
                from_z = lax.rem(z + 8 - 2 * a, 8) + (b - 2 * b * lax.rem(z, 2))
                owner = from_y * 8 + from_z
                place = (2 * a + b) * CHUNK
                to_raw = pl.ds(pl.multiple_of(owner * COEFF, COEFF), COEFF)
                to_gram = pl.ds(pl.multiple_of(owner * GROUP, GROUP), GROUP)
                raw[to_raw, :] = piece[pl.ds(place, COEFF), :]
                gram[to_gram, :] = piece[pl.ds(place + COEFF, GROUP), :]

    def rows_of(value):
        return [value[GROUP * g : GROUP * (g + 1), :] for g in range(HALF // GROUP)]

    w11 = jnp.concatenate(inverse_factor(rows_of(gram[:HALF, :HALF])), axis=0)
    l21 = mm(gram[HALF:, :HALF], w11, 1, 1, HIGHEST)
    rest = gram[HALF:, HALF:] - mm(l21, l21, 1, 1, HIGHEST)
    w22 = jnp.concatenate(inverse_factor(rows_of(rest)), axis=0)
    w21 = -mm(w22, mm(l21, w11, 1, 0, HIGHEST), 1, 0, HIGHEST)
    inverse_ref[:HALF, :HALF] = w11
    inverse_ref[:HALF, HALF:] = jnp.zeros_like(w11)
    inverse_ref[HALF:, :HALF] = w21
    inverse_ref[HALF:, HALF:] = w22
    coefficients = mm3(split(raw[...]), split(inverse_ref[...]), 1, 1)
    coeff_ref[...] = coefficients
    square_ref[...] = jnp.sum(coefficients * coefficients, axis=0, keepdims=True)


def factor(pos, pieces):
    return pl.pallas_call(
        factor_kernel,
        out_shape=(
            jax.ShapeDtypeStruct((RANK, RANK), F32),
            jax.ShapeDtypeStruct((COLS, RANK), F32),
            jax.ShapeDtypeStruct((1, RANK), F32),
        ),
        in_specs=[scalars()] + [whole()] * 4,
        out_specs=(whole(),) * 3,
        scratch_shapes=[pltpu.VMEM((COLS, RANK), F32), pltpu.VMEM((RANK, RANK), F32)],
        compiler_params=LIMIT,
        name="factor",
    )(pos, *pieces)


def write_rows(pos_ref, half, value_ref, out_ref, sems):
    x, core = pos_ref[2], pos_ref[3]
    copies = []
    for s in range(4):
        there = pl.ds(row_start(core if half == 0 else 1 - core, x, s), PIECE)
        here = pl.ds((4 * half + s) * PIECE, PIECE)
        copies.append(pltpu.make_async_copy(value_ref.at[here], out_ref.at[there], sems.at[4 * half + s]))
        copies[-1].start()
    return copies


def feedback_kernel(
    pos_ref, s0_high, s0_low, s1_high, s1_low, p_high, p_low, w_ref, c_ref, out_ref, high_ref, low_ref, buf, sems
):
    inverse = split(w_ref[...])
    coefficients = c_ref[...].astype(BF16)
    copies = []
    for t, (s_high, s_low) in enumerate(((s0_high, s0_low), (s1_high, s1_low))):
        rows = pl.ds(t * 4 * PIECE, 4 * PIECE)
        high, low = split(mm3((p_high[rows], p_low[rows]), inverse, 1, 1))
        high_ref[rows] = high
        low_ref[rows] = low
        summed = s_high[...].astype(F32) + s_low[...].astype(F32)
        buf[rows] = summed - 0.05 * mm(high, coefficients, 1, 1)
        copies += write_rows(pos_ref, t, buf, out_ref, sems)
    for copy in copies:
        copy.wait()


def feedback(pos, summed, p_high, p_low, inverse, coefficients):
    return pl.pallas_call(
        feedback_kernel,
        out_shape=(
            jax.ShapeDtypeStruct((ROWS, COLS), F32),
            jax.ShapeDtypeStruct((ROWS, RANK), BF16),
            jax.ShapeDtypeStruct((ROWS, RANK), BF16),
        ),
        in_specs=[scalars()] + [whole()] * 8,
        out_specs=(in_hbm(), whole(), whole()),
        scratch_shapes=[pltpu.VMEM((ROWS, COLS), F32), pltpu.SemaphoreType.DMA((8,))],
        compiler_params=LIMIT,
        cost_estimate=pl.CostEstimate(flops=4 * 896 * 1024 * 256, bytes_accessed=10 << 20, transcendentals=0),
        name="feedback",
    )(pos, *summed, p_high, p_low, inverse, coefficients)


def update_kernel(scale, pos_ref, high_ref, low_ref, c_ref, s_ref, basis_ref, out_ref, b_buf, buf, b_sem, sems):
    basis = c_ref[...] * (1.0 / jnp.sqrt(s_ref[...] + 1e-6))
    b_buf[...] = basis
    store = pltpu.make_async_copy(b_buf, basis_ref, b_sem)
    store.start()
    basis = split(basis)
    copies = []
    for t in range(2):
        rows = pl.ds(t * 4 * PIECE, 4 * PIECE)
        buf[rows] = (scale * mm3((high_ref[rows], low_ref[rows]), basis, 1, 1)).astype(BF16)
        copies += write_rows(pos_ref, t, buf, out_ref, sems)
    store.wait()
    for copy in copies:
        copy.wait()


def update(pos, high, low, coefficients, squares, scale):
    return pl.pallas_call(
        functools.partial(update_kernel, scale),
        out_shape=(
            jax.ShapeDtypeStruct((COLS, RANK), F32),
            jax.ShapeDtypeStruct((ROWS, COLS), BF16),
        ),
        in_specs=[scalars()] + [whole()] * 4,
        out_specs=(in_hbm(), in_hbm()),
        scratch_shapes=[
            pltpu.VMEM((COLS, RANK), F32),
            pltpu.VMEM((ROWS, COLS), BF16),
            pltpu.SemaphoreType.DMA,
            pltpu.SemaphoreType.DMA((8,)),
        ],
        compiler_params=LIMIT,
        name="update",
    )(pos, high, low, coefficients, squares)


def shards(momentum, gradient, old_basis):
    row = lax.axis_index("row")
    col = lax.axis_index("col")
    arguments = (momentum, gradient, old_basis)
    momentum, gradient, old_basis = (pltpu.with_memory_space_constraint(v, pltpu.HBM) for v in arguments)
    pos = jnp.stack([row // 8, row % 8, col // 2, col % 2]).astype(jnp.int32)

    away, s1_high, s1_low = power(pos, momentum, gradient, old_basis, False)
    came = send_core(away)
    here, s0_high, s0_low = power(pos, momentum, gradient, old_basis, True)
    summed = (s0_high, s0_low, s1_high, s1_low)
    parts = [here[s * PIECE : (s + 1) * PIECE] + came[s * PIECE : (s + 1) * PIECE] for s in range(4)]
    mine = ring_sum(parts[0], [None] + [send_x(parts[s], s) for s in (1, 2, 3)])
    own = jnp.concatenate([mine] + [send_x(mine, s) for s in (3, 2, 1)])
    high, low, gram = assemble(own, send_core(own))

    slabs = {s: slab(pos, summed, high, low, gram, s) for s in (2, 1, 3, 0)}
    mine = ring_sum(slabs[0], [None] + [send_y(slabs[s], s) for s in (1, 2, 3)])
    parts = [mine[2 * CHUNK * a : 2 * CHUNK * (a + 1)] for a in range(4)]
    mine = ring_sum(parts[0], [None] + [send_z(parts[a], 2 * a) for a in (1, 2, 3)])
    mine = mine[:CHUNK] + send_pair(mine[CHUNK:])

    mine = jnp.concatenate([mine, send_pair(mine)])
    mine = jnp.concatenate([mine] + [send_z(mine, 2 * a) for a in (1, 2, 3)])
    pieces = [mine] + [send_y(mine, s) for s in (1, 2, 3)]

    inverse, coefficients, squares = factor(pos, pieces)
    squares = squares + send_core(squares)
    squares = ring_sum(squares, [None] + [send_x(squares, s) for s in (1, 2, 3)])
    new_momentum, high, low = feedback(pos, summed, high, low, inverse, coefficients)
    rms_scale = (28672 * 8192 / 256) ** 0.5
    new_basis, new_update = update(pos, high, low, coefficients, squares, rms_scale)
    return (new_momentum, new_basis, new_update)


def solution(mesh):
    placed = (P("row", "col"), P("row", "col"), P("col", None))
    return jax.shard_map(
        shards,
        mesh=mesh,
        in_specs=placed,
        out_specs=(P("row", "col"), P("col", None), P("row", "col")),
        check_vma=False,
    )
```

```python
import functools

import jax
import jax.numpy as jnp
from jax import lax
from jax.experimental import pallas as pl
from jax.experimental.pallas import tpu as pltpu
from jax.sharding import PartitionSpec as P

HIGHEST = lax.Precision.HIGHEST
F32 = jnp.float32
BF16 = jnp.bfloat16
HALF = 128
GROUP = 8
ROWS = 896
COLS = 1024
RANK = 256
PIECE = 112
SLAB = 256
COEFF = 32
CHUNK = 40
LIMIT = pltpu.CompilerParams(vmem_limit_bytes=32 * 1024 * 1024)


def send(value, axis, move, size):
    return lax.ppermute(value, axis, [(i, move(i)) for i in range(size)])


def send_core(value):
    return send(value, "col", lambda i: i ^ 1, 8)


def send_x(value, s):
    return send(value, "col", lambda i: ((i // 2 + s) % 4) * 2 + i % 2, 8)


def send_y(value, s):
    return send(value, "row", lambda i: ((i // 8 + s) % 4) * 8 + i % 8, 32)


def send_z(value, s):
    return send(value, "row", lambda i: (i // 8) * 8 + (i % 8 + s) % 8, 32)


def send_pair(value):
    return send(value, "row", lambda i: i ^ 1, 32)


def ring_sum(own, came):
    return (own + came[2]) + (came[1] + came[3])


def mm(a, b, ca, cb, precision=None):
    return lax.dot_general(
        a, b, (((ca,), (cb,)), ((), ())), precision=precision, preferred_element_type=F32
    )


def split(value):
    high = value.astype(BF16)
    return high, (value - high.astype(F32)).astype(BF16)


def mm3(a, b, ca, cb):
    return mm(a[0], b[0], ca, cb) + (mm(a[0], b[1], ca, cb) + mm(a[1], b[0], ca, cb))


def whole():
    return pl.BlockSpec(memory_space=pltpu.VMEM)


def in_hbm():
    return pl.BlockSpec(memory_space=pltpu.HBM)


def scalars():
    return pl.BlockSpec(memory_space=pltpu.SMEM)


def row_start(half, x, s):
    return pl.multiple_of(half * (4 * PIECE) + lax.rem(x + s, 4) * PIECE, PIECE)


def power_away_kernel(
    pos_ref, m_ref, g_ref, b_ref, out_ref, high_ref, low_ref, m_own, g_own, b_high, b_low, m_buf, g_buf, b_buf, sems, b_sem
):
    x, core = pos_ref[2], pos_ref[3]
    load = pltpu.make_async_copy(b_ref, b_buf, b_sem)
    away, own = [], []
    for s in range(4):
        there = pl.ds(s * PIECE, PIECE)
        here = pl.ds(row_start(1 - core, x, s), PIECE)
        away.append(pltpu.make_async_copy(m_ref.at[here], m_buf.at[there], sems.at[s, 0]))
        away.append(pltpu.make_async_copy(g_ref.at[here], g_buf.at[there], sems.at[s, 1]))
        here = pl.ds(row_start(core, x, s), PIECE)
        own.append(pltpu.make_async_copy(m_ref.at[here], m_own.at[there], sems.at[4 + s, 0]))
        own.append(pltpu.make_async_copy(g_ref.at[here], g_own.at[there], sems.at[4 + s, 1]))
    load.start()
    for copy in away:
        copy.start()
    load.wait()
    basis = split(b_buf[...])
    b_high[...], b_low[...] = basis
    for t in range(2):
        for copy in away[4 * t : 4 * t + 4]:
            copy.wait()
        if t == 0:
            for copy in own:
                copy.start()
        rows = pl.ds(t * 2 * PIECE, 2 * PIECE)
        high, low = split(m_buf[rows] + g_buf[rows].astype(F32))
        high_ref[rows] = high
        low_ref[rows] = low
        out_ref[rows] = mm3((high, low), basis, 1, 0)
    for copy in own:
        copy.wait()


def power_away(pos, momentum, gradient, basis):
    half = (4 * PIECE, COLS)
    return pl.pallas_call(
        power_away_kernel,
        out_shape=(
            jax.ShapeDtypeStruct((4 * PIECE, RANK), F32),
            jax.ShapeDtypeStruct(half, BF16),
            jax.ShapeDtypeStruct(half, BF16),
            jax.ShapeDtypeStruct(half, F32),
            jax.ShapeDtypeStruct(half, BF16),
            jax.ShapeDtypeStruct((COLS, RANK), BF16),
            jax.ShapeDtypeStruct((COLS, RANK), BF16),
        ),
        in_specs=[scalars(), in_hbm(), in_hbm(), in_hbm()],
        out_specs=(whole(),) * 7,
        scratch_shapes=[
            pltpu.VMEM(half, F32),
            pltpu.VMEM(half, BF16),
            pltpu.VMEM((COLS, RANK), F32),
            pltpu.SemaphoreType.DMA((8, 2)),
            pltpu.SemaphoreType.DMA,
        ],
        compiler_params=LIMIT,
        name="power_away",
    )(pos, momentum, gradient, basis)


def power_own_kernel(m_ref, g_ref, b_high, b_low, out_ref, high_ref, low_ref):
    for t in range(2):
        rows = pl.ds(t * 2 * PIECE, 2 * PIECE)
        high, low = split(m_ref[rows] + g_ref[rows].astype(F32))
        high_ref[rows] = high
        low_ref[rows] = low
        out_ref[rows] = mm3((high, low), (b_high[...], b_low[...]), 1, 0)


def power_own(momentum, gradient, b_high, b_low):
    return pl.pallas_call(
        power_own_kernel,
        out_shape=(
            jax.ShapeDtypeStruct((4 * PIECE, RANK), F32),
            jax.ShapeDtypeStruct((4 * PIECE, COLS), BF16),
            jax.ShapeDtypeStruct((4 * PIECE, COLS), BF16),
        ),
        in_specs=[whole()] * 4,
        out_specs=(whole(),) * 3,
        compiler_params=LIMIT,
        cost_estimate=pl.CostEstimate(flops=6 * 448 * 1024 * 256, bytes_accessed=4 << 20, transcendentals=0),
        name="power_own",
    )(momentum, gradient, b_high, b_low)


def assemble_kernel(own_ref, other_ref, high_ref, low_ref, gram_ref):
    for t, half_ref in enumerate((own_ref, other_ref)):
        high, low = split(half_ref[...])
        rows = pl.ds(t * 4 * PIECE, 4 * PIECE)
        high_ref[rows] = high
        low_ref[rows] = low
    value = (high_ref[...], low_ref[...])
    gram_ref[...] = mm3(value, value, 0, 0)


def assemble(own, other):
    return pl.pallas_call(
        assemble_kernel,
        out_shape=(
            jax.ShapeDtypeStruct((ROWS, RANK), BF16),
            jax.ShapeDtypeStruct((ROWS, RANK), BF16),
            jax.ShapeDtypeStruct((RANK, RANK), F32),
        ),
        in_specs=[whole()] * 2,
        out_specs=(whole(),) * 3,
        compiler_params=LIMIT,
        name="assemble",
    )(own, other)


def slab_kernel(shift, pos_ref, s0_high, s0_low, s1_high, s1_low, high_ref, low_ref, gram_ref, out0_ref, out1_ref, total):
    y, z = pos_ref[0], pos_ref[1]
    target = lax.rem(y + shift, 4)
    columns = pl.ds(pl.multiple_of(target * SLAB, SLAB), SLAB)
    first, second = pl.ds(0, 4 * PIECE), pl.ds(4 * PIECE, 4 * PIECE)
    total[...] = mm3(
        (s0_high[:, columns], s0_low[:, columns]), (high_ref[first], low_ref[first]), 0, 0
    ) + mm3((s1_high[:, columns], s1_low[:, columns]), (high_ref[second], low_ref[second]), 0, 0)
    for out_ref, position, a in ((out0_ref, 0, 2), (out0_ref, 1, 1), (out1_ref, 0, 3), (out1_ref, 1, 0)):
        for b in range(2):
            source = lax.rem(z + 2 * a, 8) + (b - 2 * b * lax.rem(z, 2))
            place = (2 * position + b) * CHUNK
            from_total = pl.ds(pl.multiple_of(source * COEFF, COEFF), COEFF)
            from_gram = pl.ds(pl.multiple_of(target * 64 + source * GROUP, GROUP), GROUP)
            out_ref[pl.ds(place, COEFF), :] = total[from_total, :]
            out_ref[pl.ds(place + COEFF, GROUP), :] = gram_ref[from_gram, :]


def slab(pos, summed, high, low, gram, shift):
    return pl.pallas_call(
        functools.partial(slab_kernel, shift),
        out_shape=(jax.ShapeDtypeStruct((4 * CHUNK, RANK), F32),) * 2,
        in_specs=[scalars()] + [whole()] * 7,
        out_specs=(whole(),) * 2,
        scratch_shapes=[pltpu.VMEM((SLAB, RANK), F32)],
        compiler_params=LIMIT,
        cost_estimate=pl.CostEstimate(flops=6 * 896 * 256 * 256, bytes_accessed=3 << 20, transcendentals=0),
        name="slab",
    )(pos, *summed, high, low, gram)


def splat_row(value, row):
    return jnp.broadcast_to(value[row : row + 1, :], value.shape)


def splat_col(value, col):
    return jnp.broadcast_to(value[:, col : col + 1], value.shape)


def owner(y, z, j, a, b):
    from_z = lax.rem(z + 8 - 2 * a, 8) + (b - 2 * b * lax.rem(z, 2))
    return lax.rem(y + 4 - j, 4) * 8 + from_z


def inverse_factor(groups):
    lane = lax.broadcasted_iota(jnp.int32, (GROUP, HALF), 1)
    sub = lax.broadcasted_iota(jnp.int32, (GROUP, HALF), 0)
    groups = list(groups)
    count = len(groups)
    result = []
    for g in range(count):
        base = g * GROUP
        inside = (lane >= base) & (lane < base + GROUP)
        pivot = groups[g]
        cols = [splat_col(pivot, base + a) for a in range(GROUP)]
        s = [[splat_row(cols[a], b) if b >= a else None for a in range(GROUP)] for b in range(GROUP)]
        low = [[None] * GROUP for _ in range(GROUP)]
        inverse = []
        for a in range(GROUP):
            inverse.append(1.0 / s[a][a])
            for b in range(a + 1, GROUP):
                low[b][a] = s[b][a] * inverse[a]
            for b in range(a + 1, GROUP):
                for c in range(a + 1, b + 1):
                    s[b][c] = s[b][c] - low[b][a] * s[c][a]
        outside = jnp.where(inside, 0.0, pivot)
        rows = []
        for a in range(GROUP):
            row = splat_row(outside, a)
            for e in range(a):
                row = row - low[a][e] * rows[e]
            rows.append(jnp.where(lane == base + a, 1.0, row))
        for i in range(g + 1, count):
            here = groups[i]
            kept = jnp.where(inside, 0.0, here)
            factors = []
            for a in range(GROUP):
                c = splat_col(here, base + a)
                for e in range(a):
                    c = c - factors[e] * s[a][e]
                factors.append(c * inverse[a])
            for a in range(GROUP):
                kept = kept - factors[a] * rows[a]
            groups[i] = kept
        final = jnp.zeros_like(pivot)
        for a in range(GROUP):
            final = jnp.where(sub == a, rows[a] * lax.rsqrt(s[a][a]), final)
        result.append(jnp.where(lane <= sub + base, final, 0.0))
    return result


def factor_kernel(pos_ref, p0, p1, p2, p3, p_high, p_low, inverse_ref, high_ref, low_ref, gram):
    y, z = pos_ref[0], pos_ref[1]
    for j, piece in enumerate((p0, p1, p2, p3)):
        for a in range(4):
            for b in range(2):
                to_gram = pl.ds(pl.multiple_of(owner(y, z, j, a, b) * GROUP, GROUP), GROUP)
                gram[to_gram, :] = piece[pl.ds((2 * a + b) * GROUP, GROUP), :]

    def rows_of(value):
        return [value[GROUP * g : GROUP * (g + 1), :] for g in range(HALF // GROUP)]

    w11 = jnp.concatenate(inverse_factor(rows_of(gram[:HALF, :HALF])), axis=0)
    l21 = mm(gram[HALF:, :HALF], w11, 1, 1, HIGHEST)
    rest = gram[HALF:, HALF:] - mm(l21, l21, 1, 1, HIGHEST)
    w22 = jnp.concatenate(inverse_factor(rows_of(rest)), axis=0)
    w21 = -mm(w22, mm(l21, w11, 1, 0, HIGHEST), 1, 0, HIGHEST)
    inverse_ref[:HALF, :HALF] = w11
    inverse_ref[:HALF, HALF:] = jnp.zeros_like(w11)
    inverse_ref[HALF:, :HALF] = w21
    inverse_ref[HALF:, HALF:] = w22
    high, low = split(mm3((p_high[...], p_low[...]), split(inverse_ref[...]), 1, 1))
    high_ref[...] = high
    low_ref[...] = low


def factor(pos, pieces, p_high, p_low):
    return pl.pallas_call(
        factor_kernel,
        out_shape=(
            jax.ShapeDtypeStruct((RANK, RANK), F32),
            jax.ShapeDtypeStruct((ROWS, RANK), BF16),
            jax.ShapeDtypeStruct((ROWS, RANK), BF16),
        ),
        in_specs=[scalars()] + [whole()] * 6,
        out_specs=(whole(),) * 3,
        scratch_shapes=[pltpu.VMEM((RANK, RANK), F32)],
        compiler_params=LIMIT,
        cost_estimate=pl.CostEstimate(flops=10 << 30, bytes_accessed=32 << 20, transcendentals=0),
        name="factor",
    )(pos, *pieces, p_high, p_low)


def coefficients_kernel(pos_ref, p0, p1, p2, p3, inverse_ref, coeff_ref, square_ref):
    y, z = pos_ref[0], pos_ref[1]
    inverse = split(inverse_ref[...])
    for j, piece in enumerate((p0, p1, p2, p3)):
        value = mm3(split(piece[...]), inverse, 1, 1)
        for a in range(4):
            for b in range(2):
                place = pl.ds(pl.multiple_of(owner(y, z, j, a, b) * COEFF, COEFF), COEFF)
                coeff_ref[place, :] = value[(2 * a + b) * COEFF : (2 * a + b + 1) * COEFF]
    value = coeff_ref[...]
    square_ref[...] = jnp.sum(value * value, axis=0, keepdims=True)


def coefficients_of(pos, pieces, inverse):
    return pl.pallas_call(
        coefficients_kernel,
        out_shape=(jax.ShapeDtypeStruct((COLS, RANK), F32), jax.ShapeDtypeStruct((1, RANK), F32)),
        in_specs=[scalars()] + [whole()] * 5,
        out_specs=(whole(),) * 2,
        compiler_params=LIMIT,
        name="coefficients",
    )(pos, *pieces, inverse)


def write_rows(pos_ref, half, value_ref, out_ref, sems):
    x, core = pos_ref[2], pos_ref[3]
    copies = []
    for s in range(4):
        there = pl.ds(row_start(core if half == 0 else 1 - core, x, s), PIECE)
        here = pl.ds((4 * half + s) * PIECE, PIECE)
        copies.append(pltpu.make_async_copy(value_ref.at[here], out_ref.at[there], sems.at[4 * half + s]))
        copies[-1].start()
    return copies


def feedback_kernel(pos_ref, s0_high, s0_low, s1_high, s1_low, q_ref, c_ref, out_ref, buf, sems):
    coefficients = c_ref[...].astype(BF16)
    copies = []
    for t, (s_high, s_low) in enumerate(((s0_high, s0_low), (s1_high, s1_low))):
        rows = pl.ds(t * 4 * PIECE, 4 * PIECE)
        summed = s_high[...].astype(F32) + s_low[...].astype(F32)
        buf[rows] = summed - 0.05 * mm(q_ref[rows], coefficients, 1, 1)
        copies += write_rows(pos_ref, t, buf, out_ref, sems)
    for copy in copies:
        copy.wait()


def feedback(pos, summed, high, coefficients):
    return pl.pallas_call(
        feedback_kernel,
        out_shape=jax.ShapeDtypeStruct((ROWS, COLS), F32),
        in_specs=[scalars()] + [whole()] * 6,
        out_specs=in_hbm(),
        scratch_shapes=[pltpu.VMEM((ROWS, COLS), F32), pltpu.SemaphoreType.DMA((8,))],
        compiler_params=LIMIT,
        cost_estimate=pl.CostEstimate(flops=4 * 896 * 1024 * 256, bytes_accessed=10 << 20, transcendentals=0),
        name="feedback",
    )(pos, *summed, high, coefficients)


def update_kernel(scale, pos_ref, high_ref, low_ref, c_ref, s_ref, basis_ref, out_ref, b_buf, buf, b_sem, sems):
    basis = c_ref[...] * (1.0 / jnp.sqrt(s_ref[...] + 1e-6))
    b_buf[...] = basis
    store = pltpu.make_async_copy(b_buf, basis_ref, b_sem)
    store.start()
    basis = split(basis)
    copies = []
    for t in range(2):
        rows = pl.ds(t * 4 * PIECE, 4 * PIECE)
        buf[rows] = (scale * mm3((high_ref[rows], low_ref[rows]), basis, 1, 1)).astype(BF16)
        copies += write_rows(pos_ref, t, buf, out_ref, sems)
    store.wait()
    for copy in copies:
        copy.wait()


def update(pos, high, low, coefficients, squares, scale):
    return pl.pallas_call(
        functools.partial(update_kernel, scale),
        out_shape=(
            jax.ShapeDtypeStruct((COLS, RANK), F32),
            jax.ShapeDtypeStruct((ROWS, COLS), BF16),
        ),
        in_specs=[scalars()] + [whole()] * 4,
        out_specs=(in_hbm(), in_hbm()),
        scratch_shapes=[
            pltpu.VMEM((COLS, RANK), F32),
            pltpu.VMEM((ROWS, COLS), BF16),
            pltpu.SemaphoreType.DMA,
            pltpu.SemaphoreType.DMA((8,)),
        ],
        compiler_params=LIMIT,
        name="update",
    )(pos, high, low, coefficients, squares)


def shards(momentum, gradient, old_basis):
    row = lax.axis_index("row")
    col = lax.axis_index("col")
    arguments = (momentum, gradient, old_basis)
    momentum, gradient, old_basis = (pltpu.with_memory_space_constraint(v, pltpu.HBM) for v in arguments)
    pos = jnp.stack([row // 8, row % 8, col // 2, col % 2]).astype(jnp.int32)

    away, s1_high, s1_low, m_own, g_own, b_high, b_low = power_away(pos, momentum, gradient, old_basis)
    came = send_core(away)
    here, s0_high, s0_low = power_own(m_own, g_own, b_high, b_low)
    summed = (s0_high, s0_low, s1_high, s1_low)
    parts = [here[s * PIECE : (s + 1) * PIECE] + came[s * PIECE : (s + 1) * PIECE] for s in range(4)]
    mine = ring_sum(parts[0], [None] + [send_x(parts[s], s) for s in (1, 2, 3)])
    own = jnp.concatenate([mine] + [send_x(mine, s) for s in (3, 2, 1)])
    p_high, p_low, gram = assemble(own, send_core(own))

    slabs = {s: slab(pos, summed, p_high, p_low, gram, s) for s in (2, 1, 3, 0)}
    part0, part1 = (
        ring_sum(slabs[0][h], [None] + [send_y(slabs[s][h], s) for s in (1, 2, 3)]) for h in range(2)
    )
    two = 2 * CHUNK
    came2, came1 = send_z(part0[:two], 4), send_z(part0[two:], 2)
    mine = ring_sum(part1[two:], [None, came1, came2, send_z(part1[:two], 6)])
    mine = mine[:CHUNK] + send_pair(mine[CHUNK:])

    other = send_pair(mine)
    mine = jnp.concatenate([mine[:COEFF], other[:COEFF], mine[COEFF:], other[COEFF:]])
    pieces = [mine] + [send_z(mine, 2 * a) for a in (1, 2, 3)]
    gram = jnp.concatenate([piece[2 * COEFF :] for piece in pieces])
    raw = jnp.concatenate([piece[: 2 * COEFF] for piece in pieces])
    grams = [gram] + [send_y(gram, s) for s in (1, 2, 3)]
    raws = [raw] + [send_y(raw, s) for s in (1, 2, 3)]
    inverse, high, low = factor(pos, grams, p_high, p_low)

    coefficients, squares = coefficients_of(pos, raws, inverse)
    came = [send_x(squares, s) for s in (1, 2, 3)]
    new_momentum = feedback(pos, summed, high, coefficients)
    new_momentum, *came = lax.optimization_barrier((new_momentum, *came))
    squares = ring_sum(squares, [None] + came)
    squares = squares + send_core(squares)
    rms_scale = (28672 * 8192 / 256) ** 0.5
    new_basis, new_update = update(pos, high, low, coefficients, squares, rms_scale)
    return (new_momentum, new_basis, new_update)


def solution(mesh):
    placed = (P("row", "col"), P("row", "col"), P("col", None))
    return jax.shard_map(
        shards,
        mesh=mesh,
        in_specs=placed,
        out_specs=(P("row", "col"), P("col", None), P("row", "col")),
        check_vma=False,
    )
```

```python
import functools

import jax
import jax.numpy as jnp
from jax import lax
from jax.experimental import pallas as pl
from jax.experimental.pallas import tpu as pltpu
from jax.sharding import PartitionSpec as P

HIGHEST = lax.Precision.HIGHEST
F32 = jnp.float32
BF16 = jnp.bfloat16
HALF = 128
GROUP = 8
ROWS = 896
COLS = 1024
RANK = 256
PIECE = 112
SLAB = 256
COEFF = 32
CHUNK = 40
LIMIT = pltpu.CompilerParams(vmem_limit_bytes=32 * 1024 * 1024)


def send(value, axis, move, size):
    return lax.ppermute(value, axis, [(i, move(i)) for i in range(size)])


def send_core(value):
    return send(value, "col", lambda i: i ^ 1, 8)


def send_x(value, s):
    return send(value, "col", lambda i: ((i // 2 + s) % 4) * 2 + i % 2, 8)


def send_y(value, s):
    return send(value, "row", lambda i: ((i // 8 + s) % 4) * 8 + i % 8, 32)


def send_z(value, s):
    return send(value, "row", lambda i: (i // 8) * 8 + (i % 8 + s) % 8, 32)


def send_pair(value):
    return send(value, "row", lambda i: i ^ 1, 32)


def ring_sum(own, came):
    return (own + came[2]) + (came[1] + came[3])


def mm(a, b, ca, cb, precision=None):
    return lax.dot_general(
        a, b, (((ca,), (cb,)), ((), ())), precision=precision, preferred_element_type=F32
    )


def split(value):
    high = value.astype(BF16)
    return high, (value - high.astype(F32)).astype(BF16)


def mm3(a, b, ca, cb):
    return mm(a[0], b[0], ca, cb) + (mm(a[0], b[1], ca, cb) + mm(a[1], b[0], ca, cb))


def whole():
    return pl.BlockSpec(memory_space=pltpu.VMEM)


def in_hbm():
    return pl.BlockSpec(memory_space=pltpu.HBM)


def scalars():
    return pl.BlockSpec(memory_space=pltpu.SMEM)


def row_start(half, x, s):
    return pl.multiple_of(half * (4 * PIECE) + lax.rem(x + s, 4) * PIECE, PIECE)


def power_away_kernel(
    pos_ref, m_ref, g_ref, b_ref, out_ref, high_ref, low_ref, m_own, g_own, b_high, b_low, m_buf, g_buf, b_buf, sems, b_sem
):
    x, core = pos_ref[2], pos_ref[3]
    load = pltpu.make_async_copy(b_ref, b_buf, b_sem)
    away, own = [], []
    for s in range(4):
        there = pl.ds(s * PIECE, PIECE)
        here = pl.ds(row_start(1 - core, x, s), PIECE)
        away.append(pltpu.make_async_copy(m_ref.at[here], m_buf.at[there], sems.at[s, 0]))
        away.append(pltpu.make_async_copy(g_ref.at[here], g_buf.at[there], sems.at[s, 1]))
        here = pl.ds(row_start(core, x, s), PIECE)
        own.append(pltpu.make_async_copy(m_ref.at[here], m_own.at[there], sems.at[4 + s, 0]))
        own.append(pltpu.make_async_copy(g_ref.at[here], g_own.at[there], sems.at[4 + s, 1]))
    load.start()
    for copy in away + own:
        copy.start()
    load.wait()
    basis = split(b_buf[...])
    b_high[...], b_low[...] = basis
    for t in range(2):
        for copy in away[4 * t : 4 * t + 4]:
            copy.wait()
        rows = pl.ds(t * 2 * PIECE, 2 * PIECE)
        high, low = split(m_buf[rows] + g_buf[rows].astype(F32))
        high_ref[rows] = high
        low_ref[rows] = low
        out_ref[rows] = mm3((high, low), basis, 1, 0)
    for copy in own:
        copy.wait()


def power_away(pos, momentum, gradient, basis):
    half = (4 * PIECE, COLS)
    return pl.pallas_call(
        power_away_kernel,
        out_shape=(
            jax.ShapeDtypeStruct((4 * PIECE, RANK), F32),
            jax.ShapeDtypeStruct(half, BF16),
            jax.ShapeDtypeStruct(half, BF16),
            jax.ShapeDtypeStruct(half, F32),
            jax.ShapeDtypeStruct(half, BF16),
            jax.ShapeDtypeStruct((COLS, RANK), BF16),
            jax.ShapeDtypeStruct((COLS, RANK), BF16),
        ),
        in_specs=[scalars(), in_hbm(), in_hbm(), in_hbm()],
        out_specs=(whole(),) * 7,
        scratch_shapes=[
            pltpu.VMEM(half, F32),
            pltpu.VMEM(half, BF16),
            pltpu.VMEM((COLS, RANK), F32),
            pltpu.SemaphoreType.DMA((8, 2)),
            pltpu.SemaphoreType.DMA,
        ],
        compiler_params=LIMIT,
        name="power_away",
    )(pos, momentum, gradient, basis)


def power_own_kernel(m_ref, g_ref, b_high, b_low, out_ref, high_ref, low_ref):
    for t in range(2):
        rows = pl.ds(t * 2 * PIECE, 2 * PIECE)
        high, low = split(m_ref[rows] + g_ref[rows].astype(F32))
        high_ref[rows] = high
        low_ref[rows] = low
        out_ref[rows] = mm3((high, low), (b_high[...], b_low[...]), 1, 0)


def power_own(momentum, gradient, b_high, b_low):
    return pl.pallas_call(
        power_own_kernel,
        out_shape=(
            jax.ShapeDtypeStruct((4 * PIECE, RANK), F32),
            jax.ShapeDtypeStruct((4 * PIECE, COLS), BF16),
            jax.ShapeDtypeStruct((4 * PIECE, COLS), BF16),
        ),
        in_specs=[whole()] * 4,
        out_specs=(whole(),) * 3,
        compiler_params=LIMIT,
        cost_estimate=pl.CostEstimate(flops=6 * 448 * 1024 * 256, bytes_accessed=4 << 20, transcendentals=0),
        name="power_own",
    )(momentum, gradient, b_high, b_low)


def project_own_kernel(s_high, s_low, own_ref, high_ref, low_ref, total_ref, gram_ref):
    value = split(own_ref[...])
    high_ref[...], low_ref[...] = value
    gram_ref[...] = mm3(value, value, 0, 0)
    for t in range(4):
        columns = pl.ds(t * SLAB, SLAB)
        total_ref[columns, :] = mm3((s_high[:, columns], s_low[:, columns]), value, 0, 0)


def project_own(s_high, s_low, own):
    return pl.pallas_call(
        project_own_kernel,
        out_shape=(
            jax.ShapeDtypeStruct((4 * PIECE, RANK), BF16),
            jax.ShapeDtypeStruct((4 * PIECE, RANK), BF16),
            jax.ShapeDtypeStruct((COLS, RANK), F32),
            jax.ShapeDtypeStruct((RANK, RANK), F32),
        ),
        in_specs=[whole()] * 3,
        out_specs=(whole(),) * 4,
        compiler_params=LIMIT,
        cost_estimate=pl.CostEstimate(flops=6 * 448 * 1280 * 256, bytes_accessed=4 << 20, transcendentals=0),
        name="project_own",
    )(s_high, s_low, own)


def project_kernel(pos_ref, s_high, s_low, other_ref, total_ref, gram_ref, high_ref, low_ref, *refs):
    y, z = pos_ref[0], pos_ref[1]
    outs, (total, gram) = refs[:8], refs[8:]
    value = split(other_ref[...])
    high_ref[...], low_ref[...] = value
    gram[...] = gram_ref[...] + mm3(value, value, 0, 0)
    for t in range(4):
        columns = pl.ds(t * SLAB, SLAB)
        total[columns, :] = total_ref[columns, :] + mm3((s_high[:, columns], s_low[:, columns]), value, 0, 0)
    for shift in range(4):
        target = lax.rem(y + shift, 4) * 8
        for part, position, a in ((0, 0, 2), (0, 1, 1), (0, 2, 3), (1, 0, 0)):
            out_ref = outs[2 * shift + part]
            for b in range(2):
                source = target + lax.rem(z + 2 * a, 8) + (b - 2 * b * lax.rem(z, 2))
                place = (2 * position + b) * CHUNK
                from_total = pl.ds(pl.multiple_of(source * COEFF, COEFF), COEFF)
                from_gram = pl.ds(pl.multiple_of(source * GROUP, GROUP), GROUP)
                out_ref[pl.ds(place, COEFF), :] = total[from_total, :]
                out_ref[pl.ds(place + COEFF, GROUP), :] = gram[from_gram, :]


def project(pos, s_high, s_low, other, total, gram):
    return pl.pallas_call(
        project_kernel,
        out_shape=(
            jax.ShapeDtypeStruct((4 * PIECE, RANK), BF16),
            jax.ShapeDtypeStruct((4 * PIECE, RANK), BF16),
        )
        + (
            jax.ShapeDtypeStruct((6 * CHUNK, RANK), F32),
            jax.ShapeDtypeStruct((2 * CHUNK, RANK), F32),
        )
        * 4,
        in_specs=[scalars()] + [whole()] * 5,
        out_specs=(whole(),) * 10,
        scratch_shapes=[pltpu.VMEM((COLS, RANK), F32), pltpu.VMEM((RANK, RANK), F32)],
        compiler_params=LIMIT,
        name="project",
    )(pos, s_high, s_low, other, total, gram)


def splat_row(value, row):
    return jnp.broadcast_to(value[row : row + 1, :], value.shape)


def splat_col(value, col):
    return jnp.broadcast_to(value[:, col : col + 1], value.shape)


def owner(y, z, j, a, b):
    from_z = lax.rem(z + 8 - 2 * a, 8) + (b - 2 * b * lax.rem(z, 2))
    return lax.rem(y + 4 - j, 4) * 8 + from_z


def inverse_factor(groups):
    lane = lax.broadcasted_iota(jnp.int32, (GROUP, HALF), 1)
    sub = lax.broadcasted_iota(jnp.int32, (GROUP, HALF), 0)
    groups = list(groups)
    count = len(groups)
    result = []
    for g in range(count):
        base = g * GROUP
        inside = (lane >= base) & (lane < base + GROUP)
        pivot = groups[g]
        cols = [splat_col(pivot, base + a) for a in range(GROUP)]
        s = [[splat_row(cols[a], b) if b >= a else None for a in range(GROUP)] for b in range(GROUP)]
        low = [[None] * GROUP for _ in range(GROUP)]
        inverse = []
        for a in range(GROUP):
            inverse.append(1.0 / s[a][a])
            for b in range(a + 1, GROUP):
                low[b][a] = s[b][a] * inverse[a]
            for b in range(a + 1, GROUP):
                for c in range(a + 1, b + 1):
                    s[b][c] = s[b][c] - low[b][a] * s[c][a]
        outside = jnp.where(inside, 0.0, pivot)
        rows = []
        for a in range(GROUP):
            row = splat_row(outside, a)
            for e in range(a):
                row = row - low[a][e] * rows[e]
            rows.append(jnp.where(lane == base + a, 1.0, row))
        for i in range(g + 1, count):
            here = groups[i]
            kept = jnp.where(inside, 0.0, here)
            factors = []
            for a in range(GROUP):
                c = splat_col(here, base + a)
                for e in range(a):
                    c = c - factors[e] * s[a][e]
                factors.append(c * inverse[a])
            for a in range(GROUP):
                kept = kept - factors[a] * rows[a]
            groups[i] = kept
        final = jnp.zeros_like(pivot)
        for a in range(GROUP):
            final = jnp.where(sub == a, rows[a] * lax.rsqrt(s[a][a]), final)
        result.append(jnp.where(lane <= sub + base, final, 0.0))
    return result


def factor_kernel(pos_ref, p0, p1, p2, p3, p0_high, p0_low, p1_high, p1_low, inverse_ref, high_ref, low_ref, gram):
    y, z = pos_ref[0], pos_ref[1]
    for j, piece in enumerate((p0, p1, p2, p3)):
        for a in range(4):
            for b in range(2):
                to_gram = pl.ds(pl.multiple_of(owner(y, z, j, a, b) * GROUP, GROUP), GROUP)
                gram[to_gram, :] = piece[pl.ds((2 * a + b) * GROUP, GROUP), :]

    def rows_of(value):
        return [value[GROUP * g : GROUP * (g + 1), :] for g in range(HALF // GROUP)]

    w11 = jnp.concatenate(inverse_factor(rows_of(gram[:HALF, :HALF])), axis=0)
    l21 = mm(gram[HALF:, :HALF], w11, 1, 1, HIGHEST)
    rest = gram[HALF:, HALF:] - mm(l21, l21, 1, 1, HIGHEST)
    w22 = jnp.concatenate(inverse_factor(rows_of(rest)), axis=0)
    w21 = -mm(w22, mm(l21, w11, 1, 0, HIGHEST), 1, 0, HIGHEST)
    inverse_ref[:HALF, :HALF] = w11
    inverse_ref[:HALF, HALF:] = jnp.zeros_like(w11)
    inverse_ref[HALF:, :HALF] = w21
    inverse_ref[HALF:, HALF:] = w22
    inverse = split(inverse_ref[...])
    for t, (p_high, p_low) in enumerate(((p0_high, p0_low), (p1_high, p1_low))):
        rows = pl.ds(t * 4 * PIECE, 4 * PIECE)
        high_ref[rows], low_ref[rows] = split(mm3((p_high[...], p_low[...]), inverse, 1, 1))


def factor(pos, pieces, powered):
    return pl.pallas_call(
        factor_kernel,
        out_shape=(
            jax.ShapeDtypeStruct((RANK, RANK), F32),
            jax.ShapeDtypeStruct((ROWS, RANK), BF16),
            jax.ShapeDtypeStruct((ROWS, RANK), BF16),
        ),
        in_specs=[scalars()] + [whole()] * 8,
        out_specs=(whole(),) * 3,
        scratch_shapes=[pltpu.VMEM((RANK, RANK), F32)],
        compiler_params=LIMIT,
        cost_estimate=pl.CostEstimate(flops=10 << 30, bytes_accessed=32 << 20, transcendentals=0),
        name="factor",
    )(pos, *pieces, *powered)


def coefficients_kernel(pos_ref, p0, p1, p2, p3, inverse_ref, coeff_ref, square_ref):
    y, z = pos_ref[0], pos_ref[1]
    inverse = split(inverse_ref[...])
    for j, piece in enumerate((p0, p1, p2, p3)):
        value = mm3(split(piece[...]), inverse, 1, 1)
        for a in range(4):
            for b in range(2):
                place = pl.ds(pl.multiple_of(owner(y, z, j, a, b) * COEFF, COEFF), COEFF)
                coeff_ref[place, :] = value[(2 * a + b) * COEFF : (2 * a + b + 1) * COEFF]
    value = coeff_ref[...]
    square_ref[...] = jnp.sum(value * value, axis=0, keepdims=True)


def coefficients_of(pos, pieces, inverse):
    return pl.pallas_call(
        coefficients_kernel,
        out_shape=(jax.ShapeDtypeStruct((COLS, RANK), F32), jax.ShapeDtypeStruct((1, RANK), F32)),
        in_specs=[scalars()] + [whole()] * 5,
        out_specs=(whole(),) * 2,
        compiler_params=LIMIT,
        name="coefficients",
    )(pos, *pieces, inverse)


def write_rows(pos_ref, half, value_ref, out_ref, sems, places=(0, 1, 2, 3)):
    x, core = pos_ref[2], pos_ref[3]
    copies = []
    for s in places:
        there = pl.ds(row_start(core if half == 0 else 1 - core, x, s), PIECE)
        here = pl.ds((4 * half + s) * PIECE, PIECE)
        copies.append(pltpu.make_async_copy(value_ref.at[here], out_ref.at[there], sems.at[4 * half + s]))
        copies[-1].start()
    return copies


def feedback_kernel(pos_ref, s0_high, s0_low, s1_high, s1_low, q_ref, c_ref, out_ref, buf, sems):
    coefficients = c_ref[...].astype(BF16)
    copies = []
    for t, (s_high, s_low) in enumerate(((s0_high, s0_low), (s1_high, s1_low))):
        rows = pl.ds(t * 4 * PIECE, 4 * PIECE)
        summed = s_high[...].astype(F32) + s_low[...].astype(F32)
        buf[rows] = summed - 0.05 * mm(q_ref[rows], coefficients, 1, 1)
        copies += write_rows(pos_ref, t, buf, out_ref, sems)
    for copy in copies:
        copy.wait()


def feedback(pos, summed, high, coefficients):
    return pl.pallas_call(
        feedback_kernel,
        out_shape=jax.ShapeDtypeStruct((ROWS, COLS), F32),
        in_specs=[scalars()] + [whole()] * 6,
        out_specs=in_hbm(),
        scratch_shapes=[pltpu.VMEM((ROWS, COLS), F32), pltpu.SemaphoreType.DMA((8,))],
        compiler_params=LIMIT,
        cost_estimate=pl.CostEstimate(flops=4 * 896 * 1024 * 256, bytes_accessed=10 << 20, transcendentals=0),
        name="feedback",
    )(pos, *summed, high, coefficients)


def update_kernel(scale, pos_ref, high_ref, low_ref, c_ref, s_ref, basis_ref, out_ref, b_buf, buf, b_sem, sems):
    basis = c_ref[...] * (1.0 / jnp.sqrt(s_ref[...] + 1e-6))
    b_buf[...] = basis
    store = pltpu.make_async_copy(b_buf, basis_ref, b_sem)
    store.start()
    basis = split(basis)
    copies = []
    for t in range(4):
        rows = pl.ds(t * 2 * PIECE, 2 * PIECE)
        buf[rows] = (scale * mm3((high_ref[rows], low_ref[rows]), basis, 1, 1)).astype(BF16)
        copies += write_rows(pos_ref, t // 2, buf, out_ref, sems, (2 * (t % 2), 2 * (t % 2) + 1))
    store.wait()
    for copy in copies:
        copy.wait()


def update(pos, high, low, coefficients, squares, scale):
    return pl.pallas_call(
        functools.partial(update_kernel, scale),
        out_shape=(
            jax.ShapeDtypeStruct((COLS, RANK), F32),
            jax.ShapeDtypeStruct((ROWS, COLS), BF16),
        ),
        in_specs=[scalars()] + [whole()] * 4,
        out_specs=(in_hbm(), in_hbm()),
        scratch_shapes=[
            pltpu.VMEM((COLS, RANK), F32),
            pltpu.VMEM((ROWS, COLS), BF16),
            pltpu.SemaphoreType.DMA,
            pltpu.SemaphoreType.DMA((8,)),
        ],
        compiler_params=LIMIT,
        name="update",
    )(pos, high, low, coefficients, squares)


def shards(momentum, gradient, old_basis):
    row = lax.axis_index("row")
    col = lax.axis_index("col")
    arguments = (momentum, gradient, old_basis)
    momentum, gradient, old_basis = (pltpu.with_memory_space_constraint(v, pltpu.HBM) for v in arguments)
    pos = jnp.stack([row // 8, row % 8, col // 2, col % 2]).astype(jnp.int32)

    away, s1_high, s1_low, m_own, g_own, b_high, b_low = power_away(pos, momentum, gradient, old_basis)
    came = send_core(away)
    here, s0_high, s0_low = power_own(m_own, g_own, b_high, b_low)
    summed = (s0_high, s0_low, s1_high, s1_low)
    parts = [here[s * PIECE : (s + 1) * PIECE] + came[s * PIECE : (s + 1) * PIECE] for s in range(4)]
    mine = ring_sum(parts[0], [None] + [send_x(parts[s], s) for s in (1, 2, 3)])
    own = jnp.concatenate([mine] + [send_x(mine, s) for s in (3, 2, 1)])
    other = send_core(own)
    p0_high, p0_low, total, gram = project_own(s0_high, s0_low, own)
    p1_high, p1_low, *slabs = project(pos, s1_high, s1_low, other, total, gram)
    powered = (p0_high, p0_low, p1_high, p1_low)

    part0, part1 = (
        ring_sum(slabs[h], [None] + [send_y(slabs[2 * s + h], s) for s in (1, 2, 3)]) for h in range(2)
    )
    two = 2 * CHUNK
    came2, came1, came3 = send_z(part0[:two], 4), send_z(part0[two : 2 * two], 2), send_z(part0[2 * two :], 6)
    mine = ring_sum(part1, [None, came1, came2, came3])
    mine = mine[:CHUNK] + send_pair(mine[CHUNK:])

    other = send_pair(mine)
    mine = jnp.concatenate([mine[:COEFF], other[:COEFF], mine[COEFF:], other[COEFF:]])
    pieces = [mine] + [send_z(mine, 2 * a) for a in (1, 2, 3)]
    gram = jnp.concatenate([piece[2 * COEFF :] for piece in pieces])
    raw = jnp.concatenate([piece[: 2 * COEFF] for piece in pieces])
    grams = [gram] + [send_y(gram, s) for s in (1, 2, 3)]
    raws = [raw] + [send_y(raw, s) for s in (1, 2, 3)]
    inverse, high, low = factor(pos, grams, powered)

    coefficients, squares = coefficients_of(pos, raws, inverse)
    squares = squares + send_core(squares)
    came = [send_x(squares, s) for s in (1, 2, 3)]
    new_momentum = feedback(pos, summed, high, coefficients)
    new_momentum, *came = lax.optimization_barrier((new_momentum, *came))
    squares = ring_sum(squares, [None] + came)
    rms_scale = (28672 * 8192 / 256) ** 0.5
    new_basis, new_update = update(pos, high, low, coefficients, squares, rms_scale)
    return (new_momentum, new_basis, new_update)


def solution(mesh):
    placed = (P("row", "col"), P("row", "col"), P("col", None))
    return jax.shard_map(
        shards,
        mesh=mesh,
        in_specs=placed,
        out_specs=(P("row", "col"), P("col", None), P("row", "col")),
        check_vma=False,
    )
```

```python
import functools

import jax
import jax.numpy as jnp
from jax import lax
from jax.experimental import pallas as pl
from jax.experimental.pallas import tpu as pltpu
from jax.sharding import PartitionSpec as P

HIGHEST = lax.Precision.HIGHEST
F32 = jnp.float32
BF16 = jnp.bfloat16
HALF = 128
GROUP = 8
ROWS = 896
COLS = 1024
RANK = 256
PIECE = 112
SLAB = 256
COEFF = 32
PAIR = 80
LIMIT = pltpu.CompilerParams(vmem_limit_bytes=32 * 1024 * 1024)


def send(value, axis, move, size):
    return lax.ppermute(value, axis, [(i, move(i)) for i in range(size)])


def send_core(value):
    return send(value, "col", lambda i: i ^ 1, 8)


def send_x(value, s):
    return send(value, "col", lambda i: ((i // 2 + s) % 4) * 2 + i % 2, 8)


def send_y(value, s):
    return send(value, "row", lambda i: ((i // 8 + s) % 4) * 8 + i % 8, 32)


def send_z(value, s):
    return send(value, "row", lambda i: (i // 8) * 8 + (i % 8 + s) % 8, 32)


Z_SHIFTS = (0, 1, 2, 7)


def ring_sum(own, came):
    return (own + came[2]) + (came[1] + came[3])


def mm(a, b, ca, cb, precision=None):
    return lax.dot_general(
        a, b, (((ca,), (cb,)), ((), ())), precision=precision, preferred_element_type=F32
    )


def split(value):
    high = value.astype(BF16)
    return high, (value - high.astype(F32)).astype(BF16)


def mm3(a, b, ca, cb):
    return mm(a[0], b[0], ca, cb) + (mm(a[0], b[1], ca, cb) + mm(a[1], b[0], ca, cb))


def whole():
    return pl.BlockSpec(memory_space=pltpu.VMEM)


def in_hbm():
    return pl.BlockSpec(memory_space=pltpu.HBM)


def scalars():
    return pl.BlockSpec(memory_space=pltpu.SMEM)


def row_start(half, x, s):
    return pl.multiple_of(half * (4 * PIECE) + lax.rem(x + s, 4) * PIECE, PIECE)


def power_away_kernel(
    pos_ref, m_ref, g_ref, b_ref, out_ref, high_ref, low_ref, m_own, g_own, b_high, b_low, m_buf, g_buf, b_buf, sems, b_sem
):
    x, core = pos_ref[2], pos_ref[3]
    load = pltpu.make_async_copy(b_ref, b_buf, b_sem)
    away, own = [], []
    for s in range(4):
        there = pl.ds(s * PIECE, PIECE)
        here = pl.ds(row_start(1 - core, x, s), PIECE)
        away.append(pltpu.make_async_copy(m_ref.at[here], m_buf.at[there], sems.at[s, 0]))
        away.append(pltpu.make_async_copy(g_ref.at[here], g_buf.at[there], sems.at[s, 1]))
        here = pl.ds(row_start(core, x, s), PIECE)
        own.append(pltpu.make_async_copy(m_ref.at[here], m_own.at[there], sems.at[4 + s, 0]))
        own.append(pltpu.make_async_copy(g_ref.at[here], g_own.at[there], sems.at[4 + s, 1]))
    load.start()
    for copy in away[:4]:
        copy.start()
    load.wait()
    for copy in away[4:]:
        copy.start()
    basis = split(b_buf[...])
    b_high[...], b_low[...] = basis
    for t in range(2):
        for copy in away[4 * t : 4 * t + 4]:
            copy.wait()
        if t == 0:
            for copy in own:
                copy.start()
        rows = pl.ds(t * 2 * PIECE, 2 * PIECE)
        high, low = split(m_buf[rows] + g_buf[rows].astype(F32))
        high_ref[rows] = high
        low_ref[rows] = low
        out_ref[rows] = mm3((high, low), basis, 1, 0)
    for copy in own:
        copy.wait()


def power_away(pos, momentum, gradient, basis):
    half = (4 * PIECE, COLS)
    return pl.pallas_call(
        power_away_kernel,
        out_shape=(
            jax.ShapeDtypeStruct((4 * PIECE, RANK), F32),
            jax.ShapeDtypeStruct(half, BF16),
            jax.ShapeDtypeStruct(half, BF16),
            jax.ShapeDtypeStruct(half, F32),
            jax.ShapeDtypeStruct(half, BF16),
            jax.ShapeDtypeStruct((COLS, RANK), BF16),
            jax.ShapeDtypeStruct((COLS, RANK), BF16),
        ),
        in_specs=[scalars(), in_hbm(), in_hbm(), in_hbm()],
        out_specs=(whole(),) * 7,
        scratch_shapes=[
            pltpu.VMEM(half, F32),
            pltpu.VMEM(half, BF16),
            pltpu.VMEM((COLS, RANK), F32),
            pltpu.SemaphoreType.DMA((8, 2)),
            pltpu.SemaphoreType.DMA,
        ],
        compiler_params=LIMIT,
        name="power_away",
    )(pos, momentum, gradient, basis)


def power_own_kernel(m_ref, g_ref, b_high, b_low, out_ref, high_ref, low_ref):
    for t in range(2):
        rows = pl.ds(t * 2 * PIECE, 2 * PIECE)
        high, low = split(m_ref[rows] + g_ref[rows].astype(F32))
        high_ref[rows] = high
        low_ref[rows] = low
        out_ref[rows] = mm3((high, low), (b_high[...], b_low[...]), 1, 0)


def power_own(momentum, gradient, b_high, b_low):
    return pl.pallas_call(
        power_own_kernel,
        out_shape=(
            jax.ShapeDtypeStruct((4 * PIECE, RANK), F32),
            jax.ShapeDtypeStruct((4 * PIECE, COLS), BF16),
            jax.ShapeDtypeStruct((4 * PIECE, COLS), BF16),
        ),
        in_specs=[whole()] * 4,
        out_specs=(whole(),) * 3,
        compiler_params=LIMIT,
        cost_estimate=pl.CostEstimate(flops=6 * 448 * 1024 * 256, bytes_accessed=4 << 20, transcendentals=0),
        name="power_own",
    )(momentum, gradient, b_high, b_low)


def project_own_kernel(s_high, s_low, own_ref, high_ref, low_ref, total_ref, gram_ref):
    value = split(own_ref[...])
    high_ref[...], low_ref[...] = value
    gram_ref[...] = mm3(value, value, 0, 0)
    for t in range(4):
        columns = pl.ds(t * SLAB, SLAB)
        total_ref[columns, :] = mm3((s_high[:, columns], s_low[:, columns]), value, 0, 0)


def project_own(s_high, s_low, own):
    return pl.pallas_call(
        project_own_kernel,
        out_shape=(
            jax.ShapeDtypeStruct((4 * PIECE, RANK), BF16),
            jax.ShapeDtypeStruct((4 * PIECE, RANK), BF16),
            jax.ShapeDtypeStruct((COLS, RANK), F32),
            jax.ShapeDtypeStruct((RANK, RANK), F32),
        ),
        in_specs=[whole()] * 3,
        out_specs=(whole(),) * 4,
        compiler_params=LIMIT,
        cost_estimate=pl.CostEstimate(flops=6 * 448 * 1280 * 256, bytes_accessed=4 << 20, transcendentals=0),
        name="project_own",
    )(s_high, s_low, own)


def project_kernel(pos_ref, s_high, s_low, other_ref, total_ref, gram_ref, high_ref, low_ref, *refs):
    y, z = pos_ref[0], pos_ref[1]
    outs, (total, gram) = refs[:8], refs[8:]
    value = split(other_ref[...])
    high_ref[...], low_ref[...] = value
    gram[...] = gram_ref[...] + mm3(value, value, 0, 0)
    for t in range(4):
        columns = pl.ds(t * SLAB, SLAB)
        total[columns, :] = total_ref[columns, :] + mm3((s_high[:, columns], s_low[:, columns]), value, 0, 0)
    for shift in range(4):
        target = lax.rem(y + shift, 4) * 8
        for part, position, a in ((0, 0, 1), (0, 1, 2), (0, 2, 3), (1, 0, 0)):
            out_ref = outs[2 * shift + part]
            for b in range(2):
                source = target + lax.rem(z + Z_SHIFTS[a], 4) + 4 * b
                place = position * PAIR
                from_total = pl.ds(pl.multiple_of(source * COEFF, COEFF), COEFF)
                from_gram = pl.ds(pl.multiple_of(source * GROUP, GROUP), GROUP)
                out_ref[pl.ds(place + b * COEFF, COEFF), :] = total[from_total, :]
                out_ref[pl.ds(place + 2 * COEFF + b * GROUP, GROUP), :] = gram[from_gram, :]


def project(pos, s_high, s_low, other, total, gram):
    return pl.pallas_call(
        project_kernel,
        out_shape=(
            jax.ShapeDtypeStruct((4 * PIECE, RANK), BF16),
            jax.ShapeDtypeStruct((4 * PIECE, RANK), BF16),
        )
        + (
            jax.ShapeDtypeStruct((3 * PAIR, RANK), F32),
            jax.ShapeDtypeStruct((PAIR, RANK), F32),
        )
        * 4,
        in_specs=[scalars()] + [whole()] * 5,
        out_specs=(whole(),) * 10,
        scratch_shapes=[pltpu.VMEM((COLS, RANK), F32), pltpu.VMEM((RANK, RANK), F32)],
        compiler_params=LIMIT,
        name="project",
    )(pos, s_high, s_low, other, total, gram)


def splat_row(value, row):
    return jnp.broadcast_to(value[row : row + 1, :], value.shape)


def splat_col(value, col):
    return jnp.broadcast_to(value[:, col : col + 1], value.shape)


def owner(y, z, j, a, b):
    from_z = lax.rem(z + 8 - Z_SHIFTS[a], 4) + 4 * b
    return lax.rem(y + 4 - j, 4) * 8 + from_z


def inverse_factor(groups):
    lane = lax.broadcasted_iota(jnp.int32, (GROUP, HALF), 1)
    sub = lax.broadcasted_iota(jnp.int32, (GROUP, HALF), 0)
    groups = list(groups)
    count = len(groups)
    result = []
    for g in range(count):
        base = g * GROUP
        inside = (lane >= base) & (lane < base + GROUP)
        pivot = groups[g]
        cols = [splat_col(pivot, base + a) for a in range(GROUP)]
        s = [[splat_row(cols[a], b) if b >= a else None for a in range(GROUP)] for b in range(GROUP)]
        low = [[None] * GROUP for _ in range(GROUP)]
        inverse = []
        for a in range(GROUP):
            inverse.append(1.0 / s[a][a])
            for b in range(a + 1, GROUP):
                low[b][a] = s[b][a] * inverse[a]
            for b in range(a + 1, GROUP):
                for c in range(a + 1, b + 1):
                    s[b][c] = s[b][c] - low[b][a] * s[c][a]
        outside = jnp.where(inside, 0.0, pivot)
        rows = []
        for a in range(GROUP):
            row = splat_row(outside, a)
            for e in range(a):
                row = row - low[a][e] * rows[e]
            rows.append(jnp.where(lane == base + a, 1.0, row))
        for i in range(g + 1, count):
            here = groups[i]
            kept = jnp.where(inside, 0.0, here)
            factors = []
            for a in range(GROUP):
                c = splat_col(here, base + a)
                for e in range(a):
                    c = c - factors[e] * s[a][e]
                factors.append(c * inverse[a])
            for a in range(GROUP):
                kept = kept - factors[a] * rows[a]
            groups[i] = kept
        final = jnp.zeros_like(pivot)
        for a in range(GROUP):
            final = jnp.where(sub == a, rows[a] * lax.rsqrt(s[a][a]), final)
        result.append(jnp.where(lane <= sub + base, final, 0.0))
    return result


def factor_kernel(pos_ref, p0, p1, p2, p3, p0_high, p0_low, p1_high, p1_low, inverse_ref, high_ref, low_ref, gram):
    y, z = pos_ref[0], pos_ref[1]
    for j, piece in enumerate((p0, p1, p2, p3)):
        for a in range(4):
            for b in range(2):
                to_gram = pl.ds(pl.multiple_of(owner(y, z, j, a, b) * GROUP, GROUP), GROUP)
                gram[to_gram, :] = piece[pl.ds((2 * a + b) * GROUP, GROUP), :]

    def rows_of(value):
        return [value[GROUP * g : GROUP * (g + 1), :] for g in range(HALF // GROUP)]

    w11 = jnp.concatenate(inverse_factor(rows_of(gram[:HALF, :HALF])), axis=0)
    l21 = mm(gram[HALF:, :HALF], w11, 1, 1, HIGHEST)
    rest = gram[HALF:, HALF:] - mm(l21, l21, 1, 1, HIGHEST)
    w22 = jnp.concatenate(inverse_factor(rows_of(rest)), axis=0)
    w21 = -mm(w22, mm(l21, w11, 1, 0, HIGHEST), 1, 0, HIGHEST)
    inverse_ref[:HALF, :HALF] = w11
    inverse_ref[:HALF, HALF:] = jnp.zeros_like(w11)
    inverse_ref[HALF:, :HALF] = w21
    inverse_ref[HALF:, HALF:] = w22
    inverse = split(inverse_ref[...])
    for t, (p_high, p_low) in enumerate(((p0_high, p0_low), (p1_high, p1_low))):
        rows = pl.ds(t * 4 * PIECE, 4 * PIECE)
        high_ref[rows], low_ref[rows] = split(mm3((p_high[...], p_low[...]), inverse, 1, 1))


def factor(pos, pieces, powered):
    return pl.pallas_call(
        factor_kernel,
        out_shape=(
            jax.ShapeDtypeStruct((RANK, RANK), F32),
            jax.ShapeDtypeStruct((ROWS, RANK), BF16),
            jax.ShapeDtypeStruct((ROWS, RANK), BF16),
        ),
        in_specs=[scalars()] + [whole()] * 8,
        out_specs=(whole(),) * 3,
        scratch_shapes=[pltpu.VMEM((RANK, RANK), F32)],
        compiler_params=LIMIT,
        cost_estimate=pl.CostEstimate(flops=10 << 30, bytes_accessed=32 << 20, transcendentals=0),
        name="factor",
    )(pos, *pieces, *powered)


def coefficients_kernel(pos_ref, p0, p1, p2, p3, inverse_ref, coeff_ref, square_ref):
    y, z = pos_ref[0], pos_ref[1]
    inverse = split(inverse_ref[...])
    for j, piece in enumerate((p0, p1, p2, p3)):
        value = mm3(split(piece[...]), inverse, 1, 1)
        for a in range(4):
            for b in range(2):
                place = pl.ds(pl.multiple_of(owner(y, z, j, a, b) * COEFF, COEFF), COEFF)
                coeff_ref[place, :] = value[(2 * a + b) * COEFF : (2 * a + b + 1) * COEFF]
    value = coeff_ref[...]
    square_ref[...] = jnp.sum(value * value, axis=0, keepdims=True)


def coefficients_of(pos, pieces, inverse):
    return pl.pallas_call(
        coefficients_kernel,
        out_shape=(jax.ShapeDtypeStruct((COLS, RANK), F32), jax.ShapeDtypeStruct((1, RANK), F32)),
        in_specs=[scalars()] + [whole()] * 5,
        out_specs=(whole(),) * 2,
        compiler_params=LIMIT,
        name="coefficients",
    )(pos, *pieces, inverse)


def write_rows(pos_ref, half, value_ref, out_ref, sems, places=(0, 1, 2, 3)):
    x, core = pos_ref[2], pos_ref[3]
    copies = []
    for s in places:
        there = pl.ds(row_start(core if half == 0 else 1 - core, x, s), PIECE)
        here = pl.ds((4 * half + s) * PIECE, PIECE)
        copies.append(pltpu.make_async_copy(value_ref.at[here], out_ref.at[there], sems.at[4 * half + s]))
        copies[-1].start()
    return copies


def feedback_kernel(pos_ref, s0_high, s0_low, s1_high, s1_low, q_ref, c_ref, out_ref, buf, sems):
    coefficients = c_ref[...].astype(BF16)
    copies = []
    for t, (s_high, s_low) in enumerate(((s0_high, s0_low), (s1_high, s1_low))):
        rows = pl.ds(t * 4 * PIECE, 4 * PIECE)
        summed = s_high[...].astype(F32) + s_low[...].astype(F32)
        buf[rows] = summed - 0.05 * mm(q_ref[rows], coefficients, 1, 1)
        copies += write_rows(pos_ref, t, buf, out_ref, sems)
    for copy in copies:
        copy.wait()


def feedback(pos, summed, high, coefficients):
    return pl.pallas_call(
        feedback_kernel,
        out_shape=jax.ShapeDtypeStruct((ROWS, COLS), F32),
        in_specs=[scalars()] + [whole()] * 6,
        out_specs=in_hbm(),
        scratch_shapes=[pltpu.VMEM((ROWS, COLS), F32), pltpu.SemaphoreType.DMA((8,))],
        compiler_params=LIMIT,
        cost_estimate=pl.CostEstimate(flops=4 * 896 * 1024 * 256, bytes_accessed=10 << 20, transcendentals=0),
        name="feedback",
    )(pos, *summed, high, coefficients)


def update_kernel(scale, pos_ref, high_ref, low_ref, c_ref, s_ref, basis_ref, out_ref, b_buf, buf, b_sem, sems):
    basis = c_ref[...] * (1.0 / jnp.sqrt(s_ref[...] + 1e-6))
    b_buf[...] = basis
    store = pltpu.make_async_copy(b_buf, basis_ref, b_sem)
    store.start()
    basis = split(basis)
    copies = []
    for t in range(4):
        rows = pl.ds(t * 2 * PIECE, 2 * PIECE)
        buf[rows] = (scale * mm3((high_ref[rows], low_ref[rows]), basis, 1, 1)).astype(BF16)
        copies += write_rows(pos_ref, t // 2, buf, out_ref, sems, (2 * (t % 2), 2 * (t % 2) + 1))
    store.wait()
    for copy in copies:
        copy.wait()


def update(pos, high, low, coefficients, squares, scale):
    return pl.pallas_call(
        functools.partial(update_kernel, scale),
        out_shape=(
            jax.ShapeDtypeStruct((COLS, RANK), F32),
            jax.ShapeDtypeStruct((ROWS, COLS), BF16),
        ),
        in_specs=[scalars()] + [whole()] * 4,
        out_specs=(in_hbm(), in_hbm()),
        scratch_shapes=[
            pltpu.VMEM((COLS, RANK), F32),
            pltpu.VMEM((ROWS, COLS), BF16),
            pltpu.SemaphoreType.DMA,
            pltpu.SemaphoreType.DMA((8,)),
        ],
        compiler_params=LIMIT,
        name="update",
    )(pos, high, low, coefficients, squares)


def shards(momentum, gradient, old_basis):
    row = lax.axis_index("row")
    col = lax.axis_index("col")
    arguments = (momentum, gradient, old_basis)
    momentum, gradient, old_basis = (pltpu.with_memory_space_constraint(v, pltpu.HBM) for v in arguments)
    pos = jnp.stack([row // 8, row % 8, col // 2, col % 2]).astype(jnp.int32)

    away, s1_high, s1_low, m_own, g_own, b_high, b_low = power_away(pos, momentum, gradient, old_basis)
    came = send_core(away)
    here, s0_high, s0_low = power_own(m_own, g_own, b_high, b_low)
    summed = (s0_high, s0_low, s1_high, s1_low)
    parts = [here[s * PIECE : (s + 1) * PIECE] + came[s * PIECE : (s + 1) * PIECE] for s in range(4)]
    mine = ring_sum(parts[0], [None] + [send_x(parts[s], s) for s in (1, 2, 3)])
    own = jnp.concatenate([mine] + [send_x(mine, s) for s in (3, 2, 1)])
    other = send_core(own)
    p0_high, p0_low, total, gram = project_own(s0_high, s0_low, own)
    p1_high, p1_low, *slabs = project(pos, s1_high, s1_low, other, total, gram)
    powered = (p0_high, p0_low, p1_high, p1_low)

    part0, part1 = (
        ring_sum(slabs[h], [None] + [send_y(slabs[2 * s + h], s) for s in (1, 2, 3)]) for h in range(2)
    )
    came = [send_z(part0[PAIR * (a - 1) : PAIR * a], Z_SHIFTS[a]) for a in (1, 2, 3)]
    mine = ring_sum(part1, [None] + came)
    mine = mine + send_z(mine, 4)

    pieces = [mine] + [send_z(mine, s) for s in Z_SHIFTS[1:]]
    gram = jnp.concatenate([piece[2 * COEFF :] for piece in pieces])
    raw = jnp.concatenate([piece[: 2 * COEFF] for piece in pieces])
    grams = [gram] + [send_y(gram, s) for s in (1, 2, 3)]
    raws = [raw] + [send_y(raw, s) for s in (1, 2, 3)]
    inverse, high, low = factor(pos, grams, powered)

    coefficients, squares = coefficients_of(pos, raws, inverse)
    squares = squares + send_core(squares)
    came = [send_x(squares, s) for s in (1, 2, 3)]
    new_momentum = feedback(pos, summed, high, coefficients)
    new_momentum, *came = lax.optimization_barrier((new_momentum, *came))
    squares = ring_sum(squares, [None] + came)
    rms_scale = (28672 * 8192 / 256) ** 0.5
    new_basis, new_update = update(pos, high, low, coefficients, squares, rms_scale)
    return (new_momentum, new_basis, new_update)


def solution(mesh):
    placed = (P("row", "col"), P("row", "col"), P("col", None))
    return jax.shard_map(
        shards,
        mesh=mesh,
        in_specs=placed,
        out_specs=(P("row", "col"), P("col", None), P("row", "col")),
        check_vma=False,
    )
```

```python
import functools

import jax
import jax.numpy as jnp
from jax import lax
from jax.experimental import pallas as pl
from jax.experimental.pallas import tpu as pltpu
from jax.sharding import PartitionSpec as P

HIGHEST = lax.Precision.HIGHEST
F32 = jnp.float32
BF16 = jnp.bfloat16
HALF = 128
GROUP = 8
ROWS = 896
COLS = 1024
RANK = 256
PIECE = 112
SLAB = 256
COEFF = 32
PAIR = 80
LIMIT = pltpu.CompilerParams(vmem_limit_bytes=32 * 1024 * 1024)


def send(value, axis, move, size):
    return lax.ppermute(value, axis, [(i, move(i)) for i in range(size)])


def send_core(value):
    return send(value, "col", lambda i: i ^ 1, 8)


def send_x(value, s):
    return send(value, "col", lambda i: ((i // 2 + s) % 4) * 2 + i % 2, 8)


def send_y(value, s):
    return send(value, "row", lambda i: ((i // 8 + s) % 4) * 8 + i % 8, 32)


def send_z(value, s):
    return send(value, "row", lambda i: (i // 8) * 8 + (i % 8 + s) % 8, 32)


Z_SHIFTS = (0, 1, 2, 7)


def ring_sum(own, came):
    return (own + came[2]) + (came[1] + came[3])


def mm(a, b, ca, cb, precision=None):
    return lax.dot_general(
        a, b, (((ca,), (cb,)), ((), ())), precision=precision, preferred_element_type=F32
    )


def split(value):
    high = value.astype(BF16)
    return high, (value - high.astype(F32)).astype(BF16)


def mm3(a, b, ca, cb):
    return mm(a[0], b[0], ca, cb) + (mm(a[0], b[1], ca, cb) + mm(a[1], b[0], ca, cb))


def whole():
    return pl.BlockSpec(memory_space=pltpu.VMEM)


def in_hbm():
    return pl.BlockSpec(memory_space=pltpu.HBM)


def scalars():
    return pl.BlockSpec(memory_space=pltpu.SMEM)


def row_start(half, x, s):
    return pl.multiple_of(half * (4 * PIECE) + lax.rem(x + s, 4) * PIECE, PIECE)


def power_away_kernel(
    pos_ref, m_ref, g_ref, b_ref, out_ref, high_ref, low_ref, m_own, g_own, b_high, b_low, m_buf, g_buf, b_buf, sems, b_sem
):
    x, core = pos_ref[2], pos_ref[3]
    load = pltpu.make_async_copy(b_ref, b_buf, b_sem)
    away, own = [], []
    for s in range(4):
        there = pl.ds(s * PIECE, PIECE)
        here = pl.ds(row_start(1 - core, x, s), PIECE)
        away.append(pltpu.make_async_copy(m_ref.at[here], m_buf.at[there], sems.at[s, 0]))
        away.append(pltpu.make_async_copy(g_ref.at[here], g_buf.at[there], sems.at[s, 1]))
        here = pl.ds(row_start(core, x, s), PIECE)
        own.append(pltpu.make_async_copy(m_ref.at[here], m_own.at[there], sems.at[4 + s, 0]))
        own.append(pltpu.make_async_copy(g_ref.at[here], g_own.at[there], sems.at[4 + s, 1]))
    load.start()
    for copy in away[:4]:
        copy.start()
    load.wait()
    for copy in away[4:]:
        copy.start()
    basis = split(b_buf[...])
    b_high[...], b_low[...] = basis
    for t in range(2):
        for copy in away[4 * t : 4 * t + 4]:
            copy.wait()
        if t == 0:
            for copy in own:
                copy.start()
        rows = pl.ds(t * 2 * PIECE, 2 * PIECE)
        high, low = split(m_buf[rows] + g_buf[rows].astype(F32))
        high_ref[rows] = high
        low_ref[rows] = low
        out_ref[rows] = mm3((high, low), basis, 1, 0)
    for copy in own:
        copy.wait()


def power_away(pos, momentum, gradient, basis):
    half = (4 * PIECE, COLS)
    return pl.pallas_call(
        power_away_kernel,
        out_shape=(
            jax.ShapeDtypeStruct((4 * PIECE, RANK), F32),
            jax.ShapeDtypeStruct(half, BF16),
            jax.ShapeDtypeStruct(half, BF16),
            jax.ShapeDtypeStruct(half, F32),
            jax.ShapeDtypeStruct(half, BF16),
            jax.ShapeDtypeStruct((COLS, RANK), BF16),
            jax.ShapeDtypeStruct((COLS, RANK), BF16),
        ),
        in_specs=[scalars(), in_hbm(), in_hbm(), in_hbm()],
        out_specs=(whole(),) * 7,
        scratch_shapes=[
            pltpu.VMEM(half, F32),
            pltpu.VMEM(half, BF16),
            pltpu.VMEM((COLS, RANK), F32),
            pltpu.SemaphoreType.DMA((8, 2)),
            pltpu.SemaphoreType.DMA,
        ],
        compiler_params=LIMIT,
        name="power_away",
    )(pos, momentum, gradient, basis)


def power_own_kernel(m_ref, g_ref, b_high, b_low, out_ref, high_ref, low_ref):
    for t in range(2):
        rows = pl.ds(t * 2 * PIECE, 2 * PIECE)
        high, low = split(m_ref[rows] + g_ref[rows].astype(F32))
        high_ref[rows] = high
        low_ref[rows] = low
        out_ref[rows] = mm3((high, low), (b_high[...], b_low[...]), 1, 0)


def power_own(momentum, gradient, b_high, b_low):
    return pl.pallas_call(
        power_own_kernel,
        out_shape=(
            jax.ShapeDtypeStruct((4 * PIECE, RANK), F32),
            jax.ShapeDtypeStruct((4 * PIECE, COLS), BF16),
            jax.ShapeDtypeStruct((4 * PIECE, COLS), BF16),
        ),
        in_specs=[whole()] * 4,
        out_specs=(whole(),) * 3,
        compiler_params=LIMIT,
        cost_estimate=pl.CostEstimate(flops=6 * 448 * 1024 * 256, bytes_accessed=4 << 20, transcendentals=0),
        name="power_own",
    )(momentum, gradient, b_high, b_low)


def project_own_kernel(s_high, s_low, own_ref, high_ref, low_ref, total_ref, gram_ref):
    value = split(own_ref[...])
    high_ref[...], low_ref[...] = value
    gram_ref[...] = mm3(value, value, 0, 0)
    for t in range(4):
        columns = pl.ds(t * SLAB, SLAB)
        total_ref[columns, :] = mm3((s_high[:, columns], s_low[:, columns]), value, 0, 0)


def project_own(s_high, s_low, own):
    return pl.pallas_call(
        project_own_kernel,
        out_shape=(
            jax.ShapeDtypeStruct((4 * PIECE, RANK), BF16),
            jax.ShapeDtypeStruct((4 * PIECE, RANK), BF16),
            jax.ShapeDtypeStruct((COLS, RANK), F32),
            jax.ShapeDtypeStruct((RANK, RANK), F32),
        ),
        in_specs=[whole()] * 3,
        out_specs=(whole(),) * 4,
        compiler_params=LIMIT,
        cost_estimate=pl.CostEstimate(flops=6 * 448 * 1280 * 256, bytes_accessed=4 << 20, transcendentals=0),
        name="project_own",
    )(s_high, s_low, own)


def project_kernel(pos_ref, s_high, s_low, other_ref, total_ref, gram_ref, high_ref, low_ref, *refs):
    y, z = pos_ref[0], pos_ref[1]
    outs, (total, gram) = refs[:8], refs[8:]
    value = split(other_ref[...])
    high_ref[...], low_ref[...] = value
    gram[...] = gram_ref[...] + mm3(value, value, 0, 0)
    for t in range(4):
        columns = pl.ds(t * SLAB, SLAB)
        total[columns, :] = total_ref[columns, :] + mm3((s_high[:, columns], s_low[:, columns]), value, 0, 0)
    for shift in range(4):
        target = lax.rem(y + shift, 4) * 8
        for part, position, a in ((0, 0, 1), (0, 1, 2), (1, 0, 3), (1, 1, 0)):
            out_ref = outs[2 * shift + part]
            for b in range(2):
                source = target + lax.rem(z + Z_SHIFTS[a], 4) + 4 * b
                place = position * PAIR
                from_total = pl.ds(pl.multiple_of(source * COEFF, COEFF), COEFF)
                from_gram = pl.ds(pl.multiple_of(source * GROUP, GROUP), GROUP)
                out_ref[pl.ds(place + b * COEFF, COEFF), :] = total[from_total, :]
                out_ref[pl.ds(place + 2 * COEFF + b * GROUP, GROUP), :] = gram[from_gram, :]


def project(pos, s_high, s_low, other, total, gram):
    return pl.pallas_call(
        project_kernel,
        out_shape=(
            jax.ShapeDtypeStruct((4 * PIECE, RANK), BF16),
            jax.ShapeDtypeStruct((4 * PIECE, RANK), BF16),
        )
        + (jax.ShapeDtypeStruct((2 * PAIR, RANK), F32),) * 8,
        in_specs=[scalars()] + [whole()] * 5,
        out_specs=(whole(),) * 10,
        scratch_shapes=[pltpu.VMEM((COLS, RANK), F32), pltpu.VMEM((RANK, RANK), F32)],
        compiler_params=LIMIT,
        name="project",
    )(pos, s_high, s_low, other, total, gram)


def splat_row(value, row):
    return jnp.broadcast_to(value[row : row + 1, :], value.shape)


def splat_col(value, col):
    return jnp.broadcast_to(value[:, col : col + 1], value.shape)


def owner(y, z, j, a, b):
    from_z = lax.rem(z + 8 - Z_SHIFTS[a], 4) + 4 * b
    return lax.rem(y + 4 - j, 4) * 8 + from_z


def inverse_factor(groups):
    lane = lax.broadcasted_iota(jnp.int32, (GROUP, HALF), 1)
    sub = lax.broadcasted_iota(jnp.int32, (GROUP, HALF), 0)
    groups = list(groups)
    count = len(groups)
    result = []
    for g in range(count):
        base = g * GROUP
        inside = (lane >= base) & (lane < base + GROUP)
        pivot = groups[g]
        cols = [splat_col(pivot, base + a) for a in range(GROUP)]
        s = [[splat_row(cols[a], b) if b >= a else None for a in range(GROUP)] for b in range(GROUP)]
        low = [[None] * GROUP for _ in range(GROUP)]
        inverse = []
        for a in range(GROUP):
            inverse.append(1.0 / s[a][a])
            for b in range(a + 1, GROUP):
                low[b][a] = s[b][a] * inverse[a]
            for b in range(a + 1, GROUP):
                for c in range(a + 1, b + 1):
                    s[b][c] = s[b][c] - low[b][a] * s[c][a]
        outside = jnp.where(inside, 0.0, pivot)
        rows = []
        for a in range(GROUP):
            row = splat_row(outside, a)
            for e in range(a):
                row = row - low[a][e] * rows[e]
            rows.append(jnp.where(lane == base + a, 1.0, row))
        for i in range(g + 1, count):
            here = groups[i]
            kept = jnp.where(inside, 0.0, here)
            factors = []
            for a in range(GROUP):
                c = splat_col(here, base + a)
                for e in range(a):
                    c = c - factors[e] * s[a][e]
                factors.append(c * inverse[a])
            for a in range(GROUP):
                kept = kept - factors[a] * rows[a]
            groups[i] = kept
        final = jnp.zeros_like(pivot)
        for a in range(GROUP):
            final = jnp.where(sub == a, rows[a] * lax.rsqrt(s[a][a]), final)
        result.append(jnp.where(lane <= sub + base, final, 0.0))
    return result


def factor_kernel(pos_ref, p0, p1, p2, p3, p0_high, p0_low, p1_high, p1_low, inverse_ref, high_ref, low_ref, gram):
    y, z = pos_ref[0], pos_ref[1]
    for j, piece in enumerate((p0, p1, p2, p3)):
        for a in range(4):
            for b in range(2):
                to_gram = pl.ds(pl.multiple_of(owner(y, z, j, a, b) * GROUP, GROUP), GROUP)
                gram[to_gram, :] = piece[pl.ds((2 * a + b) * GROUP, GROUP), :]

    def rows_of(value):
        return [value[GROUP * g : GROUP * (g + 1), :] for g in range(HALF // GROUP)]

    w11 = jnp.concatenate(inverse_factor(rows_of(gram[:HALF, :HALF])), axis=0)
    l21 = mm(gram[HALF:, :HALF], w11, 1, 1, HIGHEST)
    rest = gram[HALF:, HALF:] - mm(l21, l21, 1, 1, HIGHEST)
    w22 = jnp.concatenate(inverse_factor(rows_of(rest)), axis=0)
    w21 = -mm(w22, mm(l21, w11, 1, 0, HIGHEST), 1, 0, HIGHEST)
    inverse_ref[:HALF, :HALF] = w11
    inverse_ref[:HALF, HALF:] = jnp.zeros_like(w11)
    inverse_ref[HALF:, :HALF] = w21
    inverse_ref[HALF:, HALF:] = w22
    inverse = split(inverse_ref[...])
    for t, (p_high, p_low) in enumerate(((p0_high, p0_low), (p1_high, p1_low))):
        rows = pl.ds(t * 4 * PIECE, 4 * PIECE)
        high_ref[rows], low_ref[rows] = split(mm3((p_high[...], p_low[...]), inverse, 1, 1))


def factor(pos, pieces, powered):
    return pl.pallas_call(
        factor_kernel,
        out_shape=(
            jax.ShapeDtypeStruct((RANK, RANK), F32),
            jax.ShapeDtypeStruct((ROWS, RANK), BF16),
            jax.ShapeDtypeStruct((ROWS, RANK), BF16),
        ),
        in_specs=[scalars()] + [whole()] * 8,
        out_specs=(whole(),) * 3,
        scratch_shapes=[pltpu.VMEM((RANK, RANK), F32)],
        compiler_params=LIMIT,
        cost_estimate=pl.CostEstimate(flops=10 << 30, bytes_accessed=32 << 20, transcendentals=0),
        name="factor",
    )(pos, *pieces, *powered)


def coefficients_kernel(pos_ref, p0, p1, p2, p3, inverse_ref, coeff_ref, square_ref):
    y, z = pos_ref[0], pos_ref[1]
    inverse = split(inverse_ref[...])
    for j, piece in enumerate((p0, p1, p2, p3)):
        value = mm3(split(piece[...]), inverse, 1, 1)
        for a in range(4):
            for b in range(2):
                place = pl.ds(pl.multiple_of(owner(y, z, j, a, b) * COEFF, COEFF), COEFF)
                coeff_ref[place, :] = value[(2 * a + b) * COEFF : (2 * a + b + 1) * COEFF]
    value = coeff_ref[...]
    square_ref[...] = jnp.sum(value * value, axis=0, keepdims=True)


def coefficients_of(pos, pieces, inverse):
    return pl.pallas_call(
        coefficients_kernel,
        out_shape=(jax.ShapeDtypeStruct((COLS, RANK), F32), jax.ShapeDtypeStruct((1, RANK), F32)),
        in_specs=[scalars()] + [whole()] * 5,
        out_specs=(whole(),) * 2,
        compiler_params=LIMIT,
        name="coefficients",
    )(pos, *pieces, inverse)


def write_rows(pos_ref, half, value_ref, out_ref, sems, places=(0, 1, 2, 3)):
    x, core = pos_ref[2], pos_ref[3]
    copies = []
    for s in places:
        there = pl.ds(row_start(core if half == 0 else 1 - core, x, s), PIECE)
        here = pl.ds((4 * half + s) * PIECE, PIECE)
        copies.append(pltpu.make_async_copy(value_ref.at[here], out_ref.at[there], sems.at[4 * half + s]))
        copies[-1].start()
    return copies


def feedback_kernel(pos_ref, s0_high, s0_low, s1_high, s1_low, q_ref, c_ref, out_ref, buf, sems):
    coefficients = c_ref[...].astype(BF16)
    copies = []
    for t, (s_high, s_low) in enumerate(((s0_high, s0_low), (s1_high, s1_low))):
        rows = pl.ds(t * 4 * PIECE, 4 * PIECE)
        summed = s_high[...].astype(F32) + s_low[...].astype(F32)
        buf[rows] = summed - 0.05 * mm(q_ref[rows], coefficients, 1, 1)
        copies += write_rows(pos_ref, t, buf, out_ref, sems)
    for copy in copies:
        copy.wait()


def feedback(pos, summed, high, coefficients):
    return pl.pallas_call(
        feedback_kernel,
        out_shape=jax.ShapeDtypeStruct((ROWS, COLS), F32),
        in_specs=[scalars()] + [whole()] * 6,
        out_specs=in_hbm(),
        scratch_shapes=[pltpu.VMEM((ROWS, COLS), F32), pltpu.SemaphoreType.DMA((8,))],
        compiler_params=LIMIT,
        cost_estimate=pl.CostEstimate(flops=4 * 896 * 1024 * 256, bytes_accessed=10 << 20, transcendentals=0),
        name="feedback",
    )(pos, *summed, high, coefficients)


def update_kernel(scale, pos_ref, high_ref, low_ref, c_ref, s_ref, basis_ref, out_ref, b_buf, buf, b_sem, sems):
    basis = c_ref[...] * (1.0 / jnp.sqrt(s_ref[...] + 1e-6))
    b_buf[...] = basis
    store = pltpu.make_async_copy(b_buf, basis_ref, b_sem)
    store.start()
    basis = split(basis)
    copies = []
    for t in range(4):
        rows = pl.ds(t * 2 * PIECE, 2 * PIECE)
        buf[rows] = (scale * mm3((high_ref[rows], low_ref[rows]), basis, 1, 1)).astype(BF16)
        copies += write_rows(pos_ref, t // 2, buf, out_ref, sems, (2 * (t % 2), 2 * (t % 2) + 1))
    store.wait()
    for copy in copies:
        copy.wait()


def update(pos, high, low, coefficients, squares, scale):
    return pl.pallas_call(
        functools.partial(update_kernel, scale),
        out_shape=(
            jax.ShapeDtypeStruct((COLS, RANK), F32),
            jax.ShapeDtypeStruct((ROWS, COLS), BF16),
        ),
        in_specs=[scalars()] + [whole()] * 4,
        out_specs=(in_hbm(), in_hbm()),
        scratch_shapes=[
            pltpu.VMEM((COLS, RANK), F32),
            pltpu.VMEM((ROWS, COLS), BF16),
            pltpu.SemaphoreType.DMA,
            pltpu.SemaphoreType.DMA((8,)),
        ],
        compiler_params=LIMIT,
        name="update",
    )(pos, high, low, coefficients, squares)


def shards(momentum, gradient, old_basis):
    row = lax.axis_index("row")
    col = lax.axis_index("col")
    arguments = (momentum, gradient, old_basis)
    momentum, gradient, old_basis = (pltpu.with_memory_space_constraint(v, pltpu.HBM) for v in arguments)
    pos = jnp.stack([row // 8, row % 8, col // 2, col % 2]).astype(jnp.int32)

    away, s1_high, s1_low, m_own, g_own, b_high, b_low = power_away(pos, momentum, gradient, old_basis)
    came = send_core(away)
    here, s0_high, s0_low = power_own(m_own, g_own, b_high, b_low)
    summed = (s0_high, s0_low, s1_high, s1_low)
    parts = [here[s * PIECE : (s + 1) * PIECE] + came[s * PIECE : (s + 1) * PIECE] for s in range(4)]
    mine = ring_sum(parts[0], [None] + [send_x(parts[s], s) for s in (1, 2, 3)])
    own = jnp.concatenate([mine] + [send_x(mine, s) for s in (3, 2, 1)])
    other = send_core(own)
    p0_high, p0_low, total, gram = project_own(s0_high, s0_low, own)
    p1_high, p1_low, *slabs = project(pos, s1_high, s1_low, other, total, gram)
    powered = (p0_high, p0_low, p1_high, p1_low)

    far0, far1 = send_y(slabs[4], 1), send_y(slabs[5], 3)
    near1, near0 = send_y(slabs[3], 1), send_y(slabs[6], 3)
    via0, via1 = send_y(slabs[2] + far0, 1), send_y(slabs[7] + far1, 3)
    part0 = (slabs[0] + near0) + via0
    part1 = (slabs[1] + near1) + via1
    came = [send_z(part0[:PAIR], 1), send_z(part0[PAIR:], 2), send_z(part1[:PAIR], 7)]
    mine = ring_sum(part1[PAIR:], [None] + came)
    mine = mine + send_z(mine, 4)

    pieces = [mine] + [send_z(mine, s) for s in Z_SHIFTS[1:]]
    gram = jnp.concatenate([piece[2 * COEFF :] for piece in pieces])
    raw = jnp.concatenate([piece[: 2 * COEFF] for piece in pieces])
    grams = [gram] + [send_y(gram, s) for s in (1, 2, 3)]
    raws = [raw] + [send_y(raw, s) for s in (1, 2, 3)]
    inverse, high, low = factor(pos, grams, powered)

    coefficients, squares = coefficients_of(pos, raws, inverse)
    squares = squares + send_core(squares)
    came = [send_x(squares, s) for s in (1, 2, 3)]
    new_momentum = feedback(pos, summed, high, coefficients)
    new_momentum, *came = lax.optimization_barrier((new_momentum, *came))
    squares = ring_sum(squares, [None] + came)
    rms_scale = (28672 * 8192 / 256) ** 0.5
    new_basis, new_update = update(pos, high, low, coefficients, squares, rms_scale)
    return (new_momentum, new_basis, new_update)


def solution(mesh):
    placed = (P("row", "col"), P("row", "col"), P("col", None))
    return jax.shard_map(
        shards,
        mesh=mesh,
        in_specs=placed,
        out_specs=(P("row", "col"), P("col", None), P("row", "col")),
        check_vma=False,
    )
```

```python
import functools

import jax
import jax.numpy as jnp
from jax import lax
from jax.experimental import pallas as pl
from jax.experimental.pallas import tpu as pltpu
from jax.sharding import PartitionSpec as P

HIGHEST = lax.Precision.HIGHEST
F32 = jnp.float32
BF16 = jnp.bfloat16
HALF = 128
GROUP = 8
PANEL = 8
ROWS = 896
COLS = 1024
RANK = 256
PIECE = 112
SLAB = 256
COEFF = 32
PAIR = 80
LIMIT = pltpu.CompilerParams(vmem_limit_bytes=32 * 1024 * 1024)


def send(value, axis, move, size):
    return lax.ppermute(value, axis, [(i, move(i)) for i in range(size)])


def send_core(value):
    return send(value, "col", lambda i: i ^ 1, 8)


def send_x(value, s):
    return send(value, "col", lambda i: ((i // 2 + s) % 4) * 2 + i % 2, 8)


def send_y(value, s):
    return send(value, "row", lambda i: ((i // 8 + s) % 4) * 8 + i % 8, 32)


def send_z(value, s):
    return send(value, "row", lambda i: (i // 8) * 8 + (i % 8 + s) % 8, 32)


Z_SHIFTS = (0, 1, 2, 7)


def ring_sum(own, came):
    return (own + came[2]) + (came[1] + came[3])


def mm(a, b, ca, cb, precision=None):
    return lax.dot_general(
        a, b, (((ca,), (cb,)), ((), ())), precision=precision, preferred_element_type=F32
    )


def split(value):
    high = value.astype(BF16)
    return high, (value - high.astype(F32)).astype(BF16)


def mm3(a, b, ca, cb):
    return mm(a[0], b[0], ca, cb) + (mm(a[0], b[1], ca, cb) + mm(a[1], b[0], ca, cb))


def whole():
    return pl.BlockSpec(memory_space=pltpu.VMEM)


def in_hbm():
    return pl.BlockSpec(memory_space=pltpu.HBM)


def scalars():
    return pl.BlockSpec(memory_space=pltpu.SMEM)


def row_start(half, x, s):
    return pl.multiple_of(half * (4 * PIECE) + lax.rem(x + s, 4) * PIECE, PIECE)


def power_away_kernel(
    pos_ref, m_ref, g_ref, b_ref, out_ref, high_ref, low_ref, m_own, g_own, b_high, b_low, m_buf, g_buf, b_buf, sems, b_sem
):
    x, core = pos_ref[2], pos_ref[3]
    load = pltpu.make_async_copy(b_ref, b_buf, b_sem)
    away, own = [], []
    for s in range(4):
        there = pl.ds(s * PIECE, PIECE)
        here = pl.ds(row_start(1 - core, x, s), PIECE)
        away.append(pltpu.make_async_copy(m_ref.at[here], m_buf.at[there], sems.at[s, 0]))
        away.append(pltpu.make_async_copy(g_ref.at[here], g_buf.at[there], sems.at[s, 1]))
        here = pl.ds(row_start(core, x, s), PIECE)
        own.append(pltpu.make_async_copy(m_ref.at[here], m_own.at[there], sems.at[4 + s, 0]))
        own.append(pltpu.make_async_copy(g_ref.at[here], g_own.at[there], sems.at[4 + s, 1]))
    load.start()
    for copy in away[:4]:
        copy.start()
    load.wait()
    for copy in away[4:]:
        copy.start()
    basis = split(b_buf[...])
    b_high[...], b_low[...] = basis
    for t in range(2):
        for copy in away[4 * t : 4 * t + 4]:
            copy.wait()
        if t == 0:
            for copy in own:
                copy.start()
        rows = pl.ds(t * 2 * PIECE, 2 * PIECE)
        high, low = split(m_buf[rows] + g_buf[rows].astype(F32))
        high_ref[rows] = high
        low_ref[rows] = low
        out_ref[rows] = mm3((high, low), basis, 1, 0)
    for copy in own:
        copy.wait()


def power_away(pos, momentum, gradient, basis):
    half = (4 * PIECE, COLS)
    return pl.pallas_call(
        power_away_kernel,
        out_shape=(
            jax.ShapeDtypeStruct((4 * PIECE, RANK), F32),
            jax.ShapeDtypeStruct(half, BF16),
            jax.ShapeDtypeStruct(half, BF16),
            jax.ShapeDtypeStruct(half, F32),
            jax.ShapeDtypeStruct(half, BF16),
            jax.ShapeDtypeStruct((COLS, RANK), BF16),
            jax.ShapeDtypeStruct((COLS, RANK), BF16),
        ),
        in_specs=[scalars(), in_hbm(), in_hbm(), in_hbm()],
        out_specs=(whole(),) * 7,
        scratch_shapes=[
            pltpu.VMEM(half, F32),
            pltpu.VMEM(half, BF16),
            pltpu.VMEM((COLS, RANK), F32),
            pltpu.SemaphoreType.DMA((8, 2)),
            pltpu.SemaphoreType.DMA,
        ],
        compiler_params=LIMIT,
        name="power_away",
    )(pos, momentum, gradient, basis)


def power_own_kernel(m_ref, g_ref, b_high, b_low, out_ref, high_ref, low_ref):
    for t in range(2):
        rows = pl.ds(t * 2 * PIECE, 2 * PIECE)
        high, low = split(m_ref[rows] + g_ref[rows].astype(F32))
        high_ref[rows] = high
        low_ref[rows] = low
        out_ref[rows] = mm3((high, low), (b_high[...], b_low[...]), 1, 0)


def power_own(momentum, gradient, b_high, b_low):
    return pl.pallas_call(
        power_own_kernel,
        out_shape=(
            jax.ShapeDtypeStruct((4 * PIECE, RANK), F32),
            jax.ShapeDtypeStruct((4 * PIECE, COLS), BF16),
            jax.ShapeDtypeStruct((4 * PIECE, COLS), BF16),
        ),
        in_specs=[whole()] * 4,
        out_specs=(whole(),) * 3,
        compiler_params=LIMIT,
        cost_estimate=pl.CostEstimate(flops=6 * 448 * 1024 * 256, bytes_accessed=4 << 20, transcendentals=0),
        name="power_own",
    )(momentum, gradient, b_high, b_low)


def project_own_kernel(s_high, s_low, own_ref, high_ref, low_ref, total_ref, gram_ref):
    value = split(own_ref[...])
    high_ref[...], low_ref[...] = value
    gram_ref[...] = mm3(value, value, 0, 0)
    for t in range(4):
        columns = pl.ds(t * SLAB, SLAB)
        total_ref[columns, :] = mm3((s_high[:, columns], s_low[:, columns]), value, 0, 0)


def project_own(s_high, s_low, own):
    return pl.pallas_call(
        project_own_kernel,
        out_shape=(
            jax.ShapeDtypeStruct((4 * PIECE, RANK), BF16),
            jax.ShapeDtypeStruct((4 * PIECE, RANK), BF16),
            jax.ShapeDtypeStruct((COLS, RANK), F32),
            jax.ShapeDtypeStruct((RANK, RANK), F32),
        ),
        in_specs=[whole()] * 3,
        out_specs=(whole(),) * 4,
        compiler_params=LIMIT,
        cost_estimate=pl.CostEstimate(flops=6 * 448 * 1280 * 256, bytes_accessed=4 << 20, transcendentals=0),
        name="project_own",
    )(s_high, s_low, own)


def fill(z, target, total_ref, gram_ref, out0_ref, out1_ref):
    for out_ref, position, a in ((out0_ref, 0, 1), (out0_ref, 1, 2), (out1_ref, 0, 3), (out1_ref, 1, 0)):
        for b in range(2):
            source = lax.rem(z + Z_SHIFTS[a], 4) + 4 * b
            place = position * PAIR
            from_total = pl.ds(pl.multiple_of(source * COEFF, COEFF), COEFF)
            from_gram = pl.ds(pl.multiple_of((target * 8 + source) * GROUP, GROUP), GROUP)
            out_ref[pl.ds(place + b * COEFF, COEFF), :] = total_ref[from_total, :]
            out_ref[pl.ds(place + 2 * COEFF + b * GROUP, GROUP), :] = gram_ref[from_gram, :]


def project_target(y, shift, s_high, s_low, value, total_ref, buf):
    target = lax.rem(y + shift, 4)
    columns = pl.ds(pl.multiple_of(target * SLAB, SLAB), SLAB)
    buf[...] = total_ref[columns, :] + mm3((s_high[:, columns], s_low[:, columns]), value, 0, 0)
    return target


def project_far_kernel(
    pos_ref, s_high, s_low, other_ref, total_ref, gram_ref, high_ref, low_ref, sum_ref, out0_ref, out1_ref, buf
):
    y, z = pos_ref[0], pos_ref[1]
    value = split(other_ref[...])
    high_ref[...], low_ref[...] = value
    sum_ref[...] = gram_ref[...] + mm3(value, value, 0, 0)
    target = project_target(y, 2, s_high, s_low, value, total_ref, buf)
    fill(z, target, buf, sum_ref, out0_ref, out1_ref)


def project_far(pos, s_high, s_low, other, total, gram):
    return pl.pallas_call(
        project_far_kernel,
        out_shape=(
            jax.ShapeDtypeStruct((4 * PIECE, RANK), BF16),
            jax.ShapeDtypeStruct((4 * PIECE, RANK), BF16),
            jax.ShapeDtypeStruct((RANK, RANK), F32),
            jax.ShapeDtypeStruct((2 * PAIR, RANK), F32),
            jax.ShapeDtypeStruct((2 * PAIR, RANK), F32),
        ),
        in_specs=[scalars()] + [whole()] * 5,
        out_specs=(whole(),) * 5,
        scratch_shapes=[pltpu.VMEM((SLAB, RANK), F32)],
        compiler_params=LIMIT,
        name="project_far",
    )(pos, s_high, s_low, other, total, gram)


def project_kernel(pos_ref, s_high, s_low, high_ref, low_ref, total_ref, gram_ref, *refs):
    y, z = pos_ref[0], pos_ref[1]
    value = (high_ref[...], low_ref[...])
    for k, shift in enumerate((0, 1, 3)):
        buf = refs[6 + k]
        target = project_target(y, shift, s_high, s_low, value, total_ref, buf)
        fill(z, target, buf, gram_ref, refs[2 * k], refs[2 * k + 1])


def project(pos, s_high, s_low, high, low, total, gram):
    return pl.pallas_call(
        project_kernel,
        out_shape=(jax.ShapeDtypeStruct((2 * PAIR, RANK), F32),) * 6,
        in_specs=[scalars()] + [whole()] * 6,
        out_specs=(whole(),) * 6,
        scratch_shapes=[pltpu.VMEM((SLAB, RANK), F32)] * 3,
        compiler_params=LIMIT,
        cost_estimate=pl.CostEstimate(flops=6 * 448 * 768 * 256, bytes_accessed=4 << 20, transcendentals=0),
        name="project",
    )(pos, s_high, s_low, high, low, total, gram)


def splat_row(value, row):
    return jnp.broadcast_to(value[row : row + 1, :], value.shape)


def splat_col(value, col):
    return jnp.broadcast_to(value[:, col : col + 1], value.shape)


def owner(y, z, j, a, b):
    from_z = lax.rem(z + 8 - Z_SHIFTS[a], 4) + 4 * b
    return lax.rem(y + 4 - j, 4) * 8 + from_z


def inverse_factor(groups):
    lane = lax.broadcasted_iota(jnp.int32, (GROUP, HALF), 1)
    sub = lax.broadcasted_iota(jnp.int32, (GROUP, HALF), 0)
    groups = list(groups)
    count = len(groups)
    result = []
    kept_rows, factor_rows = [], []
    for g in range(count):
        base = g * GROUP
        inside = (lane >= base) & (lane < base + GROUP)
        pivot = groups[g]
        cols = [splat_col(pivot, base + a) for a in range(GROUP)]
        s = [[splat_row(cols[a], b) if b >= a else None for a in range(GROUP)] for b in range(GROUP)]
        low = [[None] * GROUP for _ in range(GROUP)]
        inverse = []
        for a in range(GROUP):
            inverse.append(1.0 / s[a][a])
            for b in range(a + 1, GROUP):
                low[b][a] = s[b][a] * inverse[a]
            for b in range(a + 1, GROUP):
                for c in range(a + 1, b + 1):
                    s[b][c] = s[b][c] - low[b][a] * s[c][a]
        outside = jnp.where(inside, 0.0, pivot)
        rows = []
        for a in range(GROUP):
            row = splat_row(outside, a)
            for e in range(a):
                row = row - low[a][e] * rows[e]
            rows.append(jnp.where(lane == base + a, 1.0, row))
        last = (g // PANEL + 1) * PANEL
        for i in range(g + 1, last):
            here = groups[i]
            kept = jnp.where(inside, 0.0, here)
            factors = []
            for a in range(GROUP):
                c = splat_col(here, base + a)
                for e in range(a):
                    c = c - factors[e] * s[a][e]
                factors.append(c * inverse[a])
            for a in range(GROUP):
                kept = kept - factors[a] * rows[a]
            groups[i] = kept
        final = jnp.zeros_like(pivot)
        plain = jnp.zeros_like(pivot)
        scaled = jnp.zeros_like(pivot)
        for a in range(GROUP):
            final = jnp.where(sub == a, rows[a] * lax.rsqrt(s[a][a]), final)
            plain = jnp.where(sub == a, rows[a], plain)
            scaled = jnp.where(sub == a, rows[a] * inverse[a], scaled)
        kept_rows.append(jnp.where((lane >= base) & (lane < last * GROUP) & (lane > sub + base), 0.0, plain))
        factor_rows.append(scaled)
        if g + 1 == last and last < count:
            change = mm(jnp.concatenate(factor_rows), jnp.concatenate(kept_rows), 0, 0, HIGHEST)
            start = (last - PANEL) * GROUP
            panel = (lane >= start) & (lane < last * GROUP)
            for i in range(last, count):
                groups[i] = jnp.where(panel, 0.0, groups[i]) - change[GROUP * i : GROUP * (i + 1), :]
            kept_rows, factor_rows = [], []
        result.append(jnp.where(lane <= sub + base, final, 0.0))
    return result


def factor_kernel(pos_ref, p0, p1, p2, p3, p0_high, p0_low, p1_high, p1_low, inverse_ref, high_ref, low_ref, gram):
    y, z = pos_ref[0], pos_ref[1]
    for j, piece in enumerate((p0, p1, p2, p3)):
        for a in range(4):
            for b in range(2):
                to_gram = pl.ds(pl.multiple_of(owner(y, z, j, a, b) * GROUP, GROUP), GROUP)
                gram[to_gram, :] = piece[pl.ds((2 * a + b) * GROUP, GROUP), :]

    def rows_of(value):
        return [value[GROUP * g : GROUP * (g + 1), :] for g in range(HALF // GROUP)]

    w11 = jnp.concatenate(inverse_factor(rows_of(gram[:HALF, :HALF])), axis=0)
    l21 = mm(gram[HALF:, :HALF], w11, 1, 1, HIGHEST)
    rest = gram[HALF:, HALF:] - mm(l21, l21, 1, 1, HIGHEST)
    w22 = jnp.concatenate(inverse_factor(rows_of(rest)), axis=0)
    w21 = -mm(w22, mm(l21, w11, 1, 0, HIGHEST), 1, 0, HIGHEST)
    inverse_ref[:HALF, :HALF] = w11
    inverse_ref[:HALF, HALF:] = jnp.zeros_like(w11)
    inverse_ref[HALF:, :HALF] = w21
    inverse_ref[HALF:, HALF:] = w22
    inverse = split(inverse_ref[...])
    for t, (p_high, p_low) in enumerate(((p0_high, p0_low), (p1_high, p1_low))):
        rows = pl.ds(t * 4 * PIECE, 4 * PIECE)
        high_ref[rows], low_ref[rows] = split(mm3((p_high[...], p_low[...]), inverse, 1, 1))


def factor(pos, pieces, powered):
    return pl.pallas_call(
        factor_kernel,
        out_shape=(
            jax.ShapeDtypeStruct((RANK, RANK), F32),
            jax.ShapeDtypeStruct((ROWS, RANK), BF16),
            jax.ShapeDtypeStruct((ROWS, RANK), BF16),
        ),
        in_specs=[scalars()] + [whole()] * 8,
        out_specs=(whole(),) * 3,
        scratch_shapes=[pltpu.VMEM((RANK, RANK), F32)],
        compiler_params=LIMIT,
        cost_estimate=pl.CostEstimate(flops=10 << 30, bytes_accessed=32 << 20, transcendentals=0),
        name="factor",
    )(pos, *pieces, *powered)


def coefficients_kernel(pos_ref, p0, p1, p2, p3, inverse_ref, coeff_ref, high_ref, low_ref, square_ref):
    y, z = pos_ref[0], pos_ref[1]
    inverse = split(inverse_ref[...])
    for j, piece in enumerate((p0, p1, p2, p3)):
        value = mm3(split(piece[...]), inverse, 1, 1)
        for a in range(4):
            for b in range(2):
                place = pl.ds(pl.multiple_of(owner(y, z, j, a, b) * COEFF, COEFF), COEFF)
                coeff_ref[place, :] = value[(2 * a + b) * COEFF : (2 * a + b + 1) * COEFF]
    value = coeff_ref[...]
    high_ref[...], low_ref[...] = split(value)
    square_ref[...] = jnp.sum(value * value, axis=0, keepdims=True)


def coefficients_of(pos, pieces, inverse):
    return pl.pallas_call(
        coefficients_kernel,
        out_shape=(
            jax.ShapeDtypeStruct((COLS, RANK), F32),
            jax.ShapeDtypeStruct((COLS, RANK), BF16),
            jax.ShapeDtypeStruct((COLS, RANK), BF16),
            jax.ShapeDtypeStruct((1, RANK), F32),
        ),
        in_specs=[scalars()] + [whole()] * 5,
        out_specs=(whole(),) * 4,
        compiler_params=LIMIT,
        name="coefficients",
    )(pos, *pieces, inverse)


def write_rows(pos_ref, half, value_ref, out_ref, sems):
    x, core = pos_ref[2], pos_ref[3]
    copies = []
    for s in range(4):
        there = pl.ds(row_start(core if half == 0 else 1 - core, x, s), PIECE)
        here = pl.ds((4 * half + s) * PIECE, PIECE)
        copies.append(pltpu.make_async_copy(value_ref.at[here], out_ref.at[there], sems.at[4 * half + s]))
        copies[-1].start()
    return copies


def feedback_kernel(pos_ref, s0_high, s0_low, s1_high, s1_low, q_ref, c_ref, out_ref, buf, sems):
    coefficients = c_ref[...]
    copies = []
    for t, (s_high, s_low) in enumerate(((s0_high, s0_low), (s1_high, s1_low))):
        rows = pl.ds(t * 4 * PIECE, 4 * PIECE)
        summed = s_high[...].astype(F32) + s_low[...].astype(F32)
        buf[rows] = summed - 0.05 * mm(q_ref[rows], coefficients, 1, 1)
        copies += write_rows(pos_ref, t, buf, out_ref, sems)
    for copy in copies:
        copy.wait()


def feedback(pos, summed, high, coefficients):
    return pl.pallas_call(
        feedback_kernel,
        out_shape=jax.ShapeDtypeStruct((ROWS, COLS), F32),
        in_specs=[scalars()] + [whole()] * 6,
        out_specs=in_hbm(),
        scratch_shapes=[pltpu.VMEM((ROWS, COLS), F32), pltpu.SemaphoreType.DMA((8,))],
        compiler_params=LIMIT,
        cost_estimate=pl.CostEstimate(flops=4 * 896 * 1024 * 256, bytes_accessed=10 << 20, transcendentals=0),
        name="feedback",
    )(pos, *summed, high, coefficients)


def update_kernel(
    scale, pos_ref, high_ref, low_ref, c_ref, c_high, c_low, s_ref, basis_ref, out_ref, b_buf, buf, b_sem, sems
):
    norm = 1.0 / jnp.sqrt(s_ref[...] + 1e-6)
    b_buf[...] = c_ref[...] * norm
    store = pltpu.make_async_copy(b_buf, basis_ref, b_sem)
    store.start()
    coefficients = (c_high[...], c_low[...])
    copies = []
    for t in range(2):
        rows = pl.ds(t * 4 * PIECE, 4 * PIECE)
        q = split((high_ref[rows].astype(F32) + low_ref[rows].astype(F32)) * norm)
        buf[rows] = (scale * mm3(q, coefficients, 1, 1)).astype(BF16)
        copies += write_rows(pos_ref, t, buf, out_ref, sems)
    store.wait()
    for copy in copies:
        copy.wait()


def update(pos, high, low, coefficients, c_high, c_low, squares, scale):
    return pl.pallas_call(
        functools.partial(update_kernel, scale),
        out_shape=(
            jax.ShapeDtypeStruct((COLS, RANK), F32),
            jax.ShapeDtypeStruct((ROWS, COLS), BF16),
        ),
        in_specs=[scalars()] + [whole()] * 6,
        out_specs=(in_hbm(), in_hbm()),
        scratch_shapes=[
            pltpu.VMEM((COLS, RANK), F32),
            pltpu.VMEM((ROWS, COLS), BF16),
            pltpu.SemaphoreType.DMA,
            pltpu.SemaphoreType.DMA((8,)),
        ],
        compiler_params=LIMIT,
        name="update",
    )(pos, high, low, coefficients, c_high, c_low, squares)


def shards(momentum, gradient, old_basis):
    row = lax.axis_index("row")
    col = lax.axis_index("col")
    arguments = (momentum, gradient, old_basis)
    momentum, gradient, old_basis = (pltpu.with_memory_space_constraint(v, pltpu.HBM) for v in arguments)
    pos = jnp.stack([row // 8, row % 8, col // 2, col % 2]).astype(jnp.int32)

    away, s1_high, s1_low, m_own, g_own, b_high, b_low = power_away(pos, momentum, gradient, old_basis)
    came = send_core(away)
    here, s0_high, s0_low = power_own(m_own, g_own, b_high, b_low)
    summed = (s0_high, s0_low, s1_high, s1_low)
    parts = [here[s * PIECE : (s + 1) * PIECE] + came[s * PIECE : (s + 1) * PIECE] for s in range(4)]
    mine = ring_sum(parts[0], [None] + [send_x(parts[s], s) for s in (1, 2, 3)])
    own = jnp.concatenate([mine] + [send_x(mine, s) for s in (3, 2, 1)])
    other = send_core(own)
    p0_high, p0_low, total, gram = project_own(s0_high, s0_low, own)
    p1_high, p1_low, gram, *far = project_far(pos, s1_high, s1_low, other, total, gram)
    own0, own1, plus0, plus1, minus0, minus1 = project(pos, s1_high, s1_low, p1_high, p1_low, total, gram)
    powered = (p0_high, p0_low, p1_high, p1_low)

    far0, far1 = send_y(far[0], 1), send_y(far[1], 3)
    near1, near0 = send_y(plus1, 1), send_y(minus0, 3)
    via0, via1 = send_y(plus0 + far0, 1), send_y(minus1 + far1, 3)
    part0 = (own0 + near0) + via0
    part1 = (own1 + near1) + via1
    came = [send_z(part0[:PAIR], 1), send_z(part0[PAIR:], 2), send_z(part1[:PAIR], 7)]
    mine = ring_sum(part1[PAIR:], [None] + came)
    mine = mine + send_z(mine, 4)

    pieces = [mine] + [send_z(mine, s) for s in Z_SHIFTS[1:]]
    gram = jnp.concatenate([piece[2 * COEFF :] for piece in pieces])
    raw = jnp.concatenate([piece[: 2 * COEFF] for piece in pieces])
    grams = [gram] + [send_y(gram, s) for s in (1, 2, 3)]
    raws = [raw] + [send_y(raw, s) for s in (1, 2, 3)]
    inverse, high, low = factor(pos, grams, powered)

    coefficients, c_high, c_low, squares = coefficients_of(pos, raws, inverse)
    squares = squares + send_core(squares)
    came = [send_x(squares, s) for s in (1, 2, 3)]
    new_momentum = feedback(pos, summed, high, c_high)
    new_momentum, *came = lax.optimization_barrier((new_momentum, *came))
    squares = ring_sum(squares, [None] + came)
    rms_scale = (28672 * 8192 / 256) ** 0.5
    new_basis, new_update = update(pos, high, low, coefficients, c_high, c_low, squares, rms_scale)
    return (new_momentum, new_basis, new_update)


def solution(mesh):
    placed = (P("row", "col"), P("row", "col"), P("col", None))
    return jax.shard_map(
        shards,
        mesh=mesh,
        in_specs=placed,
        out_specs=(P("row", "col"), P("col", None), P("row", "col")),
        check_vma=False,
    )
```

```python
import functools

import jax
import jax.numpy as jnp
from jax import lax
from jax.experimental import pallas as pl
from jax.experimental.pallas import tpu as pltpu
from jax.sharding import PartitionSpec as P

HIGHEST = lax.Precision.HIGHEST
F32 = jnp.float32
BF16 = jnp.bfloat16
HALF = 128
GROUP = 8
PANEL = 8
ROWS = 896
COLS = 1024
RANK = 256
PIECE = 112
SLAB = 256
COEFF = 32
PAIR = 80
LIMIT = pltpu.CompilerParams(vmem_limit_bytes=32 * 1024 * 1024)


def send(value, axis, move, size):
    return lax.ppermute(value, axis, [(i, move(i)) for i in range(size)])


def send_core(value):
    return send(value, "col", lambda i: i ^ 1, 8)


def send_x(value, s):
    return send(value, "col", lambda i: ((i // 2 + s) % 4) * 2 + i % 2, 8)


def send_y(value, s):
    return send(value, "row", lambda i: ((i // 8 + s) % 4) * 8 + i % 8, 32)


def send_z(value, s):
    return send(value, "row", lambda i: (i // 8) * 8 + (i % 8 + s) % 8, 32)


Z_SHIFTS = (0, 1, 2, 7)


def ring_sum(own, came):
    return (own + came[2]) + (came[1] + came[3])


def mm(a, b, ca, cb, precision=None):
    return lax.dot_general(
        a, b, (((ca,), (cb,)), ((), ())), precision=precision, preferred_element_type=F32
    )


def split(value):
    high = value.astype(BF16)
    return high, (value - high.astype(F32)).astype(BF16)


def mm3(a, b, ca, cb):
    return mm(a[0], b[0], ca, cb) + (mm(a[0], b[1], ca, cb) + mm(a[1], b[0], ca, cb))


def whole():
    return pl.BlockSpec(memory_space=pltpu.VMEM)


def in_hbm():
    return pl.BlockSpec(memory_space=pltpu.HBM)


def scalars():
    return pl.BlockSpec(memory_space=pltpu.SMEM)


def row_start(half, x, s):
    return pl.multiple_of(half * (4 * PIECE) + lax.rem(x + s, 4) * PIECE, PIECE)


def power_away_kernel(
    pos_ref, m_ref, g_ref, b_ref, out_ref, high_ref, low_ref, m_own, g_own, b_high, b_low, m_buf, g_buf, b_buf, sems, b_sem
):
    x, core = pos_ref[2], pos_ref[3]
    load = pltpu.make_async_copy(b_ref, b_buf, b_sem)
    away, own = [], []
    for s in range(4):
        there = pl.ds(s * PIECE, PIECE)
        here = pl.ds(row_start(1 - core, x, s), PIECE)
        away.append(pltpu.make_async_copy(m_ref.at[here], m_buf.at[there], sems.at[s, 0]))
        away.append(pltpu.make_async_copy(g_ref.at[here], g_buf.at[there], sems.at[s, 1]))
        here = pl.ds(row_start(core, x, s), PIECE)
        own.append(pltpu.make_async_copy(m_ref.at[here], m_own.at[there], sems.at[4 + s, 0]))
        own.append(pltpu.make_async_copy(g_ref.at[here], g_own.at[there], sems.at[4 + s, 1]))
    load.start()
    for copy in away[:4]:
        copy.start()
    load.wait()
    for copy in away[4:]:
        copy.start()
    basis = split(b_buf[...])
    b_high[...], b_low[...] = basis
    for t in range(2):
        for copy in away[4 * t : 4 * t + 4]:
            copy.wait()
        if t == 0:
            for copy in own:
                copy.start()
        rows = pl.ds(t * 2 * PIECE, 2 * PIECE)
        high, low = split(m_buf[rows] + g_buf[rows].astype(F32))
        high_ref[rows] = high
        low_ref[rows] = low
        out_ref[rows] = mm3((high, low), basis, 1, 0)
    for copy in own:
        copy.wait()


def power_away(pos, momentum, gradient, basis):
    half = (4 * PIECE, COLS)
    return pl.pallas_call(
        power_away_kernel,
        out_shape=(
            jax.ShapeDtypeStruct((4 * PIECE, RANK), F32),
            jax.ShapeDtypeStruct(half, BF16),
            jax.ShapeDtypeStruct(half, BF16),
            jax.ShapeDtypeStruct(half, F32),
            jax.ShapeDtypeStruct(half, BF16),
            jax.ShapeDtypeStruct((COLS, RANK), BF16),
            jax.ShapeDtypeStruct((COLS, RANK), BF16),
        ),
        in_specs=[scalars(), in_hbm(), in_hbm(), in_hbm()],
        out_specs=(whole(),) * 7,
        scratch_shapes=[
            pltpu.VMEM(half, F32),
            pltpu.VMEM(half, BF16),
            pltpu.VMEM((COLS, RANK), F32),
            pltpu.SemaphoreType.DMA((8, 2)),
            pltpu.SemaphoreType.DMA,
        ],
        compiler_params=LIMIT,
        name="power_away",
    )(pos, momentum, gradient, basis)


def power_own_kernel(m_ref, g_ref, b_high, b_low, out_ref, high_ref, low_ref):
    for t in range(2):
        rows = pl.ds(t * 2 * PIECE, 2 * PIECE)
        high, low = split(m_ref[rows] + g_ref[rows].astype(F32))
        high_ref[rows] = high
        low_ref[rows] = low
        out_ref[rows] = mm3((high, low), (b_high[...], b_low[...]), 1, 0)


def power_own(momentum, gradient, b_high, b_low):
    return pl.pallas_call(
        power_own_kernel,
        out_shape=(
            jax.ShapeDtypeStruct((4 * PIECE, RANK), F32),
            jax.ShapeDtypeStruct((4 * PIECE, COLS), BF16),
            jax.ShapeDtypeStruct((4 * PIECE, COLS), BF16),
        ),
        in_specs=[whole()] * 4,
        out_specs=(whole(),) * 3,
        compiler_params=LIMIT,
        cost_estimate=pl.CostEstimate(flops=6 * 448 * 1024 * 256, bytes_accessed=4 << 20, transcendentals=0),
        name="power_own",
    )(momentum, gradient, b_high, b_low)


def project_own_kernel(s_high, s_low, own_ref, high_ref, low_ref, total_ref, gram_ref):
    value = split(own_ref[...])
    high_ref[...], low_ref[...] = value
    gram_ref[...] = mm3(value, value, 0, 0)
    for t in range(4):
        columns = pl.ds(t * SLAB, SLAB)
        total_ref[columns, :] = mm3((s_high[:, columns], s_low[:, columns]), value, 0, 0)


def project_own(s_high, s_low, own):
    return pl.pallas_call(
        project_own_kernel,
        out_shape=(
            jax.ShapeDtypeStruct((4 * PIECE, RANK), BF16),
            jax.ShapeDtypeStruct((4 * PIECE, RANK), BF16),
            jax.ShapeDtypeStruct((COLS, RANK), F32),
            jax.ShapeDtypeStruct((RANK, RANK), F32),
        ),
        in_specs=[whole()] * 3,
        out_specs=(whole(),) * 4,
        compiler_params=LIMIT,
        cost_estimate=pl.CostEstimate(flops=6 * 448 * 1280 * 256, bytes_accessed=4 << 20, transcendentals=0),
        name="project_own",
    )(s_high, s_low, own)


def fill(z, target, total_ref, gram_ref, out0_ref, out1_ref):
    for out_ref, position, a in ((out0_ref, 0, 1), (out0_ref, 1, 2), (out1_ref, 0, 3), (out1_ref, 1, 0)):
        for b in range(2):
            source = lax.rem(z + Z_SHIFTS[a], 4) + 4 * b
            place = position * PAIR
            from_total = pl.ds(pl.multiple_of(source * COEFF, COEFF), COEFF)
            from_gram = pl.ds(pl.multiple_of((target * 8 + source) * GROUP, GROUP), GROUP)
            out_ref[pl.ds(place + b * COEFF, COEFF), :] = total_ref[from_total, :]
            out_ref[pl.ds(place + 2 * COEFF + b * GROUP, GROUP), :] = gram_ref[from_gram, :]


def project_target(y, shift, s_high, s_low, value, total_ref, buf):
    target = lax.rem(y + shift, 4)
    columns = pl.ds(pl.multiple_of(target * SLAB, SLAB), SLAB)
    buf[...] = total_ref[columns, :] + mm3((s_high[:, columns], s_low[:, columns]), value, 0, 0)
    return target


def project_far_kernel(
    pos_ref, s_high, s_low, other_ref, total_ref, gram_ref, high_ref, low_ref, sum_ref, out0_ref, out1_ref, buf
):
    y, z = pos_ref[0], pos_ref[1]
    value = split(other_ref[...])
    high_ref[...], low_ref[...] = value
    sum_ref[...] = gram_ref[...] + mm3(value, value, 0, 0)
    target = project_target(y, 2, s_high, s_low, value, total_ref, buf)
    fill(z, target, buf, sum_ref, out0_ref, out1_ref)


def project_far(pos, s_high, s_low, other, total, gram):
    return pl.pallas_call(
        project_far_kernel,
        out_shape=(
            jax.ShapeDtypeStruct((4 * PIECE, RANK), BF16),
            jax.ShapeDtypeStruct((4 * PIECE, RANK), BF16),
            jax.ShapeDtypeStruct((RANK, RANK), F32),
            jax.ShapeDtypeStruct((2 * PAIR, RANK), F32),
            jax.ShapeDtypeStruct((2 * PAIR, RANK), F32),
        ),
        in_specs=[scalars()] + [whole()] * 5,
        out_specs=(whole(),) * 5,
        scratch_shapes=[pltpu.VMEM((SLAB, RANK), F32)],
        compiler_params=LIMIT,
        name="project_far",
    )(pos, s_high, s_low, other, total, gram)


def project_kernel(pos_ref, s_high, s_low, high_ref, low_ref, total_ref, gram_ref, *refs):
    y, z = pos_ref[0], pos_ref[1]
    value = (high_ref[...], low_ref[...])
    for k, shift in enumerate((0, 1, 3)):
        buf = refs[6 + k]
        target = project_target(y, shift, s_high, s_low, value, total_ref, buf)
        fill(z, target, buf, gram_ref, refs[2 * k], refs[2 * k + 1])


def project(pos, s_high, s_low, high, low, total, gram):
    return pl.pallas_call(
        project_kernel,
        out_shape=(jax.ShapeDtypeStruct((2 * PAIR, RANK), F32),) * 6,
        in_specs=[scalars()] + [whole()] * 6,
        out_specs=(whole(),) * 6,
        scratch_shapes=[pltpu.VMEM((SLAB, RANK), F32)] * 3,
        compiler_params=LIMIT,
        cost_estimate=pl.CostEstimate(flops=6 * 448 * 768 * 256, bytes_accessed=4 << 20, transcendentals=0),
        name="project",
    )(pos, s_high, s_low, high, low, total, gram)


def splat_row(value, row):
    return jnp.broadcast_to(value[row : row + 1, :], value.shape)


def splat_col(value, col):
    return jnp.broadcast_to(value[:, col : col + 1], value.shape)


def owner(y, z, j, a, b):
    from_z = lax.rem(z + 8 - Z_SHIFTS[a], 4) + 4 * b
    return lax.rem(y + 4 - j, 4) * 8 + from_z


def inverse_factor(groups):
    lane = lax.broadcasted_iota(jnp.int32, (GROUP, HALF), 1)
    sub = lax.broadcasted_iota(jnp.int32, (GROUP, HALF), 0)
    groups = list(groups)
    count = len(groups)
    result = []
    kept_rows, factor_rows = [], []
    for g in range(count):
        base = g * GROUP
        inside = (lane >= base) & (lane < base + GROUP)
        pivot = groups[g]
        cols = [splat_col(pivot, base + a) for a in range(GROUP)]
        s = [[splat_row(cols[a], b) if b >= a else None for a in range(GROUP)] for b in range(GROUP)]
        low = [[None] * GROUP for _ in range(GROUP)]
        inverse = []
        for a in range(GROUP):
            inverse.append(1.0 / s[a][a])
            for b in range(a + 1, GROUP):
                low[b][a] = s[b][a] * inverse[a]
            for b in range(a + 1, GROUP):
                for c in range(a + 1, b + 1):
                    s[b][c] = s[b][c] - low[b][a] * s[c][a]
        outside = jnp.where(inside, 0.0, pivot)
        rows = []
        for a in range(GROUP):
            row = splat_row(outside, a)
            for e in range(a):
                row = row - low[a][e] * rows[e]
            rows.append(jnp.where(lane == base + a, 1.0, row))
        last = (g // PANEL + 1) * PANEL
        for i in range(g + 1, last):
            here = groups[i]
            kept = jnp.where(inside, 0.0, here)
            factors = []
            for a in range(GROUP):
                c = splat_col(here, base + a)
                for e in range(a):
                    c = c - factors[e] * s[a][e]
                factors.append(c * inverse[a])
            for a in range(GROUP):
                kept = kept - factors[a] * rows[a]
            groups[i] = kept
        final = jnp.zeros_like(pivot)
        plain = jnp.zeros_like(pivot)
        scaled = jnp.zeros_like(pivot)
        for a in range(GROUP):
            final = jnp.where(sub == a, rows[a] * lax.rsqrt(s[a][a]), final)
            plain = jnp.where(sub == a, rows[a], plain)
            scaled = jnp.where(sub == a, rows[a] * inverse[a], scaled)
        kept_rows.append(jnp.where((lane >= base) & (lane < last * GROUP) & (lane > sub + base), 0.0, plain))
        factor_rows.append(scaled)
        if g + 1 == last and last < count:
            change = mm(jnp.concatenate(factor_rows), jnp.concatenate(kept_rows), 0, 0, HIGHEST)
            start = (last - PANEL) * GROUP
            panel = (lane >= start) & (lane < last * GROUP)
            for i in range(last, count):
                groups[i] = jnp.where(panel, 0.0, groups[i]) - change[GROUP * i : GROUP * (i + 1), :]
            kept_rows, factor_rows = [], []
        result.append(jnp.where(lane <= sub + base, final, 0.0))
    return result


def factor_kernel(pos_ref, p0, p1, p2, p3, inverse_ref, gram):
    y, z = pos_ref[0], pos_ref[1]
    for j, piece in enumerate((p0, p1, p2, p3)):
        for a in range(4):
            for b in range(2):
                to_gram = pl.ds(pl.multiple_of(owner(y, z, j, a, b) * GROUP, GROUP), GROUP)
                gram[to_gram, :] = piece[pl.ds((2 * a + b) * GROUP, GROUP), :]

    def rows_of(value):
        return [value[GROUP * g : GROUP * (g + 1), :] for g in range(HALF // GROUP)]

    w11 = jnp.concatenate(inverse_factor(rows_of(gram[:HALF, :HALF])), axis=0)
    l21 = mm(gram[HALF:, :HALF], w11, 1, 1, HIGHEST)
    rest = gram[HALF:, HALF:] - mm(l21, l21, 1, 1, HIGHEST)
    w22 = jnp.concatenate(inverse_factor(rows_of(rest)), axis=0)
    w21 = -mm(w22, mm(l21, w11, 1, 0, HIGHEST), 1, 0, HIGHEST)
    inverse_ref[:HALF, :HALF] = w11
    inverse_ref[:HALF, HALF:] = jnp.zeros_like(w11)
    inverse_ref[HALF:, :HALF] = w21
    inverse_ref[HALF:, HALF:] = w22


def factor(pos, pieces):
    return pl.pallas_call(
        factor_kernel,
        out_shape=jax.ShapeDtypeStruct((RANK, RANK), F32),
        in_specs=[scalars()] + [whole()] * 4,
        out_specs=whole(),
        scratch_shapes=[pltpu.VMEM((RANK, RANK), F32)],
        compiler_params=LIMIT,
        cost_estimate=pl.CostEstimate(flops=10 << 30, bytes_accessed=32 << 20, transcendentals=0),
        name="factor",
    )(pos, *pieces)


def orthonormal_kernel(p0_high, p0_low, p1_high, p1_low, inverse_ref, high_ref, low_ref):
    inverse = split(inverse_ref[...])
    for t, (p_high, p_low) in enumerate(((p0_high, p0_low), (p1_high, p1_low))):
        rows = pl.ds(t * 4 * PIECE, 4 * PIECE)
        high_ref[rows], low_ref[rows] = split(mm3((p_high[...], p_low[...]), inverse, 1, 1))


def orthonormal(powered, inverse):
    return pl.pallas_call(
        orthonormal_kernel,
        out_shape=(jax.ShapeDtypeStruct((ROWS, RANK), BF16),) * 2,
        in_specs=[whole()] * 5,
        out_specs=(whole(),) * 2,
        compiler_params=LIMIT,
        cost_estimate=pl.CostEstimate(flops=6 * 896 * 256 * 256, bytes_accessed=2 << 20, transcendentals=0),
        name="orthonormal",
    )(*powered, inverse)


def coefficients_kernel(pos_ref, p0, p1, p2, p3, inverse_ref, coeff_ref, high_ref, low_ref, square_ref):
    y, z = pos_ref[0], pos_ref[1]
    inverse = split(inverse_ref[...])
    for j, piece in enumerate((p0, p1, p2, p3)):
        value = mm3(split(piece[...]), inverse, 1, 1)
        for a in range(4):
            for b in range(2):
                place = pl.ds(pl.multiple_of(owner(y, z, j, a, b) * COEFF, COEFF), COEFF)
                coeff_ref[place, :] = value[(2 * a + b) * COEFF : (2 * a + b + 1) * COEFF]
    value = coeff_ref[...]
    high_ref[...], low_ref[...] = split(value)
    square_ref[...] = jnp.sum(value * value, axis=0, keepdims=True)


def coefficients_of(pos, pieces, inverse):
    return pl.pallas_call(
        coefficients_kernel,
        out_shape=(
            jax.ShapeDtypeStruct((COLS, RANK), F32),
            jax.ShapeDtypeStruct((COLS, RANK), BF16),
            jax.ShapeDtypeStruct((COLS, RANK), BF16),
            jax.ShapeDtypeStruct((1, RANK), F32),
        ),
        in_specs=[scalars()] + [whole()] * 5,
        out_specs=(whole(),) * 4,
        compiler_params=LIMIT,
        name="coefficients",
    )(pos, *pieces, inverse)


def write_rows(pos_ref, half, value_ref, out_ref, sems):
    x, core = pos_ref[2], pos_ref[3]
    copies = []
    for s in range(4):
        there = pl.ds(row_start(core if half == 0 else 1 - core, x, s), PIECE)
        here = pl.ds((4 * half + s) * PIECE, PIECE)
        copies.append(pltpu.make_async_copy(value_ref.at[here], out_ref.at[there], sems.at[4 * half + s]))
        copies[-1].start()
    return copies


def feedback_kernel(pos_ref, s0_high, s0_low, s1_high, s1_low, q_ref, c_ref, out_ref, buf, sems):
    coefficients = c_ref[...]
    copies = []
    for t, (s_high, s_low) in enumerate(((s0_high, s0_low), (s1_high, s1_low))):
        rows = pl.ds(t * 4 * PIECE, 4 * PIECE)
        summed = s_high[...].astype(F32) + s_low[...].astype(F32)
        buf[rows] = summed - 0.05 * mm(q_ref[rows], coefficients, 1, 1)
        copies += write_rows(pos_ref, t, buf, out_ref, sems)
    for copy in copies:
        copy.wait()


def feedback(pos, summed, high, coefficients):
    return pl.pallas_call(
        feedback_kernel,
        out_shape=jax.ShapeDtypeStruct((ROWS, COLS), F32),
        in_specs=[scalars()] + [whole()] * 6,
        out_specs=in_hbm(),
        scratch_shapes=[pltpu.VMEM((ROWS, COLS), F32), pltpu.SemaphoreType.DMA((8,))],
        compiler_params=LIMIT,
        cost_estimate=pl.CostEstimate(flops=4 * 896 * 1024 * 256, bytes_accessed=10 << 20, transcendentals=0),
        name="feedback",
    )(pos, *summed, high, coefficients)


def update_kernel(
    scale, pos_ref, high_ref, low_ref, c_ref, c_high, c_low, s_ref, basis_ref, out_ref, b_buf, buf, b_sem, sems
):
    norm = 1.0 / jnp.sqrt(s_ref[...] + 1e-6)
    b_buf[...] = c_ref[...] * norm
    store = pltpu.make_async_copy(b_buf, basis_ref, b_sem)
    store.start()
    coefficients = (c_high[...], c_low[...])
    copies = []
    for t in range(2):
        rows = pl.ds(t * 4 * PIECE, 4 * PIECE)
        q = split((high_ref[rows].astype(F32) + low_ref[rows].astype(F32)) * norm)
        buf[rows] = (scale * mm3(q, coefficients, 1, 1)).astype(BF16)
        copies += write_rows(pos_ref, t, buf, out_ref, sems)
    store.wait()
    for copy in copies:
        copy.wait()


def update(pos, high, low, coefficients, c_high, c_low, squares, scale):
    return pl.pallas_call(
        functools.partial(update_kernel, scale),
        out_shape=(
            jax.ShapeDtypeStruct((COLS, RANK), F32),
            jax.ShapeDtypeStruct((ROWS, COLS), BF16),
        ),
        in_specs=[scalars()] + [whole()] * 6,
        out_specs=(in_hbm(), in_hbm()),
        scratch_shapes=[
            pltpu.VMEM((COLS, RANK), F32),
            pltpu.VMEM((ROWS, COLS), BF16),
            pltpu.SemaphoreType.DMA,
            pltpu.SemaphoreType.DMA((8,)),
        ],
        compiler_params=LIMIT,
        name="update",
    )(pos, high, low, coefficients, c_high, c_low, squares)


def shards(momentum, gradient, old_basis):
    row = lax.axis_index("row")
    col = lax.axis_index("col")
    arguments = (momentum, gradient, old_basis)
    momentum, gradient, old_basis = (pltpu.with_memory_space_constraint(v, pltpu.HBM) for v in arguments)
    pos = jnp.stack([row // 8, row % 8, col // 2, col % 2]).astype(jnp.int32)

    away, s1_high, s1_low, m_own, g_own, b_high, b_low = power_away(pos, momentum, gradient, old_basis)
    came = send_core(away)
    here, s0_high, s0_low = power_own(m_own, g_own, b_high, b_low)
    summed = (s0_high, s0_low, s1_high, s1_low)
    parts = [here[s * PIECE : (s + 1) * PIECE] + came[s * PIECE : (s + 1) * PIECE] for s in range(4)]
    mine = ring_sum(parts[0], [None] + [send_x(parts[s], s) for s in (1, 2, 3)])
    own = jnp.concatenate([mine] + [send_x(mine, s) for s in (3, 2, 1)])
    other = send_core(own)
    p0_high, p0_low, total, gram = project_own(s0_high, s0_low, own)
    p1_high, p1_low, gram, *far = project_far(pos, s1_high, s1_low, other, total, gram)
    own0, own1, plus0, plus1, minus0, minus1 = project(pos, s1_high, s1_low, p1_high, p1_low, total, gram)
    powered = (p0_high, p0_low, p1_high, p1_low)

    far0, far1 = send_y(far[0], 1), send_y(far[1], 3)
    near1, near0 = send_y(plus1, 1), send_y(minus0, 3)
    via0, via1 = send_y(plus0 + far0, 1), send_y(minus1 + far1, 3)
    part0 = (own0 + near0) + via0
    part1 = (own1 + near1) + via1
    came = [send_z(part0[:PAIR], 1), send_z(part0[PAIR:], 2), send_z(part1[:PAIR], 7)]
    mine = ring_sum(part1[PAIR:], [None] + came)
    mine = mine + send_z(mine, 4)

    pieces = [mine] + [send_z(mine, s) for s in Z_SHIFTS[1:]]
    gram = jnp.concatenate([piece[2 * COEFF :] for piece in pieces])
    raw = jnp.concatenate([piece[: 2 * COEFF] for piece in pieces])
    grams = [gram] + [send_y(gram, s) for s in (1, 2, 3)]
    raws = [raw] + [send_y(raw, s) for s in (1, 2, 3)]
    inverse = factor(pos, grams)

    coefficients, c_high, c_low, squares = coefficients_of(pos, raws, inverse)
    came = send_core(squares)
    high, low = orthonormal(powered, inverse)
    came, high, low = lax.optimization_barrier((came, high, low))
    squares = squares + came
    came = [send_x(squares, s) for s in (1, 2, 3)]
    new_momentum = feedback(pos, summed, high, c_high)
    new_momentum, *came = lax.optimization_barrier((new_momentum, *came))
    squares = ring_sum(squares, [None] + came)
    rms_scale = (28672 * 8192 / 256) ** 0.5
    new_basis, new_update = update(pos, high, low, coefficients, c_high, c_low, squares, rms_scale)
    return (new_momentum, new_basis, new_update)


def solution(mesh):
    placed = (P("row", "col"), P("row", "col"), P("col", None))
    return jax.shard_map(
        shards,
        mesh=mesh,
        in_specs=placed,
        out_specs=(P("row", "col"), P("col", None), P("row", "col")),
        check_vma=False,
    )
```

```python
import functools

import jax
import jax.numpy as jnp
from jax import lax
from jax.experimental import pallas as pl
from jax.experimental.pallas import tpu as pltpu
from jax.sharding import PartitionSpec as P

HIGHEST = lax.Precision.HIGHEST
F32 = jnp.float32
BF16 = jnp.bfloat16
HALF = 128
GROUP = 8
PANEL = 8
ROWS = 896
COLS = 1024
RANK = 256
PIECE = 112
SLAB = 256
COEFF = 32
PAIR = 80
LIMIT = pltpu.CompilerParams(vmem_limit_bytes=32 * 1024 * 1024)


def send(value, axis, move, size):
    return lax.ppermute(value, axis, [(i, move(i)) for i in range(size)])


def send_core(value):
    return send(value, "col", lambda i: i ^ 1, 8)


def send_x(value, s):
    return send(value, "col", lambda i: ((i // 2 + s) % 4) * 2 + i % 2, 8)


def send_y(value, s):
    return send(value, "row", lambda i: ((i // 8 + s) % 4) * 8 + i % 8, 32)


def send_z(value, s):
    return send(value, "row", lambda i: (i // 8) * 8 + (i % 8 + s) % 8, 32)


Z_SHIFTS = (0, 1, 2, 7)


def ring_sum(own, came):
    return (own + came[2]) + (came[1] + came[3])


def mm(a, b, ca, cb, precision=None):
    return lax.dot_general(
        a, b, (((ca,), (cb,)), ((), ())), precision=precision, preferred_element_type=F32
    )


def split(value):
    high = value.astype(BF16)
    return high, (value - high.astype(F32)).astype(BF16)


def mm3(a, b, ca, cb):
    return mm(a[0], b[0], ca, cb) + (mm(a[0], b[1], ca, cb) + mm(a[1], b[0], ca, cb))


def whole():
    return pl.BlockSpec(memory_space=pltpu.VMEM)


def in_hbm():
    return pl.BlockSpec(memory_space=pltpu.HBM)


def scalars():
    return pl.BlockSpec(memory_space=pltpu.SMEM)


def row_start(half, x, s):
    return pl.multiple_of(half * (4 * PIECE) + lax.rem(x + s, 4) * PIECE, PIECE)


def power_away_kernel(
    pos_ref, m_ref, g_ref, b_ref, out_ref, high_ref, low_ref, m_own, g_own, b_high, b_low, m_buf, g_buf, b_buf, sems, b_sem
):
    x, core = pos_ref[2], pos_ref[3]
    load = pltpu.make_async_copy(b_ref, b_buf, b_sem)
    away, own = [], []
    for s in range(4):
        there = pl.ds(s * PIECE, PIECE)
        here = pl.ds(row_start(1 - core, x, s), PIECE)
        away.append(pltpu.make_async_copy(m_ref.at[here], m_buf.at[there], sems.at[s, 0]))
        away.append(pltpu.make_async_copy(g_ref.at[here], g_buf.at[there], sems.at[s, 1]))
        here = pl.ds(row_start(core, x, s), PIECE)
        own.append(pltpu.make_async_copy(m_ref.at[here], m_own.at[there], sems.at[4 + s, 0]))
        own.append(pltpu.make_async_copy(g_ref.at[here], g_own.at[there], sems.at[4 + s, 1]))
    load.start()
    for copy in away[:4]:
        copy.start()
    load.wait()
    for copy in away[4:]:
        copy.start()
    basis = split(b_buf[...])
    b_high[...], b_low[...] = basis
    for t in range(2):
        for copy in away[4 * t : 4 * t + 4]:
            copy.wait()
        if t == 0:
            for copy in own:
                copy.start()
        rows = pl.ds(t * 2 * PIECE, 2 * PIECE)
        high, low = split(m_buf[rows] + g_buf[rows].astype(F32))
        high_ref[rows] = high
        low_ref[rows] = low
        out_ref[rows] = mm3((high, low), basis, 1, 0)
    for copy in own:
        copy.wait()


def power_away(pos, momentum, gradient, basis):
    half = (4 * PIECE, COLS)
    return pl.pallas_call(
        power_away_kernel,
        out_shape=(
            jax.ShapeDtypeStruct((4 * PIECE, RANK), F32),
            jax.ShapeDtypeStruct(half, BF16),
            jax.ShapeDtypeStruct(half, BF16),
            jax.ShapeDtypeStruct(half, F32),
            jax.ShapeDtypeStruct(half, BF16),
            jax.ShapeDtypeStruct((COLS, RANK), BF16),
            jax.ShapeDtypeStruct((COLS, RANK), BF16),
        ),
        in_specs=[scalars(), in_hbm(), in_hbm(), in_hbm()],
        out_specs=(whole(),) * 7,
        scratch_shapes=[
            pltpu.VMEM(half, F32),
            pltpu.VMEM(half, BF16),
            pltpu.VMEM((COLS, RANK), F32),
            pltpu.SemaphoreType.DMA((8, 2)),
            pltpu.SemaphoreType.DMA,
        ],
        compiler_params=LIMIT,
        name="power_away",
    )(pos, momentum, gradient, basis)


def power_own_kernel(m_ref, g_ref, b_high, b_low, out_ref, high_ref, low_ref):
    for t in range(2):
        rows = pl.ds(t * 2 * PIECE, 2 * PIECE)
        high, low = split(m_ref[rows] + g_ref[rows].astype(F32))
        high_ref[rows] = high
        low_ref[rows] = low
        out_ref[rows] = mm3((high, low), (b_high[...], b_low[...]), 1, 0)


def power_own(momentum, gradient, b_high, b_low):
    return pl.pallas_call(
        power_own_kernel,
        out_shape=(
            jax.ShapeDtypeStruct((4 * PIECE, RANK), F32),
            jax.ShapeDtypeStruct((4 * PIECE, COLS), BF16),
            jax.ShapeDtypeStruct((4 * PIECE, COLS), BF16),
        ),
        in_specs=[whole()] * 4,
        out_specs=(whole(),) * 3,
        compiler_params=LIMIT,
        cost_estimate=pl.CostEstimate(flops=6 * 448 * 1024 * 256, bytes_accessed=4 << 20, transcendentals=0),
        name="power_own",
    )(momentum, gradient, b_high, b_low)


def project_own_kernel(s_high, s_low, own_ref, high_ref, low_ref, total_ref, gram_ref):
    value = split(own_ref[...])
    high_ref[...], low_ref[...] = value
    gram_ref[...] = mm3(value, value, 0, 0)
    for t in range(4):
        columns = pl.ds(t * SLAB, SLAB)
        total_ref[columns, :] = mm3((s_high[:, columns], s_low[:, columns]), value, 0, 0)


def project_own(s_high, s_low, own):
    return pl.pallas_call(
        project_own_kernel,
        out_shape=(
            jax.ShapeDtypeStruct((4 * PIECE, RANK), BF16),
            jax.ShapeDtypeStruct((4 * PIECE, RANK), BF16),
            jax.ShapeDtypeStruct((COLS, RANK), F32),
            jax.ShapeDtypeStruct((RANK, RANK), F32),
        ),
        in_specs=[whole()] * 3,
        out_specs=(whole(),) * 4,
        compiler_params=LIMIT,
        cost_estimate=pl.CostEstimate(flops=6 * 448 * 1280 * 256, bytes_accessed=4 << 20, transcendentals=0),
        name="project_own",
    )(s_high, s_low, own)


def fill(z, target, total_ref, gram_ref, out0_ref, out1_ref):
    for out_ref, position, a in ((out0_ref, 0, 1), (out0_ref, 1, 2), (out1_ref, 0, 3), (out1_ref, 1, 0)):
        for b in range(2):
            source = lax.rem(z + Z_SHIFTS[a], 4) + 4 * b
            place = position * PAIR
            from_total = pl.ds(pl.multiple_of(source * COEFF, COEFF), COEFF)
            from_gram = pl.ds(pl.multiple_of((target * 8 + source) * GROUP, GROUP), GROUP)
            out_ref[pl.ds(place + b * COEFF, COEFF), :] = total_ref[from_total, :]
            out_ref[pl.ds(place + 2 * COEFF + b * GROUP, GROUP), :] = gram_ref[from_gram, :]


def project_target(y, shift, s_high, s_low, value, total_ref, buf):
    target = lax.rem(y + shift, 4)
    columns = pl.ds(pl.multiple_of(target * SLAB, SLAB), SLAB)
    buf[...] = total_ref[columns, :] + mm3((s_high[:, columns], s_low[:, columns]), value, 0, 0)
    return target


def project_far_kernel(
    pos_ref, s_high, s_low, other_ref, total_ref, gram_ref, high_ref, low_ref, sum_ref, out0_ref, out1_ref, buf
):
    y, z = pos_ref[0], pos_ref[1]
    value = split(other_ref[...])
    high_ref[...], low_ref[...] = value
    sum_ref[...] = gram_ref[...] + mm3(value, value, 0, 0)
    target = project_target(y, 2, s_high, s_low, value, total_ref, buf)
    fill(z, target, buf, sum_ref, out0_ref, out1_ref)


def project_far(pos, s_high, s_low, other, total, gram):
    return pl.pallas_call(
        project_far_kernel,
        out_shape=(
            jax.ShapeDtypeStruct((4 * PIECE, RANK), BF16),
            jax.ShapeDtypeStruct((4 * PIECE, RANK), BF16),
            jax.ShapeDtypeStruct((RANK, RANK), F32),
            jax.ShapeDtypeStruct((2 * PAIR, RANK), F32),
            jax.ShapeDtypeStruct((2 * PAIR, RANK), F32),
        ),
        in_specs=[scalars()] + [whole()] * 5,
        out_specs=(whole(),) * 5,
        scratch_shapes=[pltpu.VMEM((SLAB, RANK), F32)],
        compiler_params=LIMIT,
        name="project_far",
    )(pos, s_high, s_low, other, total, gram)


def project_kernel(pos_ref, s_high, s_low, high_ref, low_ref, total_ref, gram_ref, *refs):
    y, z = pos_ref[0], pos_ref[1]
    value = (high_ref[...], low_ref[...])
    for k, shift in enumerate((0, 1, 3)):
        buf = refs[6 + k]
        target = project_target(y, shift, s_high, s_low, value, total_ref, buf)
        fill(z, target, buf, gram_ref, refs[2 * k], refs[2 * k + 1])


def project(pos, s_high, s_low, high, low, total, gram):
    return pl.pallas_call(
        project_kernel,
        out_shape=(jax.ShapeDtypeStruct((2 * PAIR, RANK), F32),) * 6,
        in_specs=[scalars()] + [whole()] * 6,
        out_specs=(whole(),) * 6,
        scratch_shapes=[pltpu.VMEM((SLAB, RANK), F32)] * 3,
        compiler_params=LIMIT,
        cost_estimate=pl.CostEstimate(flops=6 * 448 * 768 * 256, bytes_accessed=4 << 20, transcendentals=0),
        name="project",
    )(pos, s_high, s_low, high, low, total, gram)


def splat_row(value, row):
    return jnp.broadcast_to(value[row : row + 1, :], value.shape)


def splat_col(value, col):
    return jnp.broadcast_to(value[:, col : col + 1], value.shape)


def owner(y, z, j, a, b):
    from_z = lax.rem(z + 8 - Z_SHIFTS[a], 4) + 4 * b
    return lax.rem(y + 4 - j, 4) * 8 + from_z


def inverse_factor(groups):
    lane = lax.broadcasted_iota(jnp.int32, (GROUP, HALF), 1)
    sub = lax.broadcasted_iota(jnp.int32, (GROUP, HALF), 0)
    groups = list(groups)
    count = len(groups)
    result = []
    kept_rows, factor_rows = [], []
    for g in range(count):
        base = g * GROUP
        inside = (lane >= base) & (lane < base + GROUP)
        pivot = groups[g]
        cols = [splat_col(pivot, base + a) for a in range(GROUP)]
        s = [[splat_row(cols[a], b) if b >= a else None for a in range(GROUP)] for b in range(GROUP)]
        low = [[None] * GROUP for _ in range(GROUP)]
        inverse = []
        for a in range(GROUP):
            inverse.append(1.0 / s[a][a])
            for b in range(a + 1, GROUP):
                low[b][a] = s[b][a] * inverse[a]
            for b in range(a + 1, GROUP):
                for c in range(a + 1, b + 1):
                    s[b][c] = s[b][c] - low[b][a] * s[c][a]
        outside = jnp.where(inside, 0.0, pivot)
        rows = []
        for a in range(GROUP):
            row = splat_row(outside, a)
            for e in range(a):
                row = row - low[a][e] * rows[e]
            rows.append(jnp.where(lane == base + a, 1.0, row))
        last = (g // PANEL + 1) * PANEL
        for i in range(g + 1, last):
            here = groups[i]
            kept = jnp.where(inside, 0.0, here)
            factors = []
            for a in range(GROUP):
                c = splat_col(here, base + a)
                for e in range(a):
                    c = c - factors[e] * s[a][e]
                factors.append(c * inverse[a])
            for a in range(GROUP):
                kept = kept - factors[a] * rows[a]
            groups[i] = kept
        final = jnp.zeros_like(pivot)
        plain = jnp.zeros_like(pivot)
        scaled = jnp.zeros_like(pivot)
        for a in range(GROUP):
            final = jnp.where(sub == a, rows[a] * lax.rsqrt(s[a][a]), final)
            plain = jnp.where(sub == a, rows[a], plain)
            scaled = jnp.where(sub == a, rows[a] * inverse[a], scaled)
        kept_rows.append(jnp.where((lane >= base) & (lane < last * GROUP) & (lane > sub + base), 0.0, plain))
        factor_rows.append(scaled)
        if g + 1 == last and last < count:
            change = mm(jnp.concatenate(factor_rows), jnp.concatenate(kept_rows), 0, 0, HIGHEST)
            start = (last - PANEL) * GROUP
            panel = (lane >= start) & (lane < last * GROUP)
            for i in range(last, count):
                groups[i] = jnp.where(panel, 0.0, groups[i]) - change[GROUP * i : GROUP * (i + 1), :]
            kept_rows, factor_rows = [], []
        result.append(jnp.where(lane <= sub + base, final, 0.0))
    return result


def factor_kernel(pos_ref, p0, p1, p2, p3, inverse_ref, gram):
    y, z = pos_ref[0], pos_ref[1]
    for j, piece in enumerate((p0, p1, p2, p3)):
        for a in range(4):
            for b in range(2):
                to_gram = pl.ds(pl.multiple_of(owner(y, z, j, a, b) * GROUP, GROUP), GROUP)
                gram[to_gram, :] = piece[pl.ds((2 * a + b) * GROUP, GROUP), :]

    def rows_of(value):
        return [value[GROUP * g : GROUP * (g + 1), :] for g in range(HALF // GROUP)]

    w11 = jnp.concatenate(inverse_factor(rows_of(gram[:HALF, :HALF])), axis=0)
    l21 = mm(gram[HALF:, :HALF], w11, 1, 1, HIGHEST)
    rest = gram[HALF:, HALF:] - mm(l21, l21, 1, 1, HIGHEST)
    w22 = jnp.concatenate(inverse_factor(rows_of(rest)), axis=0)
    w21 = -mm(w22, mm(l21, w11, 1, 0, HIGHEST), 1, 0, HIGHEST)
    inverse_ref[:HALF, :HALF] = w11
    inverse_ref[:HALF, HALF:] = jnp.zeros_like(w11)
    inverse_ref[HALF:, :HALF] = w21
    inverse_ref[HALF:, HALF:] = w22


def factor(pos, pieces):
    return pl.pallas_call(
        factor_kernel,
        out_shape=jax.ShapeDtypeStruct((RANK, RANK), F32),
        in_specs=[scalars()] + [whole()] * 4,
        out_specs=whole(),
        scratch_shapes=[pltpu.VMEM((RANK, RANK), F32)],
        compiler_params=LIMIT,
        cost_estimate=pl.CostEstimate(flops=10 << 30, bytes_accessed=32 << 20, transcendentals=0),
        name="factor",
    )(pos, *pieces)


def orthonormal_kernel(p0_high, p0_low, p1_high, p1_low, inverse_ref, c_ref, high_ref, low_ref, c_high, c_low):
    c_high[...], c_low[...] = split(c_ref[...])
    inverse = split(inverse_ref[...])
    for t, (p_high, p_low) in enumerate(((p0_high, p0_low), (p1_high, p1_low))):
        rows = pl.ds(t * 4 * PIECE, 4 * PIECE)
        high_ref[rows], low_ref[rows] = split(mm3((p_high[...], p_low[...]), inverse, 1, 1))


def orthonormal(powered, inverse, coefficients):
    return pl.pallas_call(
        orthonormal_kernel,
        out_shape=(jax.ShapeDtypeStruct((ROWS, RANK), BF16),) * 2 + (jax.ShapeDtypeStruct((COLS, RANK), BF16),) * 2,
        in_specs=[whole()] * 6,
        out_specs=(whole(),) * 4,
        compiler_params=LIMIT,
        cost_estimate=pl.CostEstimate(flops=6 * 896 * 256 * 256, bytes_accessed=2 << 20, transcendentals=0),
        name="orthonormal",
    )(*powered, inverse, coefficients)


def coefficients_kernel(pos_ref, p0, p1, p2, p3, inverse_ref, coeff_ref, square_ref):
    y, z = pos_ref[0], pos_ref[1]
    inverse = split(inverse_ref[...])
    for j, piece in enumerate((p0, p1, p2, p3)):
        value = mm3(split(piece[...]), inverse, 1, 1)
        for a in range(4):
            for b in range(2):
                place = pl.ds(pl.multiple_of(owner(y, z, j, a, b) * COEFF, COEFF), COEFF)
                coeff_ref[place, :] = value[(2 * a + b) * COEFF : (2 * a + b + 1) * COEFF]
    value = coeff_ref[...]
    square_ref[...] = jnp.sum(value * value, axis=0, keepdims=True)


def coefficients_of(pos, pieces, inverse):
    return pl.pallas_call(
        coefficients_kernel,
        out_shape=(
            jax.ShapeDtypeStruct((COLS, RANK), F32),
            jax.ShapeDtypeStruct((1, RANK), F32),
        ),
        in_specs=[scalars()] + [whole()] * 5,
        out_specs=(whole(),) * 2,
        compiler_params=LIMIT,
        name="coefficients",
    )(pos, *pieces, inverse)


def write_rows(pos_ref, half, value_ref, out_ref, sems):
    x, core = pos_ref[2], pos_ref[3]
    copies = []
    for s in range(4):
        there = pl.ds(row_start(core if half == 0 else 1 - core, x, s), PIECE)
        here = pl.ds((4 * half + s) * PIECE, PIECE)
        copies.append(pltpu.make_async_copy(value_ref.at[here], out_ref.at[there], sems.at[4 * half + s]))
        copies[-1].start()
    return copies


def feedback_kernel(pos_ref, s0_high, s0_low, s1_high, s1_low, q_ref, c_ref, out_ref, buf, sems):
    coefficients = c_ref[...]
    copies = []
    for t, (s_high, s_low) in enumerate(((s0_high, s0_low), (s1_high, s1_low))):
        rows = pl.ds(t * 4 * PIECE, 4 * PIECE)
        summed = s_high[...].astype(F32) + s_low[...].astype(F32)
        buf[rows] = summed - 0.05 * mm(q_ref[rows], coefficients, 1, 1)
        copies += write_rows(pos_ref, t, buf, out_ref, sems)
    for copy in copies:
        copy.wait()


def feedback(pos, summed, high, coefficients):
    return pl.pallas_call(
        feedback_kernel,
        out_shape=jax.ShapeDtypeStruct((ROWS, COLS), F32),
        in_specs=[scalars()] + [whole()] * 6,
        out_specs=in_hbm(),
        scratch_shapes=[pltpu.VMEM((ROWS, COLS), F32), pltpu.SemaphoreType.DMA((8,))],
        compiler_params=LIMIT,
        cost_estimate=pl.CostEstimate(flops=4 * 896 * 1024 * 256, bytes_accessed=10 << 20, transcendentals=0),
        name="feedback",
    )(pos, *summed, high, coefficients)


def update_kernel(
    scale, pos_ref, high_ref, low_ref, c_ref, c_high, c_low, s_ref, basis_ref, out_ref, b_buf, buf, b_sem, sems
):
    norm = 1.0 / jnp.sqrt(s_ref[...] + 1e-6)
    b_buf[...] = c_ref[...] * norm
    store = pltpu.make_async_copy(b_buf, basis_ref, b_sem)
    store.start()
    coefficients = (c_high[...], c_low[...])
    copies = []
    for t in range(2):
        rows = pl.ds(t * 4 * PIECE, 4 * PIECE)
        q = split((high_ref[rows].astype(F32) + low_ref[rows].astype(F32)) * norm)
        buf[rows] = (scale * mm3(q, coefficients, 1, 1)).astype(BF16)
        copies += write_rows(pos_ref, t, buf, out_ref, sems)
    store.wait()
    for copy in copies:
        copy.wait()


def update(pos, high, low, coefficients, c_high, c_low, squares, scale):
    return pl.pallas_call(
        functools.partial(update_kernel, scale),
        out_shape=(
            jax.ShapeDtypeStruct((COLS, RANK), F32),
            jax.ShapeDtypeStruct((ROWS, COLS), BF16),
        ),
        in_specs=[scalars()] + [whole()] * 6,
        out_specs=(in_hbm(), in_hbm()),
        scratch_shapes=[
            pltpu.VMEM((COLS, RANK), F32),
            pltpu.VMEM((ROWS, COLS), BF16),
            pltpu.SemaphoreType.DMA,
            pltpu.SemaphoreType.DMA((8,)),
        ],
        compiler_params=LIMIT,
        name="update",
    )(pos, high, low, coefficients, c_high, c_low, squares)


def shards(momentum, gradient, old_basis):
    row = lax.axis_index("row")
    col = lax.axis_index("col")
    arguments = (momentum, gradient, old_basis)
    momentum, gradient, old_basis = (pltpu.with_memory_space_constraint(v, pltpu.HBM) for v in arguments)
    pos = jnp.stack([row // 8, row % 8, col // 2, col % 2]).astype(jnp.int32)

    away, s1_high, s1_low, m_own, g_own, b_high, b_low = power_away(pos, momentum, gradient, old_basis)
    came = send_core(away)
    here, s0_high, s0_low = power_own(m_own, g_own, b_high, b_low)
    summed = (s0_high, s0_low, s1_high, s1_low)
    parts = [here[s * PIECE : (s + 1) * PIECE] + came[s * PIECE : (s + 1) * PIECE] for s in range(4)]
    mine = ring_sum(parts[0], [None] + [send_x(parts[s], s) for s in (1, 2, 3)])
    own = jnp.concatenate([mine] + [send_x(mine, s) for s in (3, 2, 1)])
    other = send_core(own)
    p0_high, p0_low, total, gram = project_own(s0_high, s0_low, own)
    p1_high, p1_low, gram, *far = project_far(pos, s1_high, s1_low, other, total, gram)
    own0, own1, plus0, plus1, minus0, minus1 = project(pos, s1_high, s1_low, p1_high, p1_low, total, gram)
    powered = (p0_high, p0_low, p1_high, p1_low)

    far0, far1 = send_y(far[0], 1), send_y(far[1], 3)
    near1, near0 = send_y(plus1, 1), send_y(minus0, 3)
    via0, via1 = send_y(plus0 + far0, 1), send_y(minus1 + far1, 3)
    part0 = (own0 + near0) + via0
    part1 = (own1 + near1) + via1
    came = [send_z(part0[:PAIR], 1), send_z(part0[PAIR:], 2), send_z(part1[:PAIR], 7)]
    mine = ring_sum(part1[PAIR:], [None] + came)
    mine = mine + send_z(mine, 4)

    pieces = [mine] + [send_z(mine, s) for s in Z_SHIFTS[1:]]
    gram = jnp.concatenate([piece[2 * COEFF :] for piece in pieces])
    raw = jnp.concatenate([piece[: 2 * COEFF] for piece in pieces])
    grams = [gram] + [send_y(gram, s) for s in (1, 2, 3)]
    raws = [raw] + [send_y(raw, s) for s in (1, 2, 3)]
    inverse = factor(pos, grams)

    coefficients, squares = coefficients_of(pos, raws, inverse)
    came = send_core(squares)
    high, low, c_high, c_low = orthonormal(powered, inverse, coefficients)
    came, high, low = lax.optimization_barrier((came, high, low))
    squares = squares + came
    came = [send_x(squares, s) for s in (1, 2, 3)]
    new_momentum = feedback(pos, summed, high, c_high)
    new_momentum, *came = lax.optimization_barrier((new_momentum, *came))
    squares = ring_sum(squares, [None] + came)
    rms_scale = (28672 * 8192 / 256) ** 0.5
    new_basis, new_update = update(pos, high, low, coefficients, c_high, c_low, squares, rms_scale)
    return (new_momentum, new_basis, new_update)


def solution(mesh):
    placed = (P("row", "col"), P("row", "col"), P("col", None))
    return jax.shard_map(
        shards,
        mesh=mesh,
        in_specs=placed,
        out_specs=(P("row", "col"), P("col", None), P("row", "col")),
        check_vma=False,
    )
```
